128 devices in a mesh: row: 8 (over y, core), col: 16 (over x, z).
Axes of the slice: x: 4, y: 4, z: 4, core: 2. Of those that a mesh axis runs over, the one named last changes fastest.
Arguments:
- visible_patches: bfloat16 [16, 256, 6144], P(None, 'row', 'col'), may hold values from -16 to 16
- input_gain: float32 [6144], P('col'), may hold values from 0.25 to 1.75
- encoder_project: bfloat16 [6144, 18432], P('col', 'row'), may hold values from -0.078125 to 0.078125
- query_gain: float32 [128], replicated, may hold values from 0.25 to 2.5
- key_gain: float32 [128], replicated, may hold values from 0.25 to 2.5
- output_weight: bfloat16 [6144, 6144], P('row', 'col'), may hold values from -0.30618622 to 0.30618622
- final_gain: float32 [6144], P('col'), may hold values from 0.25 to 2.5
- embed_weight: bfloat16 [6144, 1024], P('col'), may hold values from -0.078125 to 0.078125
- embed_bias: float32 [1024], replicated, may hold values from -3 to 3
- mask_token: float32 [1024], replicated, may hold values from -4 to 4
- position_embed: bfloat16 [1024, 1024], P('row'), may hold values from -3 to 3
- script_table: bfloat16 [40, 1024], replicated, may hold values from -3 to 3
- decoder_gain: float32 [1024], replicated, may hold values from 0.25 to 1.75
- decoder_project: bfloat16 [1024, 3072], replicated, may hold values from -0.1875 to 0.1875
- decoder_query: float32 [64], replicated, may hold values from 0.25 to 2.5
- decoder_key: float32 [64], replicated, may hold values from 0.25 to 2.5
- decoder_output: bfloat16 [1024, 1024], replicated, may hold values from -0.1875 to 0.1875
- head_gain: float32 [1024], replicated, may hold values from 0.25 to 1.75
- pixel_weight: bfloat16 [1024, 768], replicated, may hold values from -0.1875 to 0.1875
- pixel_bias: float32 [768], replicated, may hold values from -3 to 3
- visible_index: int32 [16, 256], P('col'), may hold values from 0 to 1023, as said below
- script_index: int32 [16], P('col'), may hold values from 0 to 39
Outputs:
- encoded: bfloat16 [16, 256, 6144], P(None, 'row', 'col')
- predicted: bfloat16 [16, 1024, 768], P('col', 'row')
The draws below stay inside these ranges and needn't reach their ends.
Inputs may be any that keep to these rules, and one draw needn't show every extreme that they name: `visible_index`: each image's row holds 256 distinct patch positions in no particular order.
All inputs are finite; a program needn't handle non-finite values.
Results may differ from the reference program's by a relative error of at most 0.034.
Values may be sent and summed in bfloat16 or wider, within the bound.
A program may use at most 192 MiB of HBM per device.

```python
import math
from functools import partial
import jax
import jax.numpy as jnp
import numpy as np
from jax import lax

D = 6144
HEADS = 48
HEAD_DIM = 128
DD = 1024
DEC_HEADS = 16
DEC_HEAD_DIM = 64
PIX = 768
PATCHES = 1024
VIS = 256
SCRIPTS = 40
IMAGES = 16
N_COL = 16


def draw_visible_patches(key, part):
    key = jax.random.fold_in(key, 11)
    column_key, base_key = jax.random.split(key, 2)
    position = jnp.arange(D, dtype=jnp.float32) / (D - 1)
    spread_factor = jnp.exp(jax.random.uniform(column_key, (D,), jnp.float32, 0.0, math.log(10.0)))
    columns = 0.05 * spread_factor * jnp.exp(math.log(3.0) * position)
    base = jnp.clip(jax.random.normal(base_key, (IMAGES, VIS, D), jnp.float32), -3.5, 3.5)
    values = (base + 0.5) * columns
    return values.astype(jnp.bfloat16)


def draw_output_weight(key, part):
    key = jax.random.fold_in(key, 37)
    phase_key, turn_key, rough_key, tilt_key, base_key, along_key = jax.random.split(key, 6)
    position = jnp.arange(D, dtype=jnp.float32) / (D - 1)
    phase = jax.random.uniform(phase_key, (), jnp.float32, 0.0, 2.0 * math.pi)
    turn = jax.random.uniform(turn_key, (), jnp.float32, 0.0, 2.0 * math.pi)
    level = 0.5 + 0.5 * jnp.sin(2.0 * math.pi * 1.5 * position + phase)
    rough = jnp.exp(jax.random.uniform(rough_key, (D,), jnp.float32, -0.35, 0.35))
    tilt = jnp.exp(jax.random.uniform(tilt_key, (D,), jnp.float32, -0.35, 0.35))
    column_scale = 0.3 * jnp.exp(math.log(10.0) * level) * rough
    shared_column = 1.5 * jnp.cos(2.0 * math.pi * 1.25 * position + turn) * tilt
    base = jnp.clip(jax.random.normal(base_key, (D, D), jnp.float32), -4.0, 4.0)
    along = jnp.clip(jax.random.normal(along_key, (D,), jnp.float32), -3.0, 3.0)
    values = (base * column_scale[None, :] + along[:, None] * shared_column[None, :]) * (1.0 / math.sqrt(D))
    return values.astype(jnp.bfloat16)


def draw_visible_index(key, part):
    key = jax.random.fold_in(key, 23)
    image_keys = jax.random.split(key, IMAGES)
    orders = jax.vmap(lambda image_key: jax.random.permutation(image_key, PATCHES))(image_keys)
    return orders[:, :VIS].astype(jnp.int32)


def set_ends(drawn, rng, smallest, high):
    place = [jax.random.randint(jax.random.fold_in(rng, axis), (), 0, length) for axis, length in enumerate(drawn.shape)]
    longest = drawn.shape.index(max(drawn.shape))
    neighbour = place[:longest] + [(place[longest] + 1) % drawn.shape[longest]] + place[longest + 1:]
    return drawn.at[tuple(place)].set(smallest).at[tuple(neighbour)].set(high)


def block_levels(own_key, shape, cuts, least, high):
    gain = 1.0
    for dim, shards_of in cuts:
        draws = jax.random.uniform(jax.random.fold_in(jax.random.fold_in(own_key, 6), dim), (shards_of,), jnp.float32, least / len(cuts), high / len(cuts))
        gain = gain * jnp.repeat(jnp.exp(draws), shape[dim] // shards_of).reshape((-1,) + (1,) * (len(shape) - 1 - dim))
    return gain


def rank_table(number_of, slope):
    loads = [(1 << 20) // math.isqrt(standing ** slope) + 1 for standing in range(1, number_of + 1)]
    scale = 1 + sum(loads) // (1 << 30)
    return np.cumsum(np.array([max(1, weight // scale) for weight in loads]))


def ranked(own_key, dims, number_of, slope):
    table = rank_table(number_of, slope)
    ticket = jax.random.randint(jax.random.fold_in(own_key, 1), dims, 0, int(table[number_of - 1]))
    standing = jnp.searchsorted(jnp.asarray(table, jnp.int32), ticket, side="right")
    return jax.random.permutation(jax.random.fold_in(own_key, 2), number_of)[standing].astype(jnp.int32)


def bell_draw(own_key, extent, scale, most, shards=(), held_as=jnp.bfloat16):
    result = jax.random.normal(own_key, extent, jnp.float32) * scale
    if len(shards) > 0:
        result = block_levels(own_key, extent, shards, -0.22, 0.18) * result
    return jnp.clip(result, min=-most, max=most).astype(held_as)


def setup_inputs(seed: int = 0) -> dict:
    seeds = jax.random.split(jax.random.key(seed), 23)
    visible_patches = draw_visible_patches(jax.random.fold_in(seeds[22], 71), 0)
    input_gain = jnp.clip(1.0 + 0.15 * jax.random.normal(seeds[1], (D,), jnp.float32), 0.25, 1.75)
    encoder_project = bell_draw(seeds[2], (D, 3 * D), D ** -0.5, 0.078125, ((0, 16), (1, 8)))
    query_gain = jnp.clip(jnp.exp(jax.random.uniform(seeds[3], (HEAD_DIM,), jnp.float32, math.log(0.25), math.log(2.5))), 0.25, 2.5)
    key_gain = jnp.clip(jnp.exp(jax.random.uniform(seeds[4], (HEAD_DIM,), jnp.float32, math.log(0.25), math.log(2.5))), 0.25, 2.5)
    output_weight = draw_output_weight(jax.random.fold_in(seeds[22], 71), 0)
    final_gain = jnp.clip(jnp.exp(math.log(2.5) - 2.3025851 * jax.random.uniform(seeds[6], (D,), jnp.float32) ** block_levels(seeds[6], (D,), ((0, 16),), -0.2, 0.2)), 0.25, 2.5)
    embed_weight = bell_draw(seeds[7], (D, DD), D ** -0.5, 0.078125, ((0, 16),))
    embed_bias = bell_draw(seeds[8], (DD,), 0.5, 3.0, (), jnp.float32)
    mask_token = bell_draw(seeds[9], (DD,), 1.0, 4.0, (), jnp.float32)
    position_embed = bell_draw(seeds[10], (PATCHES, DD), 0.5, 3.0, ((0, 8),))
    script_table = bell_draw(seeds[11], (SCRIPTS, DD), 0.5, 3.0)
    decoder_gain = jnp.clip(1.0 + 0.15 * jax.random.normal(seeds[12], (DD,), jnp.float32), 0.25, 1.75)
    decoder_project = bell_draw(seeds[13], (DD, 3 * DD), DD ** -0.5, 0.1875)
    decoder_query = jnp.clip(jnp.exp(jax.random.uniform(seeds[14], (DEC_HEAD_DIM,), jnp.float32, math.log(0.25), math.log(2.5))), 0.25, 2.5)
    decoder_key = jnp.clip(jnp.exp(jax.random.uniform(seeds[15], (DEC_HEAD_DIM,), jnp.float32, math.log(0.25), math.log(2.5))), 0.25, 2.5)
    decoder_output = bell_draw(seeds[16], (DD, DD), DD ** -0.5, 0.1875)
    head_gain = jnp.clip(1.0 + 0.15 * jax.random.normal(seeds[17], (DD,), jnp.float32), 0.25, 1.75)
    pixel_weight = bell_draw(seeds[18], (DD, PIX), DD ** -0.5, 0.1875)
    pixel_bias = bell_draw(seeds[19], (PIX,), 0.5, 3.0, (), jnp.float32)
    visible_index = draw_visible_index(jax.random.fold_in(seeds[22], 71), 0)
    script_index = set_ends(ranked(seeds[21], (IMAGES,), SCRIPTS, 2), jax.random.fold_in(seeds[21], 3), 0, SCRIPTS - 1).astype(jnp.int32)
    return dict(visible_patches=visible_patches, input_gain=input_gain, encoder_project=encoder_project, query_gain=query_gain, key_gain=key_gain, output_weight=output_weight, final_gain=final_gain, embed_weight=embed_weight, embed_bias=embed_bias, mask_token=mask_token, position_embed=position_embed, script_table=script_table, decoder_gain=decoder_gain, decoder_project=decoder_project, decoder_query=decoder_query, decoder_key=decoder_key, decoder_output=decoder_output, head_gain=head_gain, pixel_weight=pixel_weight, pixel_bias=pixel_bias, visible_index=visible_index, script_index=script_index)


epsilon = 1e-06

def normalise(values, gain_vector):
    average = lax.optimization_barrier(jnp.mean(values, axis=-1, keepdims=True))
    spread = lax.optimization_barrier(jnp.mean(values * values, axis=-1, keepdims=True)) - average * average
    return (values - average) * lax.rsqrt(spread + epsilon) * gain_vector

def attend(queries, keys, values, factor):
    scores = jnp.dot(queries, keys.T, preferred_element_type=jnp.float32) * factor
    weights = jnp.exp(scores).astype(jnp.bfloat16)
    totals = lax.optimization_barrier(jnp.sum(weights.astype(jnp.float32), axis=-1, keepdims=True))
    mixture = jnp.dot(weights, values, preferred_element_type=jnp.float32)
    return (mixture / totals).astype(jnp.bfloat16)

def reference(visible_patches, input_gain, encoder_project, query_gain, key_gain, output_weight, final_gain, embed_weight, embed_bias, mask_token, position_embed, script_table, decoder_gain, decoder_project, decoder_query, decoder_key, decoder_output, head_gain, pixel_weight, pixel_bias, visible_index, script_index):
    images = visible_patches.shape[0]
    inputs = visible_patches.astype(jnp.float32)
    normed = normalise(inputs, input_gain).astype(jnp.bfloat16)
    piece_width = D // N_COL
    blocks = normed.astype(jnp.float32).reshape(images * VIS, N_COL, piece_width)
    per_head = encoder_project.reshape(N_COL, piece_width, HEADS, 3 * HEAD_DIM)

    def one_head(head):
        weight = lax.dynamic_index_in_dim(per_head, head, 2, keepdims=False).astype(jnp.float32)
        pieces = jnp.einsum('tkd,kdo->kto', blocks, weight)
        rounded = lax.optimization_barrier(pieces.astype(jnp.bfloat16))
        projected = lax.optimization_barrier(jnp.sum(rounded.astype(jnp.float32), axis=0)).reshape(images, VIS, 3, HEAD_DIM)
        queries = normalise(projected[:, :, 0], query_gain).astype(jnp.bfloat16)
        keys = normalise(projected[:, :, 1], key_gain).astype(jnp.bfloat16)
        values = projected[:, :, 2].astype(jnp.bfloat16)
        return jax.vmap(partial(attend, factor=HEAD_DIM ** (-0.5)))(queries, keys, values)
    heads_out = lax.map(one_head, jnp.arange(HEADS, dtype=jnp.int32))
    attended = jnp.transpose(heads_out, (1, 2, 0, 3)).reshape(images * VIS, D)
    residual = inputs + jnp.dot(attended, output_weight, preferred_element_type=jnp.float32).reshape(images, VIS, D)
    encoded = residual.astype(jnp.bfloat16)
    enc_normed = normalise(residual, final_gain).astype(jnp.bfloat16)
    embedded = (jnp.dot(enc_normed.reshape(images * VIS, D), embed_weight, preferred_element_type=jnp.float32) + embed_bias).astype(jnp.bfloat16).reshape(images, VIS, DD)
    positions = jnp.arange(PATCHES, dtype=jnp.int32)
    script_ids = jnp.arange(SCRIPTS, dtype=jnp.int32)

    def one_image(record):
        window, places, script = record
        select = (places[None, :] == positions[:, None]).astype(jnp.bfloat16)
        present = lax.optimization_barrier(jnp.sum(select.astype(jnp.float32), axis=1, keepdims=True))
        gathered = jnp.dot(select, window, preferred_element_type=jnp.float32)
        labels = (script_ids == script).astype(jnp.bfloat16)
        scripted = jnp.dot(labels[None, :], script_table, preferred_element_type=jnp.float32)
        tokens = gathered + (1.0 - present) * mask_token + position_embed.astype(jnp.float32) + scripted
        dec_normed = normalise(tokens, decoder_gain).astype(jnp.bfloat16)
        decoder_proj = jnp.dot(dec_normed, decoder_project, preferred_element_type=jnp.float32)
        decoder_proj = decoder_proj.reshape(PATCHES, DEC_HEADS, 3, DEC_HEAD_DIM)
        queries = normalise(decoder_proj[:, :, 0], decoder_query).astype(jnp.bfloat16)
        keys = normalise(decoder_proj[:, :, 1], decoder_key).astype(jnp.bfloat16)
        values = decoder_proj[:, :, 2].astype(jnp.bfloat16)
        mixture = jax.vmap(partial(attend, factor=DEC_HEAD_DIM ** (-0.5)), in_axes=1, out_axes=1)(queries, keys, values)
        decoded = tokens + jnp.dot(mixture.reshape(PATCHES, DD), decoder_output, preferred_element_type=jnp.float32)
        head_normed = normalise(decoded, head_gain).astype(jnp.bfloat16)
        return (jnp.dot(head_normed, pixel_weight, preferred_element_type=jnp.float32) + pixel_bias).astype(jnp.bfloat16)
    predicted = lax.map(one_image, (embedded, visible_index, script_index))
    return (encoded, predicted)
```

```python
import functools
import jax
import jax.numpy as jnp
from jax import lax
from jax.experimental import pallas as pl
from jax.experimental.pallas import tpu as pltpu
from jax.sharding import PartitionSpec as P

D = 6144
DD = 1024
MESH = pl.DeviceIdType.MESH
bf16 = jnp.bfloat16
f32 = jnp.float32

epsilon = 1e-06
LAST = (((1,), (1,)), ((), ()))


def place():
    row, col = lax.axis_index("row"), lax.axis_index("col")
    return col // 4, row // 2, lax.rem(col, 4), lax.rem(row, 2)


def turn(i, by):
    return lax.rem(i + by, 4)


def device(x, y, z, c):
    return (y * 2 + c, x * 4 + z)


def remote(src, dst, send_sem, recv_sem, where):
    return pltpu.make_async_remote_copy(
        src_ref=src,
        dst_ref=dst,
        send_sem=send_sem,
        recv_sem=recv_sem,
        device_id=where,
        device_id_type=MESH,
    )


def greet(peers):
    barrier = pltpu.get_barrier_semaphore()
    for peer in peers:
        pl.semaphore_signal(barrier, inc=1, device_id=peer, device_id_type=MESH)
    return lambda: pl.semaphore_wait(barrier, len(peers))


def aligned(index, multiple):
    return pl.multiple_of(index, multiple)


def row_sums(values):
    ones = jnp.ones((8, values.shape[1]), bf16)
    return lax.dot_general(ones, values, LAST, preferred_element_type=f32)


def head_norm(values, gain_vector):
    amount = values.shape[-1]
    average = jnp.sum(values, axis=-1, keepdims=True) / amount
    spread = jnp.sum(values * values, axis=-1, keepdims=True) / amount - average * average
    return (values - average) * lax.rsqrt(spread + epsilon) * gain_vector


def attention(queries, keys, values, factor):
    scores = lax.dot_general(queries, keys, LAST, preferred_element_type=f32) * factor
    weights = jnp.exp(scores).astype(bf16)
    totals = jnp.sum(weights.astype(f32), axis=-1, keepdims=True)
    mixture = jnp.dot(weights, values, preferred_element_type=f32)
    return (mixture / totals).astype(bf16)


HEADS_OWN = 6


def encoder_kernel(
    x_ref, gain_ref, w_ref, qg_ref, kg_ref, out_ref,
    stats, normed, a, w, cs, cr,
    w_own, st_s, st_r, ax_s, ax_r, ay_s, ay_r, ac_s, ac_r, wn_s, wn_r, wf_s, wf_r, c_s, c_r,
):
    x, y, z, c = place()
    col = x * 4 + z
    mate = device(x, y, z, 1 - c)
    right, left = turn(x, 1), turn(x, 3)

    def col_peer(d):
        other = lax.rem(col + d, 16)
        return device(other // 4, y, lax.rem(other, 4), c)

    entered = greet(
        [col_peer(d) for d in range(1, 16)]
        + [device(x, turn(y, e), z, c) for e in range(1, 4)]
        + [mate]
    )

    def w_block(j, owner, start, size):
        return w.at[j, pl.ds(aligned(owner * 384 + start, 192), size), :]

    def w_fetch(j):
        return pltpu.make_async_copy(
            w_ref.at[:, pl.ds(aligned(j * 384, 128), 384)], w_block(j, x, 0, 384), w_own.at[j]
        )

    def w_send(j, way):
        block = w_block(j, x, 0, 384)
        target = device(right if way == 0 else left, y, z, c)
        return remote(block, block, wn_s.at[way, j], wn_r.at[way, j], target)

    def w_got(j, way):
        block = w_block(j, left if way == 0 else right, 0, 384)
        return remote(block, block, wn_s.at[way, j], wn_r.at[way, j], mate)

    def w_forward(j, way):
        block = w_block(j, left if way == 0 else right, 192 * way, 192)
        target = device(right if way == 0 else left, y, z, c)
        return remote(block, block, wf_s.at[way, j], wf_r.at[way, j], target)

    def w_far(j, way):
        block = w_block(j, turn(x, 2), 192 * way, 192)
        return remote(block, block, wf_s.at[way, j], wf_r.at[way, j], mate)

    def w_start(j):
        w_fetch(j).wait()
        w_send(j, 0).start()
        w_send(j, 1).start()

    def w_step(j):
        w_got(j, 0).wait_recv()
        w_forward(j, 0).start()
        w_got(j, 1).wait_recv()
        w_forward(j, 1).start()

        @pl.when(j + 2 < HEADS_OWN)
        def _():
            w_start(j + 2)

    @pl.loop(0, HEADS_OWN)
    def _(j):
        w_fetch(j).start()

    values = x_ref[...].reshape(512, 384)
    wide = values.astype(f32)
    square = wide * wide
    high = square.astype(bf16)
    low = (square - high.astype(f32)).astype(bf16)
    sums = row_sums(values)
    squares = row_sums(high) + row_sums(low)
    stats[col] = jnp.concatenate(
        [sums[0:1, i * 128 : i * 128 + 128] for i in range(4)]
        + [squares[0:1, i * 128 : i * 128 + 128] for i in range(4)],
        axis=0,
    )

    entered()

    def stat_copy(d, owner):
        block = stats.at[owner]
        return remote(block, block, st_s.at[d], st_r.at[d], col_peer(d))

    @pl.loop(1, 16)
    def _(d):
        stat_copy(d, col).start()

    w_start(0)
    w_start(1)

    @pl.loop(1, 16)
    def _(d):
        stat_copy(d, lax.rem(col + 16 - d, 16)).wait_recv()

    totals = jnp.sum(stats[...], axis=0) / D
    average = totals[0:4]
    rate = lax.rsqrt(totals[4:8] - average * average + epsilon)
    turned = jnp.transpose(jnp.concatenate([average, rate], axis=0))
    for g in range(4):
        block = x_ref[4 * g : 4 * g + 4].reshape(128, 384).astype(f32)
        block = (block - turned[:, g : g + 1]) * turned[:, g + 4 : g + 5] * gain_ref[...]
        normed[g] = block.astype(bf16)

    def a_block(owner):
        return a.at[y, c, :, pl.ds(aligned(owner * 384, 128), 384)]

    def ax_copy(d):
        return remote(
            normed.at[turn(x, d)], a_block(x), ax_s.at[d], ax_r.at[d], device(turn(x, d), y, z, c)
        )

    def ax_got(d):
        block = a_block(turn(x, 4 - d))
        return remote(block, block, ax_s.at[d], ax_r.at[d], mate)

    for d in (1, 3, 2):
        ax_copy(d).start()
    a[y, c, :, pl.ds(aligned(x * 384, 128), 384)] = normed[x]

    def spread_rows(owner):
        block = a_block(owner)
        for e in (1, 3, 2):
            remote(block, block, ay_s.at[e], ay_r.at[e], device(x, turn(y, e), z, c)).start()
        remote(block, block, ac_s.at[0], ac_r.at[0], mate).start()

    spread_rows(x)
    w_step(0)
    for d in (1, 3, 2):
        ax_got(d).wait_recv()
        spread_rows(turn(x, 4 - d))
    w_step(1)

    def c_copy(j, s, d):
        rows = pl.ds(aligned(s * 64, 64), 64)
        owner = turn(z, d)
        return remote(
            cs.at[j, owner, rows, :],
            cr.at[d - 1, j, rows, :],
            c_s.at[d - 1, j],
            c_r.at[d - 1, j],
            device(x, y, owner, c),
        )

    def c_all(j, d):
        return remote(
            cs.at[j, turn(z, d)], cr.at[d - 1, j], c_s.at[d - 1, j], c_r.at[d - 1, j], mate
        )

    def attend_head(j):
        for d in range(1, 4):
            c_all(j, d).wait_recv()
        projected = cs[j, z].astype(f32)
        for d in range(3):
            projected = projected + cr[d, j].astype(f32)
        queries = head_norm(projected[:, 0:128], qg_ref[...]).astype(bf16)
        keys = head_norm(projected[:, 128:256], kg_ref[...]).astype(bf16)
        out_ref[j] = attention(queries, keys, projected[:, 256:384].astype(bf16), 128 ** (-0.5))

    @pl.loop(0, HEADS_OWN)
    def _(j):
        w_far(j, 0).wait_recv()
        w_far(j, 1).wait_recv()

        @pl.loop(0, 4)
        def _(i):
            e = i + (i // 2) * (5 - 2 * i)
            s = turn(y, 4 - e)

            @pl.when(j == 0)
            def _():
                @pl.when(i > 0)
                def _():
                    got = a.at[s, c]
                    remote(got, got, ay_s.at[e], ay_r.at[e], mate).wait_recv()
                    remote(got, got, ac_s.at[e], ac_r.at[e], mate).start()

                other = a.at[s, 1 - c]
                remote(other, other, ac_s.at[e], ac_r.at[e], mate).wait_recv()

            product = jnp.dot(a[s].reshape(256, 1536), w[j], preferred_element_type=f32).astype(bf16)
            for core in range(2):
                for image in range(4):
                    first = core * 128 + image * 32
                    rows = pl.ds(aligned(s * 64 + core * 32, 32), 32)
                    cs[j, image, rows, :] = product[first : first + 32]
            for d in (1, 3, 2):
                c_copy(j, s, d).start()

        @pl.when(j + 2 < HEADS_OWN)
        def _():
            w_step(j + 2)

        @pl.when(j > 0)
        def _():
            attend_head(j - 1)

    attend_head(HEADS_OWN - 1)

    @pl.loop(1, 16)
    def _(d):
        stat_copy(d, col).wait_send()

    for d in range(1, 4):
        ax_copy(d).wait_send()
    for e in range(4):
        whole = a.at[turn(y, 4 - e), c]
        if e > 0:
            remote(whole, whole, ay_s.at[e], ay_r.at[e], mate).wait_send()
        remote(whole, whole, ac_s.at[e], ac_r.at[e], mate).wait_send()

    @pl.loop(0, HEADS_OWN)
    def _(j):
        for way in range(2):
            w_send(j, way).wait_send()
            w_forward(j, way).wait_send()
        for d in range(1, 4):
            c_all(j, d).wait_send()


VMEM = pl.BlockSpec(memory_space=pltpu.VMEM)
ANY = pl.BlockSpec(memory_space=pl.ANY)
DMA = pltpu.SemaphoreType.DMA


def encoder_heads(visible_patches, input_gain, encoder_project, query_gain, key_gain):
    return pl.pallas_call(
        encoder_kernel,
        out_shape=jax.ShapeDtypeStruct((HEADS_OWN, 256, 128), bf16),
        in_specs=[VMEM, VMEM, ANY, VMEM, VMEM],
        out_specs=VMEM,
        scratch_shapes=[
            pltpu.VMEM((16, 8, 128), f32),
            pltpu.VMEM((4, 128, 384), bf16),
            pltpu.VMEM((4, 2, 128, 1536), bf16),
            pltpu.VMEM((HEADS_OWN, 1536, 384), bf16),
            pltpu.VMEM((HEADS_OWN, 4, 256, 384), bf16),
            pltpu.VMEM((3, HEADS_OWN, 256, 384), bf16),
            DMA((HEADS_OWN,)),
            DMA((16,)), DMA((16,)),
            DMA((4,)), DMA((4,)),
            DMA((4,)), DMA((4,)),
            DMA((4,)), DMA((4,)),
            DMA((2, HEADS_OWN)), DMA((2, HEADS_OWN)),
            DMA((2, HEADS_OWN)), DMA((2, HEADS_OWN)),
            DMA((3, HEADS_OWN)), DMA((3, HEADS_OWN)),
        ],
        compiler_params=pltpu.CompilerParams(
            collective_id=0, has_side_effects=True, vmem_limit_bytes=56 << 20
        ),
        name="encoder_heads",
    )(
        visible_patches,
        input_gain.reshape(1, 384),
        encoder_project,
        query_gain.reshape(1, 128),
        key_gain.reshape(1, 128),
    )


def finish_norm(values, totals, squares, amount, gain_vector):
    average = totals / amount
    spread = squares / amount - average * average
    return (values - average) * lax.rsqrt(spread + epsilon) * gain_vector


def local_norm(values, gain_vector):
    average = jnp.mean(values, axis=-1, keepdims=True)
    spread = jnp.mean(values * values, axis=-1, keepdims=True) - average * average
    return (values - average) * lax.rsqrt(spread + epsilon) * gain_vector


def softmax_mix(queries, keys, values, factor):
    scores = (
        jnp.einsum("iqhd,ikhd->ihqk", queries, keys, preferred_element_type=jnp.float32) * factor
    )
    weights = jnp.exp(scores).astype(jnp.bfloat16)
    totals = jnp.sum(weights.astype(jnp.float32), axis=-1)
    mixture = jnp.einsum("ihqk,ikhd->iqhd", weights, values, preferred_element_type=jnp.float32)
    return (mixture / jnp.transpose(totals, (0, 2, 1))[..., None]).astype(jnp.bfloat16)


def local(
    visible_patches,
    input_gain,
    encoder_project,
    query_gain,
    key_gain,
    output_weight,
    final_gain,
    embed_weight,
    embed_bias,
    mask_token,
    position_embed,
    script_table,
    decoder_gain,
    decoder_project,
    decoder_query,
    decoder_key,
    decoder_output,
    head_gain,
    pixel_weight,
    pixel_bias,
    visible_index,
    script_index,
):
    own_images = script_index.shape[0]
    inputs = visible_patches.astype(jnp.float32)
    heads_out = encoder_heads(visible_patches, input_gain, encoder_project, query_gain, key_gain)
    heads_out = jnp.transpose(heads_out, (1, 0, 2)).reshape(1, 256, 768)
    terms = jnp.einsum(
        "itd,de->ite",
        lax.all_gather(heads_out, "col", axis=0, tiled=True),
        output_weight,
        preferred_element_type=jnp.float32,
    )
    residual = inputs + lax.psum_scatter(
        terms.astype(jnp.bfloat16), "row", scatter_dimension=1, tiled=True
    ).astype(jnp.float32)
    encoded = residual.astype(jnp.bfloat16)
    totals_final, squares_final = lax.psum(
        (
            jnp.sum(residual, axis=-1, keepdims=True),
            jnp.sum(residual * residual, axis=-1, keepdims=True),
        ),
        "col",
    )
    enc_normed = finish_norm(residual, totals_final, squares_final, D, final_gain).astype(
        jnp.bfloat16
    )
    window = enc_normed
    embedded = (
        lax.psum_scatter(
            jnp.einsum(
                "itd,de->ite", window, embed_weight, preferred_element_type=jnp.float32
            ).astype(jnp.bfloat16),
            "col",
            scatter_dimension=0,
            tiled=True,
        ).astype(jnp.float32)
        + embed_bias
    ).astype(jnp.bfloat16)
    visible_rows = lax.all_gather(embedded, "row", axis=1, tiled=True)
    extent = position_embed.shape[0]
    places = lax.axis_index("row") * extent + jnp.arange(extent, dtype=jnp.int32)
    select = (visible_index[:, None, :] == places[None, :, None]).astype(jnp.bfloat16)
    present = jnp.sum(select.astype(jnp.float32), axis=2, keepdims=True)
    gathered_rows = jnp.einsum(
        "ipk,ikd->ipd", select, visible_rows, preferred_element_type=jnp.float32
    )
    script_ids = jnp.arange(script_table.shape[0], dtype=jnp.int32)
    labels = (script_index[:, None] == script_ids[None, :]).astype(jnp.bfloat16)
    scripted = jnp.dot(labels, script_table, preferred_element_type=jnp.float32)
    tokens = (
        gathered_rows
        + (1.0 - present) * mask_token
        + position_embed.astype(jnp.float32)
        + scripted[:, None, :]
    )
    dec_normed = local_norm(tokens, decoder_gain).astype(jnp.bfloat16)
    decoder_proj = jnp.einsum(
        "ipd,de->ipe", dec_normed, decoder_project, preferred_element_type=jnp.float32
    )
    head_dim = decoder_query.shape[0]
    head_count = DD // head_dim
    pieces = decoder_proj.reshape(own_images, extent, head_count, 3, head_dim)
    queries = local_norm(pieces[:, :, :, 0], decoder_query).astype(jnp.bfloat16)
    keys = local_norm(pieces[:, :, :, 1], decoder_key).astype(jnp.bfloat16)
    values = pieces[:, :, :, 2].astype(jnp.bfloat16)
    factor = head_dim ** (-0.5)
    packed = jnp.stack(
        [
            queries.reshape(own_images, extent, DD),
            keys.reshape(own_images, extent, DD),
            values.reshape(own_images, extent, DD),
        ],
        axis=1,
    )
    received = lax.all_to_all(packed, "row", split_axis=3, concat_axis=2, tiled=True)
    records = received.shape[0]
    positions = received.shape[2]
    group = received.shape[3] // head_dim
    parts = received.reshape(records, 3, positions, group, head_dim)
    result = softmax_mix(parts[:, 0], parts[:, 1], parts[:, 2], factor)
    result = result.reshape(records, positions, group * head_dim)
    dec_attended = lax.all_to_all(result, "row", split_axis=1, concat_axis=2, tiled=True)
    decoded = tokens + jnp.einsum(
        "ipd,de->ipe", dec_attended, decoder_output, preferred_element_type=jnp.float32
    )
    head_normed = local_norm(decoded, head_gain).astype(jnp.bfloat16)
    predicted = (
        jnp.einsum("ipd,de->ipe", head_normed, pixel_weight, preferred_element_type=jnp.float32)
        + pixel_bias
    ).astype(jnp.bfloat16)
    return (encoded, predicted)


def solution(mesh):
    return jax.shard_map(
        local,
        mesh=mesh,
        in_specs=(
            P(None, "row", "col"),
            P("col"),
            P("col", "row"),
            P(),
            P(),
            P("row", "col"),
            P("col"),
            P("col", None),
            P(),
            P(),
            P("row", None),
            P(),
            P(),
            P(),
            P(),
            P(),
            P(),
            P(),
            P(),
            P(),
            P("col", None),
            P("col"),
        ),
        out_specs=(P(None, "row", "col"), P("col", "row", None)),
        check_vma=False,
    )
```

```python
import jax
import jax.numpy as jnp
from jax import lax
from jax.experimental import pallas as pl
from jax.experimental.pallas import tpu as pltpu
from jax.sharding import PartitionSpec as P

D = 6144
DD = 1024
HEADS_OWN = 6
CHUNKS = 8
MESH = pl.DeviceIdType.MESH
bf16 = jnp.bfloat16
f32 = jnp.float32

epsilon = 1e-06
LAST = (((1,), (1,)), ((), ()))


def turn(i, by):
    return lax.rem(i + by, 4)


def near(i):
    return i + (i // 2) * (5 - 2 * i)


def device(x, y, z, c):
    return (y * 2 + c, x * 4 + z)


def remote(src, dst, send_sem, recv_sem, where):
    return pltpu.make_async_remote_copy(
        src_ref=src,
        dst_ref=dst,
        send_sem=send_sem,
        recv_sem=recv_sem,
        device_id=where,
        device_id_type=MESH,
    )


def aligned(index, multiple):
    return pl.multiple_of(index, multiple)


def norm(values, gain_vector):
    amount = values.shape[-1]
    average = jnp.sum(values, axis=-1, keepdims=True) / amount
    spread = jnp.sum(values * values, axis=-1, keepdims=True) / amount - average * average
    return (values - average) * lax.rsqrt(spread + epsilon) * gain_vector


def pair_norm(values, gain_vector):
    first = lax.broadcasted_iota(jnp.int32, values.shape, 1) < 64

    def mean(v):
        one = jnp.sum(jnp.where(first, v, 0.0), axis=-1, keepdims=True)
        two = jnp.sum(jnp.where(first, 0.0, v), axis=-1, keepdims=True)
        return jnp.where(first, one, two) / 64

    average = mean(values)
    spread = mean(values * values) - average * average
    return (values - average) * lax.rsqrt(spread + epsilon) * gain_vector


def attention(queries, keys, values, factor):
    scores = lax.dot_general(queries, keys, LAST, preferred_element_type=f32) * factor
    weights = jnp.exp(scores).astype(bf16)
    totals = jnp.sum(weights.astype(f32), axis=-1, keepdims=True)
    mixture = jnp.dot(weights, values, preferred_element_type=f32)
    return (mixture / totals).astype(bf16)


def kernel(
    x_ref, ig_ref, w_ref, qg_ref, kg_ref, wo_ref, fg_ref, ew_ref, eb_ref, mask_ref, pos_ref,
    script_ref, dg_ref, dp_ref, dqg_ref, dkg_ref, do_ref, hg_ref, pw_ref, pb_ref, vi_ref, si_ref,
    enc_ref, pred_ref,
    gains, raw, stats, a, w, cs, cr, att, po, pr, yr, res, en, es, ew, pos, dpw, dow, pxw,
    eo, er, vis, tok, dq, dk, dv, dm, da,
    l_s, w_s, g_s, g_r, x_s, x_r, st_s, st_r, ay_s, ay_r, ac_s, ac_r, wn_s, wn_r, wf_s, wf_r,
    c_s, c_r, t_s, t_r, p_s, p_r, pc_s, pc_r, ex_s, ex_r, ey_s, ey_r, ec_s, ec_r,
    m_s, m_r, y_s, y_r, en_s, en_r, eb_s, eb_r, v_s, v_r, d_s, d_r,
):
    row, col = lax.axis_index("row"), lax.axis_index("col")
    x, y, z, c = col // 4, row // 2, lax.rem(col, 4), lax.rem(row, 2)
    mate = device(x, y, z, 1 - c)
    right, left = turn(x, 1), turn(x, 3)

    def x_peer(d):
        return device(turn(x, d), y, z, c)

    def y_peer(d):
        return device(x, turn(y, d), z, c)

    def z_peer(d):
        return device(x, y, turn(z, d), c)

    def row_peer(e, m):
        return device(x, turn(y, e), z, c + m - 2 * c * m)

    def row_from(e, m):
        return turn(y, 4 - e) * 2 + c + m - 2 * c * m

    def w_block(j, owner, start, size):
        return w.at[j, pl.ds(aligned(owner * 384 + start, 192), size), :]

    def w_fetch(j):
        return pltpu.make_async_copy(
            w_ref.at[:, pl.ds(aligned(j * 384, 128), 384)], w_block(j, x, 0, 384), w_s.at[j]
        )

    @pl.loop(0, HEADS_OWN)
    def _(j):
        w_fetch(j).start()

    fetches = [
        pltpu.make_async_copy(wo_ref.at[0:384], w_block(6, x, 0, 384), l_s.at[0]),
        pltpu.make_async_copy(wo_ref.at[384:768], w_block(7, x, 0, 384), l_s.at[1]),
        pltpu.make_async_copy(ew_ref, ew.at[x], l_s.at[2]),
        pltpu.make_async_copy(pos_ref, pos.at[y, c], l_s.at[3]),
        pltpu.make_async_copy(
            dp_ref.at[:, pl.ds(aligned(row * 384, 128), 384)], dpw, l_s.at[4]
        ),
        pltpu.make_async_copy(do_ref, dow, l_s.at[5]),
        pltpu.make_async_copy(pw_ref, pxw, l_s.at[6]),
    ]
    for fetch in fetches:
        fetch.start()

    first_row = lax.broadcasted_iota(jnp.int32, (8, 384), 0) == 0
    gains[x] = jnp.where(first_row, ig_ref[...], fg_ref[...])
    raw[x] = x_ref[pl.ds(x * 4, 4)]

    barrier = pltpu.get_barrier_semaphore()
    peers = (
        [x_peer(d) for d in range(1, 4)]
        + [z_peer(d) for d in range(1, 4)]
        + [row_peer(k // 2, k % 2) for k in range(1, 8)]
    )
    for peer in peers:
        pl.semaphore_signal(barrier, inc=1, device_id=peer, device_id_type=MESH)
    pl.semaphore_wait(barrier, len(peers))

    def raw_copy(d):
        there = turn(x, d)
        return remote(x_ref.at[pl.ds(there * 4, 4)], raw.at[x], x_s.at[d], x_r.at[d], x_peer(d))

    def gain_copy(d):
        return remote(gains.at[x], gains.at[x], g_s.at[d], g_r.at[d], x_peer(d))

    for d in (1, 3, 2):
        gain_copy(d).start()
        raw_copy(d).start()

    def w_send(j, way):
        block = w_block(j, x, 0, 384)
        target = device(right if way == 0 else left, y, z, c)
        return remote(block, block, wn_s.at[way, j], wn_r.at[way, j], target)

    def w_got(j, way):
        block = w_block(j, left if way == 0 else right, 0, 384)
        return remote(block, block, wn_s.at[way, j], wn_r.at[way, j], mate)

    def w_forward(j, way):
        block = w_block(j, left if way == 0 else right, 192 * way, 192)
        target = device(right if way == 0 else left, y, z, c)
        return remote(block, block, wf_s.at[way, j], wf_r.at[way, j], target)

    def w_far(j, way):
        block = w_block(j, turn(x, 2), 192 * way, 192)
        return remote(block, block, wf_s.at[way, j], wf_r.at[way, j], mate)

    def w_start(j):
        w_send(j, 0).start()
        w_send(j, 1).start()

    def w_step(j):
        w_got(j, 0).wait_recv()
        w_forward(j, 0).start()
        w_got(j, 1).wait_recv()
        w_forward(j, 1).start()

        @pl.when(j + 2 < CHUNKS)
        def _():
            w_start(j + 2)

    @pl.loop(0, HEADS_OWN)
    def _(j):
        w_fetch(j).wait()

    fetches[0].wait()
    fetches[1].wait()
    w_start(0)
    w_start(1)

    def stat_copy(n, d, owner):
        block = stats.at[n, owner]
        return remote(block, block, st_s.at[n, d], st_r.at[n, d], z_peer(d))

    def share_stats(n, total, square):
        lane = lax.broadcasted_iota(jnp.int32, (128, 128), 1)
        stats[n, z] = jnp.transpose(jnp.where(lane == 0, total, square))[0:8]
        for d in (1, 3, 2):
            stat_copy(n, d, z).start()
        for d in (1, 3, 2):
            stat_copy(n, d, turn(z, 4 - d)).wait_recv()
        sums = jnp.transpose(jnp.sum(stats[n], axis=0))
        average = sums[:, 0:1] / D
        spread = sums[:, 1:2] / D - average * average
        return average, lax.rsqrt(spread + epsilon)

    for d in (1, 3, 2):
        there = turn(x, 4 - d)
        remote(gains.at[there], gains.at[there], g_s.at[d], g_r.at[d], mate).wait_recv()
        remote(raw.at[there], raw.at[there], x_s.at[d], x_r.at[d], mate).wait_recv()
    total, square = 0.0, 0.0
    for g in range(4):
        block = raw[g].reshape(128, 384).astype(f32)
        total = total + jnp.sum(block, axis=-1, keepdims=True)
        square = square + jnp.sum(block * block, axis=-1, keepdims=True)
    average, rate = share_stats(0, total, square)
    for g in range(4):
        block = raw[g].reshape(128, 384).astype(f32)
        block = (block - average) * rate * gains[g, 0:1, :]
        a[y, c, :, 384 * g : 384 * g + 384] = block.astype(bf16)

    def spread_rows(block, s_y, r_y, s_c, r_c):
        for e in (1, 3, 2):
            remote(block, block, s_y.at[e], r_y.at[e], y_peer(e)).start()
        remote(block, block, s_c.at[0], r_c.at[0], mate).start()

    spread_rows(a.at[y, c], ay_s, ay_r, ac_s, ac_r)
    w_step(0)
    w_step(1)

    def c_copy(j, s, d):
        rows = pl.ds(aligned(s * 64, 64), 64)
        return remote(
            cs.at[j, turn(z, d), rows, :],
            cr.at[d - 1, j, rows, :],
            c_s.at[d - 1, j],
            c_r.at[d - 1, j],
            z_peer(d),
        )

    def c_all(j, d):
        return remote(
            cs.at[j, turn(z, d)], cr.at[d - 1, j], c_s.at[d - 1, j], c_r.at[d - 1, j], mate
        )

    def t_copy(j, d):
        block = att.at[z, :, pl.ds(aligned(j * 128, 128), 128)]
        return remote(block, block, t_s.at[d], t_r.at[d], z_peer(d))

    def attend_head(j):
        for d in range(1, 4):
            c_all(j, d).wait_recv()
        projected = cs[j, z].astype(f32)
        for d in range(3):
            projected = projected + cr[d, j].astype(f32)
        queries = norm(projected[:, 0:128], qg_ref[...]).astype(bf16)
        keys = norm(projected[:, 128:256], kg_ref[...]).astype(bf16)
        mixed = attention(queries, keys, projected[:, 256:384].astype(bf16), 128 ** (-0.5))
        att[z, :, pl.ds(aligned(j * 128, 128), 128)] = mixed
        for d in (1, 3, 2):
            t_copy(j, d).start()

    def ew_part(owner, part):
        return ew.at[owner, pl.ds(aligned(part * 48, 16), 48), :]

    def ex_copy(d):
        block = ew_part(x, row)
        return remote(block, block, ex_s.at[d], ex_r.at[d], x_peer(d))

    def ex_got(d):
        block = ew_part(turn(x, 4 - d), row)
        return remote(block, block, ex_s.at[d], ex_r.at[d], mate)

    def ey_copy(d, e):
        block = ew_part(turn(x, 4 - d), row)
        return remote(block, block, ey_s.at[d, e], ey_r.at[d, e], y_peer(e))

    def ey_got(d, e):
        block = ew_part(turn(x, 4 - d), turn(y, 4 - e) * 2 + c)
        return remote(block, block, ey_s.at[d, e], ey_r.at[d, e], mate)

    def ec_copy(d, e):
        block = ew_part(turn(x, 4 - d), turn(y, 4 - e) * 2 + c)
        return remote(block, block, ec_s.at[d, e], ec_r.at[d, e], mate)

    def ec_got(d, e):
        block = ew_part(turn(x, 4 - d), turn(y, 4 - e) * 2 + 1 - c)
        return remote(block, block, ec_s.at[d, e], ec_r.at[d, e], mate)

    @pl.loop(0, HEADS_OWN)
    def _(j):
        w_far(j, 0).wait_recv()
        w_far(j, 1).wait_recv()

        @pl.loop(0, 4)
        def _(i):
            e = near(i)
            s = turn(y, 4 - e)

            @pl.when(j == 0)
            def _():
                @pl.when(i > 0)
                def _():
                    got = a.at[s, c]
                    remote(got, got, ay_s.at[e], ay_r.at[e], mate).wait_recv()
                    remote(got, got, ac_s.at[e], ac_r.at[e], mate).start()

                other = a.at[s, 1 - c]
                remote(other, other, ac_s.at[e], ac_r.at[e], mate).wait_recv()

            product = jnp.dot(a[s].reshape(256, 1536), w[j], preferred_element_type=f32).astype(bf16)
            for core in range(2):
                for image in range(4):
                    first = core * 128 + image * 32
                    rows = pl.ds(aligned(s * 64 + core * 32, 32), 32)
                    cs[j, image, rows, :] = product[first : first + 32]
            for d in (1, 3, 2):
                c_copy(j, s, d).start()

        @pl.when(j == 1)
        def _():
            fetches[2].wait()
            fetches[3].wait()
            spread_rows(pos.at[y, c], p_s, p_r, pc_s, pc_r)
            for d in (1, 3, 2):
                ex_copy(d).start()

        @pl.when(j == 3)
        def _():
            for e in (1, 3, 2):
                got = pos.at[turn(y, 4 - e), c]
                remote(got, got, p_s.at[e], p_r.at[e], mate).wait_recv()
                remote(got, got, pc_s.at[e], pc_r.at[e], mate).start()
            for d in (1, 3, 2):
                ex_got(d).wait_recv()
                for e in (1, 3, 2):
                    ey_copy(d, e).start()
                ec_copy(d, 0).start()

        @pl.when(j > 0)
        def _():
            attend_head(j - 1)

        w_step(j + 2)

    attend_head(HEADS_OWN - 1)
    for e in (1, 3, 2):
        for d in (1, 3, 2):
            ey_got(d, e).wait_recv()
            ec_copy(d, e).start()
    for d in (1, 3, 2):
        whole = att.at[turn(z, 4 - d)]
        remote(whole, whole, t_s.at[d], t_r.at[d], mate).wait_recv()

    def block_at(i):
        return turn(x, 4 - near(i))

    def mate_copy(i):
        there = block_at(i)
        return remote(po.at[there, 1 - c], pr.at[there], m_s.at[i], m_r.at[i], mate)

    def y_copy(i, e):
        there = block_at(i)
        return remote(
            po.at[there, c, turn(y, e)], yr.at[e - 1, there], y_s.at[e, i], y_r.at[e, i], y_peer(e)
        )

    def reduce_rows(i):
        there = block_at(i)
        mate_copy(i).wait_recv()
        both = po[there, c].astype(f32) + pr[there].astype(f32)
        po[there, c] = both.astype(bf16)
        for e in (1, 3, 2):
            y_copy(i, e).start()

    @pl.loop(0, 4)
    def _(i):
        there = block_at(i)

        @pl.when(i == 3)
        def _():
            for j in (6, 7):
                w_far(j, 0).wait_recv()
                w_far(j, 1).wait_recv()

        rows = pl.ds(aligned(there * 384, 384), 384)
        both = att[...].reshape(1024, 768)
        product = jnp.dot(both[:, 0:384], w[6, rows, :], preferred_element_type=f32)
        product = product + jnp.dot(both[:, 384:768], w[7, rows, :], preferred_element_type=f32)
        product = product.astype(bf16)
        for image in range(4):
            for part in range(8):
                first = image * 256 + part * 32
                po[there, part % 2, part // 2, image * 32 : image * 32 + 32, :] = product[
                    first : first + 32
                ]
        mate_copy(i).start()

        @pl.when(i > 0)
        def _():
            reduce_rows(i - 1)

    reduce_rows(3)

    res[...] = jnp.zeros_like(res)

    def enc_copy(d):
        there = turn(x, d)
        return remote(
            es.at[there], enc_ref.at[pl.ds(x * 4, 4)], en_s.at[d], en_r.at[d], x_peer(d)
        )

    total, square = 0.0, 0.0
    for i in range(4):
        there = block_at(i)
        for e in (1, 3, 2):
            y_copy(i, e).wait_recv()
        block = raw[there].reshape(128, 384).astype(f32) + po[there, c, y].astype(f32)
        for e in range(3):
            block = block + yr[e, there].astype(f32)
        res[there] = block
        es[there] = block.astype(bf16).reshape(4, 32, 384)
        total = total + jnp.sum(block, axis=-1, keepdims=True)
        square = square + jnp.sum(block * block, axis=-1, keepdims=True)
    average, rate = share_stats(1, total, square)
    for g in range(4):
        block = (res[g] - average) * rate * gains[g, 1:2, :]
        en[:, 384 * g : 384 * g + 384] = block.astype(bf16)
    for d in (1, 3, 2):
        enc_copy(d).start()
    enc_ref[pl.ds(x * 4, 4)] = es[x]

    for d in (1, 3, 2):
        for e in range(4):
            ec_got(d, e).wait_recv()
    product = jnp.dot(en[...], ew[...].reshape(1536, DD), preferred_element_type=f32)
    eo[...] = product.astype(bf16).reshape(4, 32, DD)

    def eb_copy(d):
        return remote(eo.at[turn(z, d)], er.at[d - 1], eb_s.at[d], eb_r.at[d], z_peer(d))

    for d in (1, 3, 2):
        eb_copy(d).start()
    embedded = eo[z].astype(f32)
    for d in (1, 3, 2):
        eb_copy(d).wait_recv()
        embedded = embedded + er[d - 1].astype(f32)
    vis[row] = (embedded + eb_ref[...]).astype(bf16)

    def vis_copy(k):
        block = vis.at[row]
        return remote(block, block, v_s.at[k], v_r.at[k], row_peer(k // 2, k % 2))

    for k in (4, 5, 2, 3, 6, 7, 1):
        vis_copy(k).start()

    ids = lax.broadcasted_iota(jnp.int32, script_ref.shape, 0)
    scripted = jnp.sum(
        jnp.where(ids == si_ref[...], script_ref[...].astype(f32), 0.0), axis=0, keepdims=True
    )
    fetches[4].wait()
    for e in range(4):
        got = pos.at[turn(y, 4 - e), 1 - c]
        remote(got, got, pc_s.at[e], pc_r.at[e], mate).wait_recv()
    dv[:, 128:256] = jnp.ones((1024, 128), bf16)
    for k in range(1, 8):
        block = vis.at[row_from(k // 2, k % 2)]
        remote(block, block, v_s.at[k], v_r.at[k], mate).wait_recv()
    query_gain = jnp.concatenate([dqg_ref[...], dqg_ref[...]], axis=1)
    key_gain = jnp.concatenate([dkg_ref[...], dkg_ref[...]], axis=1)

    @pl.loop(0, 4)
    def _(i):
        rows = pl.ds(aligned(i * 256, 256), 256)
        positions = lax.broadcasted_iota(jnp.int32, (256, 256), 0) + i * 256
        select = jnp.where(positions == vi_ref[...], 1.0, 0.0)
        present = jnp.sum(select, axis=1, keepdims=True)
        tokens = jnp.dot(
            select.astype(bf16), vis[...].reshape(256, DD), preferred_element_type=f32
        )
        tokens = tokens + (1.0 - present) * mask_ref[...]
        tokens = tokens + pos[i].reshape(256, DD).astype(f32) + scripted
        tok[rows, :] = tokens
        normed = norm(tokens, dg_ref[...]).astype(bf16)
        made = jnp.dot(normed, dpw[...], preferred_element_type=f32)
        queries = jnp.concatenate([made[:, 0:64], made[:, 192:256]], axis=1)
        keys = jnp.concatenate([made[:, 64:128], made[:, 256:320]], axis=1)
        values = jnp.concatenate([made[:, 128:192], made[:, 320:384]], axis=1)
        queries = pair_norm(queries, query_gain)
        first = lax.broadcasted_iota(jnp.int32, queries.shape, 1) < 64
        dq[0, rows, :] = jnp.where(first, queries, 0.0).astype(bf16)
        dq[1, rows, :] = jnp.where(first, 0.0, queries).astype(bf16)
        dk[rows, :] = pair_norm(keys, key_gain).astype(bf16)
        dv[rows, 0:128] = values.astype(bf16)

    def mix_copy(e, m):
        owner = turn(y, e) * 2 + c + m - 2 * c * m
        block = da.at[:, pl.ds(aligned(row * 128, 128), 128)]
        return remote(dm.at[owner], block, d_s.at[e, m], d_r.at[e, m], row_peer(e, m))

    def mix_got(e, m):
        block = da.at[:, pl.ds(aligned(row_from(e, m) * 128, 128), 128)]
        return remote(block, block, d_s.at[e, m], d_r.at[e, m], mate)

    @pl.loop(0, 4)
    def _(i):
        e = near(3 - i)
        there = turn(y, e)
        rows = pl.ds(aligned(there * 256, 256), 256)
        mixtures = []
        for h in range(2):
            scores = lax.dot_general(dq[h, rows, :], dk[...], LAST, preferred_element_type=f32)
            weights = jnp.exp(scores * 64 ** (-0.5)).astype(bf16)
            both = jnp.dot(weights, dv[...], preferred_element_type=f32)
            mixtures.append(both[:, 0:128] / both[:, 128:256])
        first = lax.broadcasted_iota(jnp.int32, (256, 128), 1) < 64
        mixed = jnp.where(first, mixtures[0], mixtures[1]).astype(bf16)
        dm[there * 2] = mixed[0:128]
        dm[there * 2 + 1] = mixed[128:256]

        @pl.when(e > 0)
        def _():
            mix_copy(e, 0).start()

        mix_copy(e, 1).start()

    da[:, pl.ds(aligned(row * 128, 128), 128)] = dm[row]
    fetches[5].wait()
    fetches[6].wait()
    for k in range(1, 8):
        mix_got(k // 2, k % 2).wait_recv()
    decoded = tok[pl.ds(aligned(row * 128, 128), 128), :] + jnp.dot(
        da[...], dow[...], preferred_element_type=f32
    )
    normed = norm(decoded, hg_ref[...]).astype(bf16)
    predicted = jnp.dot(normed, pxw[...], preferred_element_type=f32) + pb_ref[...]
    pred_ref[0] = predicted.astype(bf16)

    for d in range(1, 4):
        block = enc_ref.at[pl.ds(turn(x, 4 - d) * 4, 4)]
        remote(block, block, en_s.at[d], en_r.at[d], mate).wait_recv()
        enc_copy(d).wait_send()
        gain_copy(d).wait_send()
        raw_copy(d).wait_send()
        stat_copy(0, d, z).wait_send()
        stat_copy(1, d, z).wait_send()
        ex_copy(d).wait_send()
        eb_copy(d).wait_send()
        whole = att.at[z]
        remote(whole, whole, t_s.at[d], t_r.at[d], mate).wait_send()
        ec_copy(d, 0).wait_send()
        for e in range(1, 4):
            ey_copy(d, e).wait_send()
            ec_copy(d, e).wait_send()
    for e in range(4):
        for block, s_y, r_y, s_c, r_c in (
            (a, ay_s, ay_r, ac_s, ac_r),
            (pos, p_s, p_r, pc_s, pc_r),
        ):
            if e > 0:
                own = block.at[y, c]
                remote(own, own, s_y.at[e], r_y.at[e], mate).wait_send()
            passed = block.at[turn(y, 4 - e), c]
            remote(passed, passed, s_c.at[e], r_c.at[e], mate).wait_send()
        mate_copy(e).wait_send()
        for i in range(1, 4):
            y_copy(e, i).wait_send()
    for k in range(1, 8):
        vis_copy(k).wait_send()
        mix_copy(k // 2, k % 2).wait_send()

    @pl.loop(0, CHUNKS)
    def _(j):
        for way in range(2):
            w_send(j, way).wait_send()
            w_forward(j, way).wait_send()

    @pl.loop(0, HEADS_OWN)
    def _(j):
        for d in range(1, 4):
            c_all(j, d).wait_send()


VMEM = pl.BlockSpec(memory_space=pltpu.VMEM)
ANY = pl.BlockSpec(memory_space=pl.ANY)


def local(
    visible_patches,
    input_gain,
    encoder_project,
    query_gain,
    key_gain,
    output_weight,
    final_gain,
    embed_weight,
    embed_bias,
    mask_token,
    position_embed,
    script_table,
    decoder_gain,
    decoder_project,
    decoder_query,
    decoder_key,
    decoder_output,
    head_gain,
    pixel_weight,
    pixel_bias,
    visible_index,
    script_index,
):
    def flat(vector):
        return vector.reshape(1, -1)

    dma = pltpu.SemaphoreType.DMA
    two = [dma((4,)), dma((4,))]
    return pl.pallas_call(
        kernel,
        out_shape=(
            jax.ShapeDtypeStruct((16, 32, 384), bf16),
            jax.ShapeDtypeStruct((1, 128, 768), bf16),
        ),
        in_specs=[
            VMEM, VMEM, ANY, VMEM, VMEM, ANY, VMEM, ANY, VMEM, VMEM, ANY,
            VMEM, VMEM, ANY, VMEM, VMEM, ANY, VMEM, ANY, VMEM, VMEM, VMEM,
        ],
        out_specs=(VMEM, VMEM),
        scratch_shapes=[
            pltpu.VMEM((4, 8, 384), f32),
            pltpu.VMEM((4, 4, 32, 384), bf16),
            pltpu.VMEM((2, 4, 8, 128), f32),
            pltpu.VMEM((4, 2, 128, 1536), bf16),
            pltpu.VMEM((CHUNKS, 1536, 384), bf16),
            pltpu.VMEM((HEADS_OWN, 4, 256, 384), bf16),
            pltpu.VMEM((3, HEADS_OWN, 256, 384), bf16),
            pltpu.VMEM((4, 256, 768), bf16),
            pltpu.VMEM((4, 2, 4, 128, 384), bf16),
            pltpu.VMEM((4, 4, 128, 384), bf16),
            pltpu.VMEM((3, 4, 128, 384), bf16),
            pltpu.VMEM((4, 128, 384), f32),
            pltpu.VMEM((128, 1536), bf16),
            pltpu.VMEM((4, 4, 32, 384), bf16),
            pltpu.VMEM((4, 384, DD), bf16),
            pltpu.VMEM((4, 2, 128, DD), bf16),
            pltpu.VMEM((DD, 384), bf16),
            pltpu.VMEM((DD, DD), bf16),
            pltpu.VMEM((DD, 768), bf16),
            pltpu.VMEM((4, 32, DD), bf16),
            pltpu.VMEM((3, 32, DD), bf16),
            pltpu.VMEM((8, 32, DD), bf16),
            pltpu.VMEM((1024, DD), f32),
            pltpu.VMEM((2, 1024, 128), bf16),
            pltpu.VMEM((1024, 128), bf16),
            pltpu.VMEM((1024, 256), bf16),
            pltpu.VMEM((8, 128, 128), bf16),
            pltpu.VMEM((128, DD), bf16),
            dma((7,)),
            dma((HEADS_OWN,)),
            *two,
            *two,
            dma((2, 4)), dma((2, 4)),
            *two,
            *two,
            dma((2, CHUNKS)), dma((2, CHUNKS)),
            dma((2, CHUNKS)), dma((2, CHUNKS)),
            dma((3, HEADS_OWN)), dma((3, HEADS_OWN)),
            *two,
            *two,
            *two,
            *two,
            dma((4, 4)), dma((4, 4)),
            dma((4, 4)), dma((4, 4)),
            *two,
            dma((4, 4)), dma((4, 4)),
            *two,
            *two,
            dma((8,)), dma((8,)),
            dma((4, 2)), dma((4, 2)),
        ],
        compiler_params=pltpu.CompilerParams(
            collective_id=0, has_side_effects=True, vmem_limit_bytes=62 << 20
        ),
        name="masked_patches",
    )(
        visible_patches, flat(input_gain), encoder_project, flat(query_gain), flat(key_gain),
        output_weight, flat(final_gain), embed_weight, flat(embed_bias), flat(mask_token),
        position_embed, script_table, flat(decoder_gain), decoder_project, flat(decoder_query),
        flat(decoder_key), decoder_output, flat(head_gain), pixel_weight, flat(pixel_bias),
        visible_index, flat(script_index),
    )


def solution(mesh):
    return jax.shard_map(
        local,
        mesh=mesh,
        in_specs=(
            P(None, "row", "col"),
            P("col"),
            P("col", "row"),
            P(),
            P(),
            P("row", "col"),
            P("col"),
            P("col", None),
            P(),
            P(),
            P("row", None),
            P(),
            P(),
            P(),
            P(),
            P(),
            P(),
            P(),
            P(),
            P(),
            P("col", None),
            P("col"),
        ),
        out_specs=(P(None, "row", "col"), P("col", "row", None)),
        check_vma=False,
    )
```

```python
import jax
import jax.numpy as jnp
from jax import lax
from jax.experimental import pallas as pl
from jax.experimental.pallas import tpu as pltpu
from jax.sharding import PartitionSpec as P

D = 6144
DD = 1024
HEADS_OWN = 6
CHUNKS = 8
MESH = pl.DeviceIdType.MESH
bf16 = jnp.bfloat16
f32 = jnp.float32

epsilon = 1e-06
LAST = (((1,), (1,)), ((), ()))


def turn(i, by):
    return lax.rem(i + by, 4)


def near(i):
    return i + (i // 2) * (5 - 2 * i)


def device(x, y, z, c):
    return (y * 2 + c, x * 4 + z)


def remote(src, dst, send_sem, recv_sem, where):
    return pltpu.make_async_remote_copy(
        src_ref=src,
        dst_ref=dst,
        send_sem=send_sem,
        recv_sem=recv_sem,
        device_id=where,
        device_id_type=MESH,
    )


def aligned(index, multiple):
    return pl.multiple_of(index, multiple)


def norm(values, gain_vector):
    amount = values.shape[-1]
    average = jnp.sum(values, axis=-1, keepdims=True) / amount
    spread = jnp.sum(values * values, axis=-1, keepdims=True) / amount - average * average
    return (values - average) * lax.rsqrt(spread + epsilon) * gain_vector


def pair_norm(values, gain_vector):
    first = lax.broadcasted_iota(jnp.int32, values.shape, 1) < 64

    def mean(v):
        one = jnp.sum(jnp.where(first, v, 0.0), axis=-1, keepdims=True)
        two = jnp.sum(jnp.where(first, 0.0, v), axis=-1, keepdims=True)
        return jnp.where(first, one, two) / 64

    average = mean(values)
    spread = mean(values * values) - average * average
    return (values - average) * lax.rsqrt(spread + epsilon) * gain_vector


def attention(queries, keys, values, factor):
    scores = lax.dot_general(queries, keys, LAST, preferred_element_type=f32) * factor
    weights = jnp.exp(scores).astype(bf16)
    totals = jnp.sum(weights.astype(f32), axis=-1, keepdims=True)
    mixture = jnp.dot(weights, values, preferred_element_type=f32)
    return (mixture / totals).astype(bf16)


def kernel(
    x_ref, ig_ref, w_ref, qg_ref, kg_ref, wo_ref, fg_ref, ew_ref, eb_ref, mask_ref, pos_ref,
    script_ref, dg_ref, dp_ref, dqg_ref, dkg_ref, do_ref, hg_ref, pw_ref, pb_ref, vi_ref, si_ref,
    enc_ref, pred_ref,
    gains, raw, stats, a, w, cs, cr, hop, att, po, pr, yr, res, en, es, ew, pos, dpw, dow, pxw,
    eo, er, vis, scr, sel, tok, tokv, dq, dk, dv, base, vq, vk, vv, dm, da,
    l_s, w_s, g_s, g_r, x_s, x_r, st_s, st_r, ay_s, ay_r, ac_s, ac_r, wn_s, wn_r, wf_s, wf_r,
    h_s, h_r, c_s, c_r, t_s, t_r, p_s, p_r, pc_s, pc_r, ex_s, ex_r, ec_s, ec_r,
    m_s, m_r, y_s, y_r, en_s, en_r, eb_s, eb_r, v_s, v_r, d_s, d_r,
):
    row, col = lax.axis_index("row"), lax.axis_index("col")
    x, y, z, c = col // 4, row // 2, lax.rem(col, 4), lax.rem(row, 2)
    mate = device(x, y, z, 1 - c)
    right, left = turn(x, 1), turn(x, 3)

    def x_peer(d):
        return device(turn(x, d), y, z, c)

    def y_peer(d):
        return device(x, turn(y, d), z, c)

    def z_peer(d):
        return device(x, y, turn(z, d), c)

    def row_peer(e, m):
        return device(x, turn(y, e), z, c + m - 2 * c * m)

    def row_from(e, m):
        return turn(y, 4 - e) * 2 + c + m - 2 * c * m

    def w_block(j, owner, start, size):
        return w.at[j, pl.ds(aligned(owner * 384 + start, 192), size), :]

    def w_fetch(j):
        return pltpu.make_async_copy(
            w_ref.at[:, pl.ds(aligned(j * 384, 128), 384)], w_block(j, x, 0, 384), w_s.at[j]
        )

    @pl.loop(0, HEADS_OWN)
    def _(j):
        w_fetch(j).start()

    fetches = [
        pltpu.make_async_copy(wo_ref.at[0:384], w_block(6, x, 0, 384), l_s.at[0]),
        pltpu.make_async_copy(wo_ref.at[384:768], w_block(7, x, 0, 384), l_s.at[1]),
        pltpu.make_async_copy(ew_ref, ew.at[x], l_s.at[2]),
        pltpu.make_async_copy(pos_ref, pos.at[y, c], l_s.at[3]),
        pltpu.make_async_copy(
            dp_ref.at[:, pl.ds(aligned(row * 384, 128), 384)], dpw, l_s.at[4]
        ),
        pltpu.make_async_copy(do_ref, dow, l_s.at[5]),
        pltpu.make_async_copy(pw_ref, pxw, l_s.at[6]),
    ]
    for fetch in fetches:
        fetch.start()

    first_row = lax.broadcasted_iota(jnp.int32, (8, 384), 0) == 0
    gains[x] = jnp.where(first_row, ig_ref[...], fg_ref[...])
    raw[x] = x_ref[pl.ds(x * 4, 4)]

    barrier = pltpu.get_barrier_semaphore()
    peers = (
        [x_peer(d) for d in range(1, 4)]
        + [z_peer(d) for d in range(1, 4)]
        + [row_peer(k // 2, k % 2) for k in range(1, 8)]
    )
    for peer in peers:
        pl.semaphore_signal(barrier, inc=1, device_id=peer, device_id_type=MESH)
    pl.semaphore_wait(barrier, len(peers))

    def raw_copy(d):
        there = turn(x, d)
        return remote(x_ref.at[pl.ds(there * 4, 4)], raw.at[x], x_s.at[d], x_r.at[d], x_peer(d))

    def gain_copy(d):
        return remote(gains.at[x], gains.at[x], g_s.at[d], g_r.at[d], x_peer(d))

    for d in (1, 3, 2):
        gain_copy(d).start()
        raw_copy(d).start()

    def w_send(j, way):
        block = w_block(j, x, 0, 384)
        target = device(right if way == 0 else left, y, z, c)
        return remote(block, block, wn_s.at[way, j], wn_r.at[way, j], target)

    def w_got(j, way):
        block = w_block(j, left if way == 0 else right, 0, 384)
        return remote(block, block, wn_s.at[way, j], wn_r.at[way, j], mate)

    def w_forward(j, way):
        block = w_block(j, left if way == 0 else right, 192 * way, 192)
        target = device(right if way == 0 else left, y, z, c)
        return remote(block, block, wf_s.at[way, j], wf_r.at[way, j], target)

    def w_far(j, way):
        block = w_block(j, turn(x, 2), 192 * way, 192)
        return remote(block, block, wf_s.at[way, j], wf_r.at[way, j], mate)

    def w_start(j):
        w_send(j, 0).start()
        w_send(j, 1).start()

    def w_step(j):
        w_got(j, 0).wait_recv()
        w_forward(j, 0).start()
        w_got(j, 1).wait_recv()
        w_forward(j, 1).start()

        @pl.when(j + 2 < CHUNKS)
        def _():
            w_start(j + 2)

    @pl.loop(0, HEADS_OWN)
    def _(j):
        w_fetch(j).wait()

    fetches[0].wait()
    fetches[1].wait()
    w_start(0)
    w_start(1)

    def stat_copy(n, d, owner):
        block = stats.at[n, owner]
        return remote(block, block, st_s.at[n, d], st_r.at[n, d], z_peer(d))

    def share_stats(n, total, square):
        lane = lax.broadcasted_iota(jnp.int32, (128, 128), 1)
        stats[n, z] = jnp.transpose(jnp.where(lane == 0, total, square))[0:8]
        for d in (1, 3, 2):
            stat_copy(n, d, z).start()
        for d in (1, 3, 2):
            stat_copy(n, d, turn(z, 4 - d)).wait_recv()
        sums = jnp.transpose(jnp.sum(stats[n], axis=0))
        average = sums[:, 0:1] / D
        spread = sums[:, 1:2] / D - average * average
        return average, lax.rsqrt(spread + epsilon)

    for d in (1, 3, 2):
        there = turn(x, 4 - d)
        remote(gains.at[there], gains.at[there], g_s.at[d], g_r.at[d], mate).wait_recv()
        remote(raw.at[there], raw.at[there], x_s.at[d], x_r.at[d], mate).wait_recv()
    total, square = 0.0, 0.0
    for g in range(4):
        block = raw[g].reshape(128, 384).astype(f32)
        total = total + jnp.sum(block, axis=-1, keepdims=True)
        square = square + jnp.sum(block * block, axis=-1, keepdims=True)
    average, rate = share_stats(0, total, square)
    for g in range(4):
        block = raw[g].reshape(128, 384).astype(f32)
        block = (block - average) * rate * gains[g, 0:1, :]
        a[y, c, :, 384 * g : 384 * g + 384] = block.astype(bf16)

    def spread_rows(block, s_y, r_y, s_c, r_c):
        for e in (1, 3, 2):
            remote(block, block, s_y.at[e], r_y.at[e], y_peer(e)).start()
        remote(block, block, s_c.at[0], r_c.at[0], mate).start()

    spread_rows(a.at[y, c], ay_s, ay_r, ac_s, ac_r)
    fetches[3].wait()
    spread_rows(pos.at[y, c], p_s, p_r, pc_s, pc_r)
    w_step(0)
    w_step(1)

    def way_of(s):
        return s // 2

    def ahead(way):
        return turn(z, 1 + 2 * way)

    def behind(way):
        return turn(z, 3 - 2 * way)

    def piece(s):
        return pl.ds(aligned(s * 64, 64), 64)

    def hop_copy(j, s):
        way = way_of(s)
        return remote(
            cs.at[j, turn(z, 2), piece(s), :],
            hop.at[j, piece(s), :],
            h_s.at[j, s],
            h_r.at[j, s],
            device(x, y, ahead(way), c),
        )

    def c_copy(j, s, way):
        there = ahead(way)
        return remote(
            cs.at[j, there, piece(s), :],
            cr.at[way, j, piece(s), :],
            c_s.at[way, j],
            c_r.at[way, j],
            device(x, y, there, c),
        )

    def c_all(j, way):
        return remote(
            cs.at[j, ahead(way)], cr.at[way, j], c_s.at[way, j], c_r.at[way, j], mate
        )

    def combine(j, i):
        s = turn(y, 4 - near(i))
        way = way_of(s)
        hop_copy(j, s).wait_recv()
        both = cs[j, ahead(way), piece(s), :].astype(f32) + hop[j, piece(s), :].astype(f32)
        cs[j, ahead(way), piece(s), :] = both.astype(bf16)
        c_copy(j, s, way).start()

    def t_copy(j, d):
        block = att.at[z, :, pl.ds(aligned(j * 128, 128), 128)]
        return remote(block, block, t_s.at[d], t_r.at[d], z_peer(d))

    def attend_head(j):
        c_all(j, 0).wait_recv()
        c_all(j, 1).wait_recv()
        projected = cs[j, z].astype(f32) + cr[0, j].astype(f32) + cr[1, j].astype(f32)
        queries = norm(projected[:, 0:128], qg_ref[...]).astype(bf16)
        keys = norm(projected[:, 128:256], kg_ref[...]).astype(bf16)
        mixed = attention(queries, keys, projected[:, 256:384].astype(bf16), 128 ** (-0.5))
        att[z, :, pl.ds(aligned(j * 128, 128), 128)] = mixed
        for d in (1, 3, 2):
            t_copy(j, d).start()

    def ew_half(owner, half):
        return ew.at[owner, pl.ds(aligned(half * 192, 192), 192), :]

    def ex_copy(d):
        block = ew_half(x, c)
        return remote(block, block, ex_s.at[d], ex_r.at[d], x_peer(d))

    def ex_got(d):
        block = ew_half(turn(x, 4 - d), c)
        return remote(block, block, ex_s.at[d], ex_r.at[d], mate)

    def ec_copy(d):
        block = ew_half(turn(x, 4 - d), c)
        return remote(block, block, ec_s.at[d], ec_r.at[d], mate)

    def ec_got(d):
        block = ew_half(turn(x, 4 - d), 1 - c)
        return remote(block, block, ec_s.at[d], ec_r.at[d], mate)

    first_half = lax.broadcasted_iota(jnp.int32, (256, 128), 1) < 64

    def decoder_heads(tokens):
        normed = norm(tokens, dg_ref[...]).astype(bf16)
        made = jnp.dot(normed, dpw[...], preferred_element_type=f32)
        queries = jnp.concatenate([made[:, 0:64], made[:, 192:256]], axis=1)
        keys = jnp.concatenate([made[:, 64:128], made[:, 256:320]], axis=1)
        values = jnp.concatenate([made[:, 128:192], made[:, 320:384]], axis=1)
        query_gain = jnp.concatenate([dqg_ref[...], dqg_ref[...]], axis=1)
        key_gain = jnp.concatenate([dkg_ref[...], dkg_ref[...]], axis=1)
        queries = pair_norm(queries, query_gain)
        one = jnp.where(first_half, queries, 0.0).astype(bf16)
        two = jnp.where(first_half, 0.0, queries).astype(bf16)
        return one, two, pair_norm(keys, key_gain).astype(bf16), values

    def decoder_mix(queries, keys, values):
        scores = lax.dot_general(queries, keys, LAST, preferred_element_type=f32)
        weights = jnp.exp(scores * 64 ** (-0.5)).astype(bf16)
        return jnp.dot(weights, values, preferred_element_type=f32)

    def block_rows(i):
        return pl.ds(aligned(i * 256, 256), 256)

    def hidden_heads(i):
        rows = block_rows(i)
        positions = lax.broadcasted_iota(jnp.int32, (256, 256), 0) + i * 256
        select = jnp.where(positions == vi_ref[...], 1.0, 0.0)
        sel[rows, :] = select.astype(bf16)
        hidden = 1.0 - jnp.sum(select, axis=1, keepdims=True)
        tokens = hidden * mask_ref[...] + pos[i].reshape(256, DD).astype(f32) + scr[0:1, :]

        @pl.when(i == y)
        def _():
            tok[...] = tokens

        one, two, keys, values = decoder_heads(tokens)
        dq[0, rows, :] = one
        dq[1, rows, :] = two
        dk[rows, :] = keys
        dv[rows, 0:128] = (values * hidden).astype(bf16)
        dv[rows, 128:256] = jnp.broadcast_to(hidden, (256, 128)).astype(bf16)

    def hidden_mix(i):
        rows = block_rows(i)
        for h in range(2):
            base[h, rows, :] = decoder_mix(dq[h, rows, :], dk[...], dv[...])

    def visible_base():
        places = jnp.broadcast_to(vi_ref[...].astype(f32), (8, 256))
        places = jnp.transpose(places)[:, 0:1].astype(jnp.int32)
        positions = lax.broadcasted_iota(jnp.int32, (256, 1024), 1)
        select = jnp.where(positions == places, 1.0, 0.0).astype(bf16)
        chosen = jnp.dot(select, pos[...].reshape(1024, DD), preferred_element_type=f32)
        tokv[...] = chosen + scr[0:1, :]

    ids = lax.broadcasted_iota(jnp.int32, script_ref.shape, 0)
    scripted = jnp.sum(
        jnp.where(ids == si_ref[...], script_ref[...].astype(f32), 0.0), axis=0, keepdims=True
    )
    scr[...] = jnp.broadcast_to(scripted, (8, DD))

    @pl.loop(0, HEADS_OWN)
    def _(j):
        w_far(j, 0).wait_recv()
        w_far(j, 1).wait_recv()

        @pl.loop(0, 4)
        def _(i):
            e = near(i)
            s = turn(y, 4 - e)

            @pl.when(j == 0)
            def _():
                @pl.when(i > 0)
                def _():
                    got = a.at[s, c]
                    remote(got, got, ay_s.at[e], ay_r.at[e], mate).wait_recv()
                    remote(got, got, ac_s.at[e], ac_r.at[e], mate).start()

                other = a.at[s, 1 - c]
                remote(other, other, ac_s.at[e], ac_r.at[e], mate).wait_recv()

            product = jnp.dot(a[s].reshape(256, 1536), w[j], preferred_element_type=f32).astype(bf16)
            for core in range(2):
                for image in range(4):
                    first = core * 128 + image * 32
                    rows = pl.ds(aligned(s * 64 + core * 32, 32), 32)
                    cs[j, image, rows, :] = product[first : first + 32]
            hop_copy(j, s).start()
            c_copy(j, s, 1 - way_of(s)).start()

            @pl.when((j == 0) & (i > 0))
            def _():
                combine(0, i - 1)

        @pl.when(j == 0)
        def _():
            combine(0, 3)

        @pl.when(j == 2)
        def _():
            for e in (1, 3, 2):
                got = pos.at[turn(y, 4 - e), c]
                remote(got, got, p_s.at[e], p_r.at[e], mate).wait_recv()
                remote(got, got, pc_s.at[e], pc_r.at[e], mate).start()

        @pl.when(j > 0)
        def _():
            attend_head(j - 1)

            @pl.loop(0, 4)
            def _(i):
                combine(j, i)

        w_step(j + 2)

        @pl.when(j == 3)
        def _():
            fetches[4].wait()
            for e in range(4):
                got = pos.at[turn(y, 4 - e), 1 - c]
                remote(got, got, pc_s.at[e], pc_r.at[e], mate).wait_recv()

        @pl.when((j == 3) | (j == 4))
        def _():
            @pl.loop(0, 2)
            def _(i):
                hidden_heads((j - 3) * 2 + i)

    fetches[2].wait()
    for d in (1, 3, 2):
        ex_copy(d).start()

    @pl.loop(0, 4)
    def _(i):
        hidden_mix(i)

    visible_base()
    attend_head(HEADS_OWN - 1)
    for d in (1, 3, 2):
        whole = att.at[turn(z, 4 - d)]
        remote(whole, whole, t_s.at[d], t_r.at[d], mate).wait_recv()

    def block_at(i):
        return turn(x, 4 - near(i))

    def mate_copy(i):
        there = block_at(i)
        return remote(po.at[there, 1 - c], pr.at[there], m_s.at[i], m_r.at[i], mate)

    def y_copy(i, e):
        there = block_at(i)
        return remote(
            po.at[there, c, turn(y, e)], yr.at[e - 1, there], y_s.at[e, i], y_r.at[e, i], y_peer(e)
        )

    def reduce_rows(i):
        there = block_at(i)
        mate_copy(i).wait_recv()
        both = po[there, c].astype(f32) + pr[there].astype(f32)
        po[there, c] = both.astype(bf16)
        for e in (1, 3, 2):
            y_copy(i, e).start()

    @pl.loop(0, 4)
    def _(i):
        there = block_at(i)

        @pl.when(i == 3)
        def _():
            for j in (6, 7):
                w_far(j, 0).wait_recv()
                w_far(j, 1).wait_recv()

        rows = pl.ds(aligned(there * 384, 384), 384)
        both = att[...].reshape(1024, 768)
        product = jnp.dot(both[:, 0:384], w[6, rows, :], preferred_element_type=f32)
        product = product + jnp.dot(both[:, 384:768], w[7, rows, :], preferred_element_type=f32)
        product = product.astype(bf16)
        for image in range(4):
            for part in range(8):
                first = image * 256 + part * 32
                po[there, part % 2, part // 2, image * 32 : image * 32 + 32, :] = product[
                    first : first + 32
                ]
        mate_copy(i).start()

        @pl.when(i > 0)
        def _():
            reduce_rows(i - 1)

    reduce_rows(3)

    res[...] = jnp.zeros_like(res)

    def enc_copy(d):
        there = turn(x, d)
        return remote(
            es.at[there], enc_ref.at[pl.ds(x * 4, 4)], en_s.at[d], en_r.at[d], x_peer(d)
        )

    total, square = 0.0, 0.0
    for i in range(4):
        there = block_at(i)
        for e in (1, 3, 2):
            y_copy(i, e).wait_recv()
        block = raw[there].reshape(128, 384).astype(f32) + po[there, c, y].astype(f32)
        for e in range(3):
            block = block + yr[e, there].astype(f32)
        res[there] = block
        es[there] = block.astype(bf16).reshape(4, 32, 384)
        total = total + jnp.sum(block, axis=-1, keepdims=True)
        square = square + jnp.sum(block * block, axis=-1, keepdims=True)
    for d in (1, 3, 2):
        ex_got(d).wait_recv()
        ec_copy(d).start()
    average, rate = share_stats(1, total, square)
    for g in range(4):
        block = (res[g] - average) * rate * gains[g, 1:2, :]
        en[:, 384 * g : 384 * g + 384] = block.astype(bf16)
    for d in (1, 3, 2):
        enc_copy(d).start()
    enc_ref[pl.ds(x * 4, 4)] = es[x]

    for d in (1, 3, 2):
        ec_got(d).wait_recv()
    product = jnp.dot(en[...], ew[...].reshape(1536, DD), preferred_element_type=f32)
    eo[...] = product.astype(bf16).reshape(4, 32, DD)

    def eb_copy(d):
        return remote(eo.at[turn(z, d)], er.at[d - 1], eb_s.at[d], eb_r.at[d], z_peer(d))

    for d in (1, 3, 2):
        eb_copy(d).start()
    embedded = eo[z].astype(f32)
    for d in (1, 3, 2):
        eb_copy(d).wait_recv()
        embedded = embedded + er[d - 1].astype(f32)
    vis[row] = (embedded + eb_ref[...]).astype(bf16)

    def vis_copy(k):
        block = vis.at[row]
        return remote(block, block, v_s.at[k], v_r.at[k], row_peer(k // 2, k % 2))

    for k in (4, 5, 2, 3, 6, 7, 1):
        vis_copy(k).start()

    for k in range(1, 8):
        block = vis.at[row_from(k // 2, k % 2)]
        remote(block, block, v_s.at[k], v_r.at[k], mate).wait_recv()
    one, two, keys, values = decoder_heads(vis[...].reshape(256, DD).astype(f32) + tokv[...])
    vq[0] = one
    vq[1] = two
    vk[...] = keys
    vv[:, 0:128] = values.astype(bf16)
    vv[:, 128:256] = jnp.ones((256, 128), bf16)

    def mix_copy(e, m):
        owner = turn(y, e) * 2 + c + m - 2 * c * m
        block = da.at[:, pl.ds(aligned(row * 128, 128), 128)]
        return remote(dm.at[owner], block, d_s.at[e, m], d_r.at[e, m], row_peer(e, m))

    def mix_got(e, m):
        block = da.at[:, pl.ds(aligned(row_from(e, m) * 128, 128), 128)]
        return remote(block, block, d_s.at[e, m], d_r.at[e, m], mate)

    def finish(both):
        one = both[0][:, 0:128] / both[0][:, 128:256]
        two = both[1][:, 0:128] / both[1][:, 128:256]
        return jnp.where(first_half, one, two).astype(bf16)

    visible = finish(
        [
            decoder_mix(vq[h], dk[...], dv[...]) + decoder_mix(vq[h], vk[...], vv[...])
            for h in range(2)
        ]
    )

    @pl.loop(0, 4)
    def _(i):
        e = near(3 - i)
        there = turn(y, e)
        rows = block_rows(there)
        mixed = finish(
            [base[h, rows, :] + decoder_mix(dq[h, rows, :], vk[...], vv[...]) for h in range(2)]
        )
        placed = jnp.dot(sel[rows, :], visible, preferred_element_type=f32)
        hidden = dv[rows, 128:256].astype(f32) > 0.5
        mixed = jnp.where(hidden, mixed.astype(f32), placed).astype(bf16)
        dm[there * 2] = mixed[0:128]
        dm[there * 2 + 1] = mixed[128:256]

        @pl.when(e > 0)
        def _():
            mix_copy(e, 0).start()

        mix_copy(e, 1).start()

    da[:, pl.ds(aligned(row * 128, 128), 128)] = dm[row]
    fetches[5].wait()
    fetches[6].wait()
    for k in range(1, 8):
        mix_got(k // 2, k % 2).wait_recv()
    tokens = tok[pl.ds(aligned(c * 128, 128), 128), :] + jnp.dot(
        sel[pl.ds(aligned(row * 128, 128), 128), :],
        vis[...].reshape(256, DD),
        preferred_element_type=f32,
    )
    decoded = tokens + jnp.dot(da[...], dow[...], preferred_element_type=f32)
    normed = norm(decoded, hg_ref[...]).astype(bf16)
    predicted = jnp.dot(normed, pxw[...], preferred_element_type=f32) + pb_ref[...]
    pred_ref[0] = predicted.astype(bf16)

    for d in range(1, 4):
        block = enc_ref.at[pl.ds(turn(x, 4 - d) * 4, 4)]
        remote(block, block, en_s.at[d], en_r.at[d], mate).wait_recv()
        enc_copy(d).wait_send()
        gain_copy(d).wait_send()
        raw_copy(d).wait_send()
        stat_copy(0, d, z).wait_send()
        stat_copy(1, d, z).wait_send()
        ex_copy(d).wait_send()
        eb_copy(d).wait_send()
        whole = att.at[z]
        remote(whole, whole, t_s.at[d], t_r.at[d], mate).wait_send()
        ec_copy(d).wait_send()
    for e in range(4):
        for block, s_y, r_y, s_c, r_c in (
            (a, ay_s, ay_r, ac_s, ac_r),
            (pos, p_s, p_r, pc_s, pc_r),
        ):
            if e > 0:
                own = block.at[y, c]
                remote(own, own, s_y.at[e], r_y.at[e], mate).wait_send()
            passed = block.at[turn(y, 4 - e), c]
            remote(passed, passed, s_c.at[e], r_c.at[e], mate).wait_send()
        mate_copy(e).wait_send()
        for i in range(1, 4):
            y_copy(e, i).wait_send()
    for k in range(1, 8):
        vis_copy(k).wait_send()
        mix_copy(k // 2, k % 2).wait_send()

    @pl.loop(0, CHUNKS)
    def _(j):
        for way in range(2):
            w_send(j, way).wait_send()
            w_forward(j, way).wait_send()

    @pl.loop(0, HEADS_OWN)
    def _(j):
        for way in range(2):
            c_all(j, way).wait_send()

        @pl.loop(0, 4)
        def _(s):
            hop_copy(j, s).wait_send()


VMEM = pl.BlockSpec(memory_space=pltpu.VMEM)
ANY = pl.BlockSpec(memory_space=pl.ANY)


def local(
    visible_patches,
    input_gain,
    encoder_project,
    query_gain,
    key_gain,
    output_weight,
    final_gain,
    embed_weight,
    embed_bias,
    mask_token,
    position_embed,
    script_table,
    decoder_gain,
    decoder_project,
    decoder_query,
    decoder_key,
    decoder_output,
    head_gain,
    pixel_weight,
    pixel_bias,
    visible_index,
    script_index,
):
    def flat(vector):
        return vector.reshape(1, -1)

    dma = pltpu.SemaphoreType.DMA
    two = [dma((4,)), dma((4,))]
    return pl.pallas_call(
        kernel,
        out_shape=(
            jax.ShapeDtypeStruct((16, 32, 384), bf16),
            jax.ShapeDtypeStruct((1, 128, 768), bf16),
        ),
        in_specs=[
            VMEM, VMEM, ANY, VMEM, VMEM, ANY, VMEM, ANY, VMEM, VMEM, ANY,
            VMEM, VMEM, ANY, VMEM, VMEM, ANY, VMEM, ANY, VMEM, VMEM, VMEM,
        ],
        out_specs=(VMEM, VMEM),
        scratch_shapes=[
            pltpu.VMEM((4, 8, 384), f32),
            pltpu.VMEM((4, 4, 32, 384), bf16),
            pltpu.VMEM((2, 4, 8, 128), f32),
            pltpu.VMEM((4, 2, 128, 1536), bf16),
            pltpu.VMEM((CHUNKS, 1536, 384), bf16),
            pltpu.VMEM((HEADS_OWN, 4, 256, 384), bf16),
            pltpu.VMEM((2, HEADS_OWN, 256, 384), bf16),
            pltpu.VMEM((HEADS_OWN, 256, 384), bf16),
            pltpu.VMEM((4, 256, 768), bf16),
            pltpu.VMEM((4, 2, 4, 128, 384), bf16),
            pltpu.VMEM((4, 4, 128, 384), bf16),
            pltpu.VMEM((3, 4, 128, 384), bf16),
            pltpu.VMEM((4, 128, 384), f32),
            pltpu.VMEM((128, 1536), bf16),
            pltpu.VMEM((4, 4, 32, 384), bf16),
            pltpu.VMEM((4, 384, DD), bf16),
            pltpu.VMEM((4, 2, 128, DD), bf16),
            pltpu.VMEM((DD, 384), bf16),
            pltpu.VMEM((DD, DD), bf16),
            pltpu.VMEM((DD, 768), bf16),
            pltpu.VMEM((4, 32, DD), bf16),
            pltpu.VMEM((3, 32, DD), bf16),
            pltpu.VMEM((8, 32, DD), bf16),
            pltpu.VMEM((8, DD), f32),
            pltpu.VMEM((1024, 256), bf16),
            pltpu.VMEM((256, DD), f32),
            pltpu.VMEM((256, DD), f32),
            pltpu.VMEM((2, 1024, 128), bf16),
            pltpu.VMEM((1024, 128), bf16),
            pltpu.VMEM((1024, 256), bf16),
            pltpu.VMEM((2, 1024, 256), f32),
            pltpu.VMEM((2, 256, 128), bf16),
            pltpu.VMEM((256, 128), bf16),
            pltpu.VMEM((256, 256), bf16),
            pltpu.VMEM((8, 128, 128), bf16),
            pltpu.VMEM((128, DD), bf16),
            dma((7,)),
            dma((HEADS_OWN,)),
            *two,
            *two,
            dma((2, 4)), dma((2, 4)),
            *two,
            *two,
            dma((2, CHUNKS)), dma((2, CHUNKS)),
            dma((2, CHUNKS)), dma((2, CHUNKS)),
            dma((HEADS_OWN, 4)), dma((HEADS_OWN, 4)),
            dma((2, HEADS_OWN)), dma((2, HEADS_OWN)),
            *two,
            *two,
            *two,
            *two,
            *two,
            *two,
            dma((4, 4)), dma((4, 4)),
            *two,
            *two,
            dma((8,)), dma((8,)),
            dma((4, 2)), dma((4, 2)),
        ],
        compiler_params=pltpu.CompilerParams(
            collective_id=0, has_side_effects=True, vmem_limit_bytes=62 << 20
        ),
        name="masked_patches",
    )(
        visible_patches, flat(input_gain), encoder_project, flat(query_gain), flat(key_gain),
        output_weight, flat(final_gain), embed_weight, flat(embed_bias), flat(mask_token),
        position_embed, script_table, flat(decoder_gain), decoder_project, flat(decoder_query),
        flat(decoder_key), decoder_output, flat(head_gain), pixel_weight, flat(pixel_bias),
        visible_index, flat(script_index),
    )


def solution(mesh):
    return jax.shard_map(
        local,
        mesh=mesh,
        in_specs=(
            P(None, "row", "col"),
            P("col"),
            P("col", "row"),
            P(),
            P(),
            P("row", "col"),
            P("col"),
            P("col", None),
            P(),
            P(),
            P("row", None),
            P(),
            P(),
            P(),
            P(),
            P(),
            P(),
            P(),
            P(),
            P(),
            P("col", None),
            P("col"),
        ),
        out_specs=(P(None, "row", "col"), P("col", "row", None)),
        check_vma=False,
    )
```

```python
import jax
import jax.numpy as jnp
from jax import lax
from jax.experimental import pallas as pl
from jax.experimental.pallas import tpu as pltpu
from jax.sharding import PartitionSpec as P

D = 6144
DD = 1024
HEADS_OWN = 6
MESH = pl.DeviceIdType.MESH
bf16 = jnp.bfloat16
f32 = jnp.float32

epsilon = 1e-06
LAST = (((1,), (1,)), ((), ()))


def turn(i, by):
    return lax.rem(i + by, 4)


def near(i):
    return i + (i // 2) * (5 - 2 * i)


def device(x, y, z, c):
    return (y * 2 + c, x * 4 + z)


def remote(src, dst, send_sem, recv_sem, where):
    return pltpu.make_async_remote_copy(
        src_ref=src,
        dst_ref=dst,
        send_sem=send_sem,
        recv_sem=recv_sem,
        device_id=where,
        device_id_type=MESH,
    )


def aligned(index, multiple):
    return pl.multiple_of(index, multiple)


def norm(values, gain_vector):
    amount = values.shape[-1]
    average = jnp.sum(values, axis=-1, keepdims=True) / amount
    spread = jnp.sum(values * values, axis=-1, keepdims=True) / amount - average * average
    return (values - average) * lax.rsqrt(spread + epsilon) * gain_vector


def pair_norm(values, gain_vector):
    first = lax.broadcasted_iota(jnp.int32, values.shape, 1) < 64

    def mean(v):
        one = jnp.sum(jnp.where(first, v, 0.0), axis=-1, keepdims=True)
        two = jnp.sum(jnp.where(first, 0.0, v), axis=-1, keepdims=True)
        return jnp.where(first, one, two) / 64

    average = mean(values)
    spread = mean(values * values) - average * average
    return (values - average) * lax.rsqrt(spread + epsilon) * gain_vector


def attention(queries, keys, values, factor):
    scores = lax.dot_general(queries, keys, LAST, preferred_element_type=f32) * factor
    weights = jnp.exp(scores).astype(bf16)
    totals = jnp.sum(weights.astype(f32), axis=-1, keepdims=True)
    mixture = jnp.dot(weights, values, preferred_element_type=f32)
    return (mixture / totals).astype(bf16)


def kernel(
    x_ref, ig_ref, w_ref, qg_ref, kg_ref, wo_ref, fg_ref, ew_ref, eb_ref, mask_ref, pos_ref,
    script_ref, dg_ref, dp_ref, dqg_ref, dkg_ref, do_ref, hg_ref, pw_ref, pb_ref, vi_ref, si_ref,
    enc_ref, pred_ref,
    gains, fgains, raw, own, stats, a, w, wo, cs, cr, hop, att, po, pr, yr, res, en, es, ew, pos, dpw, dow, pxw,
    eo, er, vis, scr, sel, tok, tokv, dq, dk, dv, base, vq, vk, vv, dm, da,
    l_s, w_s, g_s, g_r, f_s, f_r, x_s, x_r, o_s, o_r, wo_s, wo_r, st_s, st_r, ay_s, ay_r, ac_s, ac_r, wn_s, wn_r, wf_s, wf_r,
    h_s, h_r, c_s, c_r, t_s, t_r, p_s, p_r, pc_s, pc_r, ex_s, ex_r, ec_s, ec_r,
    m_s, m_r, y_s, y_r, en_s, en_r, eb_s, eb_r, v_s, v_r, d_s, d_r,
):
    row, col = lax.axis_index("row"), lax.axis_index("col")
    x, y, z, c = col // 4, row // 2, lax.rem(col, 4), lax.rem(row, 2)
    mate = device(x, y, z, 1 - c)
    right, left = turn(x, 1), turn(x, 3)

    def x_peer(d):
        return device(turn(x, d), y, z, c)

    def y_peer(d):
        return device(x, turn(y, d), z, c)

    def z_peer(d):
        return device(x, y, turn(z, d), c)

    def row_peer(e, m):
        return device(x, turn(y, e), z, c + m - 2 * c * m)

    def row_from(e, m):
        return turn(y, 4 - e) * 2 + c + m - 2 * c * m

    def w_block(j, owner, start, size):
        return w.at[j, pl.ds(aligned(owner * 384 + start, 192), size), :]

    def w_fetch(j):
        return pltpu.make_async_copy(
            w_ref.at[:, pl.ds(aligned(j * 384, 128), 384)], w_block(j, x, 0, 384), w_s.at[j]
        )

    @pl.loop(0, HEADS_OWN)
    def _(j):
        w_fetch(j).start()

    fetches = [
        pltpu.make_async_copy(wo_ref, wo.at[z], l_s.at[0]),
        pltpu.make_async_copy(ew_ref, ew.at[z], l_s.at[1]),
        pltpu.make_async_copy(pos_ref, pos.at[y, c], l_s.at[2]),
        pltpu.make_async_copy(
            dp_ref.at[:, pl.ds(aligned(row * 384, 128), 384)], dpw, l_s.at[3]
        ),
        pltpu.make_async_copy(do_ref, dow, l_s.at[4]),
        pltpu.make_async_copy(pw_ref, pxw, l_s.at[5]),
    ]

    gains[x] = jnp.broadcast_to(ig_ref[...], (8, 384))
    fgains[z] = jnp.broadcast_to(fg_ref[...], (8, 384))

    barrier = pltpu.get_barrier_semaphore()
    peers = (
        [x_peer(d) for d in range(1, 4)]
        + [z_peer(d) for d in range(1, 4)]
        + [row_peer(k // 2, k % 2) for k in range(1, 8)]
    )
    for peer in peers:
        pl.semaphore_signal(barrier, inc=1, device_id=peer, device_id_type=MESH)
    pl.semaphore_wait(barrier, len(peers))

    def raw_copy(d):
        return remote(x_ref.at[turn(x, d)], raw.at[x], x_s.at[d], x_r.at[d], x_peer(d))

    def gain_copy(d):
        return remote(gains.at[x], gains.at[x], g_s.at[d], g_r.at[d], x_peer(d))

    def own_copy(d):
        return remote(x_ref.at[:, turn(z, d)], own.at[z], o_s.at[d], o_r.at[d], z_peer(d))

    def fgain_copy(d):
        return remote(fgains.at[z], fgains.at[z], f_s.at[d], f_r.at[d], z_peer(d))

    def wo_copy(d):
        return remote(wo.at[z], wo.at[z], wo_s.at[d], wo_r.at[d], z_peer(d))

    for d in (1, 3, 2):
        gain_copy(d).start()
        raw_copy(d).start()
    for fetch in fetches:
        fetch.start()
    raw[x] = x_ref[x]
    own[z] = x_ref[:, z]

    def w_send(j, way):
        block = w_block(j, x, 0, 384)
        target = device(right if way == 0 else left, y, z, c)
        return remote(block, block, wn_s.at[way, j], wn_r.at[way, j], target)

    def w_got(j, way):
        block = w_block(j, left if way == 0 else right, 0, 384)
        return remote(block, block, wn_s.at[way, j], wn_r.at[way, j], mate)

    def w_forward(j, way):
        block = w_block(j, left if way == 0 else right, 192 * way, 192)
        target = device(right if way == 0 else left, y, z, c)
        return remote(block, block, wf_s.at[way, j], wf_r.at[way, j], target)

    def w_far(j, way):
        block = w_block(j, turn(x, 2), 192 * way, 192)
        return remote(block, block, wf_s.at[way, j], wf_r.at[way, j], mate)

    def w_start(j):
        w_fetch(j).wait()
        w_send(j, 0).start()
        w_send(j, 1).start()

    def w_step(j):
        w_got(j, 0).wait_recv()
        w_forward(j, 0).start()
        w_got(j, 1).wait_recv()
        w_forward(j, 1).start()

        @pl.when(j + 2 < HEADS_OWN)
        def _():
            w_start(j + 2)

    w_start(0)
    w_start(1)

    def stat_copy(n, d, owner):
        block = stats.at[n, owner]
        peer = z_peer(d) if n == 0 else x_peer(d)
        return remote(block, block, st_s.at[n, d], st_r.at[n, d], peer)

    def share_stats(n, total, square):
        lane = lax.broadcasted_iota(jnp.int32, (128, 128), 1)
        me = z if n == 0 else x
        stats[n, me] = jnp.transpose(jnp.where(lane == 0, total, square))[0:8]
        for d in (1, 3, 2):
            stat_copy(n, d, me).start()
        for d in (1, 3, 2):
            stat_copy(n, d, turn(me, 4 - d)).wait_recv()
        sums = jnp.transpose(jnp.sum(stats[n], axis=0))
        average = sums[:, 0:1] / D
        spread = sums[:, 1:2] / D - average * average
        return average, lax.rsqrt(spread + epsilon)

    for d in (1, 3, 2):
        there = turn(x, 4 - d)
        remote(gains.at[there], gains.at[there], g_s.at[d], g_r.at[d], mate).wait_recv()
        remote(raw.at[there], raw.at[there], x_s.at[d], x_r.at[d], mate).wait_recv()
    total, square = 0.0, 0.0
    for g in range(4):
        block = raw[g].reshape(128, 384).astype(f32)
        total = total + jnp.sum(block, axis=-1, keepdims=True)
        square = square + jnp.sum(block * block, axis=-1, keepdims=True)
    average, rate = share_stats(0, total, square)
    for g in range(4):
        block = raw[g].reshape(128, 384).astype(f32)
        block = (block - average) * rate * gains[g, 0:1, :]
        a[y, c, :, 384 * g : 384 * g + 384] = block.astype(bf16)

    def spread_rows(block, s_y, r_y, s_c, r_c):
        for e in (1, 3, 2):
            remote(block, block, s_y.at[e], r_y.at[e], y_peer(e)).start()
        remote(block, block, s_c.at[0], r_c.at[0], mate).start()

    spread_rows(a.at[y, c], ay_s, ay_r, ac_s, ac_r)
    fetches[2].wait()
    spread_rows(pos.at[y, c], p_s, p_r, pc_s, pc_r)
    fetches[0].wait()
    for d in (1, 3, 2):
        fgain_copy(d).start()
        own_copy(d).start()
        wo_copy(d).start()
    w_step(0)
    w_step(1)

    def way_of(s):
        return s // 2

    def ahead(way):
        return turn(z, 1 + 2 * way)

    def behind(way):
        return turn(z, 3 - 2 * way)

    def piece(s):
        return pl.ds(aligned(s * 64, 64), 64)

    def hop_copy(j, s):
        way = way_of(s)
        return remote(
            cs.at[j, turn(z, 2), piece(s), :],
            hop.at[j, piece(s), :],
            h_s.at[j, s],
            h_r.at[j, s],
            device(x, y, ahead(way), c),
        )

    def c_copy(j, s, way):
        there = ahead(way)
        return remote(
            cs.at[j, there, piece(s), :],
            cr.at[way, j, piece(s), :],
            c_s.at[way, j],
            c_r.at[way, j],
            device(x, y, there, c),
        )

    def c_all(j, way):
        return remote(
            cs.at[j, ahead(way)], cr.at[way, j], c_s.at[way, j], c_r.at[way, j], mate
        )

    def combine(j, i):
        s = turn(y, 4 - near(i))
        way = way_of(s)
        hop_copy(j, s).wait_recv()
        both = cs[j, ahead(way), piece(s), :].astype(f32) + hop[j, piece(s), :].astype(f32)
        cs[j, ahead(way), piece(s), :] = both.astype(bf16)
        c_copy(j, s, way).start()

    def att_send(j, heads):
        block = att.at[x, :, pl.ds(aligned(j * 128, 128), heads * 128)]
        for d in (1, 3, 2):
            remote(block, block, t_s.at[d], t_r.at[d], x_peer(d)).start()

    def attend_head(j):
        c_all(j, 0).wait_recv()
        c_all(j, 1).wait_recv()
        projected = cs[j, z].astype(f32) + cr[0, j].astype(f32) + cr[1, j].astype(f32)
        queries = norm(projected[:, 0:128], qg_ref[...]).astype(bf16)
        keys = norm(projected[:, 128:256], kg_ref[...]).astype(bf16)
        mixed = attention(queries, keys, projected[:, 256:384].astype(bf16), 128 ** (-0.5))
        att[x, :, pl.ds(aligned(j * 128, 128), 128)] = mixed

    def ew_half(owner, half):
        return ew.at[owner, pl.ds(aligned(half * 192, 192), 192), :]

    def ex_copy(d):
        block = ew_half(z, c)
        return remote(block, block, ex_s.at[d], ex_r.at[d], z_peer(d))

    def ex_got(d):
        block = ew_half(turn(z, 4 - d), c)
        return remote(block, block, ex_s.at[d], ex_r.at[d], mate)

    def ec_copy(d):
        block = ew_half(turn(z, 4 - d), c)
        return remote(block, block, ec_s.at[d], ec_r.at[d], mate)

    def ec_got(d):
        block = ew_half(turn(z, 4 - d), 1 - c)
        return remote(block, block, ec_s.at[d], ec_r.at[d], mate)

    first_half = lax.broadcasted_iota(jnp.int32, (256, 128), 1) < 64

    def decoder_heads(tokens):
        normed = norm(tokens, dg_ref[...]).astype(bf16)
        made = jnp.dot(normed, dpw[...], preferred_element_type=f32)
        queries = jnp.concatenate([made[:, 0:64], made[:, 192:256]], axis=1)
        keys = jnp.concatenate([made[:, 64:128], made[:, 256:320]], axis=1)
        values = jnp.concatenate([made[:, 128:192], made[:, 320:384]], axis=1)
        query_gain = jnp.concatenate([dqg_ref[...], dqg_ref[...]], axis=1)
        key_gain = jnp.concatenate([dkg_ref[...], dkg_ref[...]], axis=1)
        queries = pair_norm(queries, query_gain)
        one = jnp.where(first_half, queries, 0.0).astype(bf16)
        two = jnp.where(first_half, 0.0, queries).astype(bf16)
        return one, two, pair_norm(keys, key_gain).astype(bf16), values

    def decoder_mix(queries, keys, values):
        scores = lax.dot_general(queries, keys, LAST, preferred_element_type=f32)
        weights = jnp.exp(scores * 64 ** (-0.5)).astype(bf16)
        return jnp.dot(weights, values, preferred_element_type=f32)

    def block_rows(i):
        return pl.ds(aligned(i * 256, 256), 256)

    def hidden_heads(i):
        rows = block_rows(i)
        positions = lax.broadcasted_iota(jnp.int32, (256, 256), 0) + i * 256
        select = jnp.where(positions == vi_ref[...], 1.0, 0.0)
        sel[rows, :] = select.astype(bf16)
        hidden = 1.0 - jnp.sum(select, axis=1, keepdims=True)
        tokens = hidden * mask_ref[...] + pos[i].reshape(256, DD).astype(f32) + scr[0:1, :]

        @pl.when(i == y)
        def _():
            tok[...] = tokens

        one, two, keys, values = decoder_heads(tokens)
        dq[0, rows, :] = one
        dq[1, rows, :] = two
        dk[rows, :] = keys
        dv[rows, 0:128] = (values * hidden).astype(bf16)
        dv[rows, 128:256] = jnp.broadcast_to(hidden, (256, 128)).astype(bf16)

    def hidden_mix(i):
        rows = block_rows(i)
        for h in range(2):
            base[h, rows, :] = decoder_mix(dq[h, rows, :], dk[...], dv[...])

    def visible_base():
        places = jnp.broadcast_to(vi_ref[...].astype(f32), (8, 256))
        places = jnp.transpose(places)[:, 0:1].astype(jnp.int32)
        positions = lax.broadcasted_iota(jnp.int32, (256, 1024), 1)
        select = jnp.where(positions == places, 1.0, 0.0).astype(bf16)
        chosen = jnp.dot(select, pos[...].reshape(1024, DD), preferred_element_type=f32)
        tokv[...] = chosen + scr[0:1, :]

    ids = lax.broadcasted_iota(jnp.int32, script_ref.shape, 0)
    scripted = jnp.sum(
        jnp.where(ids == si_ref[...], script_ref[...].astype(f32), 0.0), axis=0, keepdims=True
    )
    scr[...] = jnp.broadcast_to(scripted, (8, DD))

    @pl.loop(0, HEADS_OWN)
    def _(j):
        w_far(j, 0).wait_recv()
        w_far(j, 1).wait_recv()

        @pl.loop(0, 4)
        def _(i):
            e = near(i)
            s = turn(y, 4 - e)

            @pl.when(j == 0)
            def _():
                @pl.when(i > 0)
                def _():
                    got = a.at[s, c]
                    remote(got, got, ay_s.at[e], ay_r.at[e], mate).wait_recv()
                    remote(got, got, ac_s.at[e], ac_r.at[e], mate).start()

                other = a.at[s, 1 - c]
                remote(other, other, ac_s.at[e], ac_r.at[e], mate).wait_recv()

            product = jnp.dot(a[s].reshape(256, 1536), w[j], preferred_element_type=f32).astype(bf16)
            for core in range(2):
                for image in range(4):
                    first = core * 128 + image * 32
                    rows = pl.ds(aligned(s * 64 + core * 32, 32), 32)
                    cs[j, image, rows, :] = product[first : first + 32]
            hop_copy(j, s).start()
            c_copy(j, s, 1 - way_of(s)).start()

            @pl.when((j == 0) & (i > 0))
            def _():
                combine(0, i - 1)

        @pl.when(j == 0)
        def _():
            combine(0, 3)

        @pl.when(j == 2)
        def _():
            for e in (1, 3, 2):
                got = pos.at[turn(y, 4 - e), c]
                remote(got, got, p_s.at[e], p_r.at[e], mate).wait_recv()
                remote(got, got, pc_s.at[e], pc_r.at[e], mate).start()

        @pl.when(j > 0)
        def _():
            attend_head(j - 1)

            @pl.loop(0, 4)
            def _(i):
                combine(j, i)

        @pl.when(j + 2 < HEADS_OWN)
        def _():
            w_step(j + 2)

        @pl.when(j == 3)
        def _():
            att_send(0, 3)

        @pl.when(j > 3)
        def _():
            att_send(j - 1, 1)

        @pl.when(j == 3)
        def _():
            fetches[3].wait()
            for e in range(4):
                got = pos.at[turn(y, 4 - e), 1 - c]
                remote(got, got, pc_s.at[e], pc_r.at[e], mate).wait_recv()

        @pl.when((j == 3) | (j == 4))
        def _():
            @pl.loop(0, 2)
            def _(i):
                hidden_heads((j - 3) * 2 + i)

    fetches[1].wait()
    for d in (1, 3, 2):
        ex_copy(d).start()

    @pl.loop(0, 4)
    def _(i):
        hidden_mix(i)

    visible_base()
    attend_head(HEADS_OWN - 1)
    att_send(HEADS_OWN - 1, 1)
    for d in (1, 3, 2):
        there = turn(z, 4 - d)
        remote(fgains.at[there], fgains.at[there], f_s.at[d], f_r.at[d], mate).wait_recv()
        remote(own.at[there], own.at[there], o_s.at[d], o_r.at[d], mate).wait_recv()
        remote(wo.at[there], wo.at[there], wo_s.at[d], wo_r.at[d], mate).wait_recv()
    for d in (1, 3, 2):
        whole = att.at[turn(x, 4 - d)]
        remote(whole, whole, t_s.at[d], t_r.at[d], mate).wait_recv()

    def block_at(i):
        return turn(z, 4 - near(i))

    def mate_copy(i):
        there = block_at(i)
        return remote(po.at[there, 1 - c], pr.at[there], m_s.at[i], m_r.at[i], mate)

    def y_copy(i, e):
        there = block_at(i)
        return remote(
            po.at[there, c, turn(y, e)], yr.at[e - 1, there], y_s.at[e, i], y_r.at[e, i], y_peer(e)
        )

    def reduce_rows(i):
        there = block_at(i)
        mate_copy(i).wait_recv()
        both = po[there, c].astype(f32) + pr[there].astype(f32)
        po[there, c] = both.astype(bf16)
        for e in (1, 3, 2):
            y_copy(i, e).start()

    @pl.loop(0, 4)
    def _(i):
        there = block_at(i)

        product = jnp.dot(
            att[...].reshape(1024, 768), wo[there], preferred_element_type=f32
        )
        product = product.astype(bf16)
        for image in range(4):
            for part in range(8):
                first = image * 256 + part * 32
                po[there, part % 2, part // 2, image * 32 : image * 32 + 32, :] = product[
                    first : first + 32
                ]
        mate_copy(i).start()

        @pl.when(i > 0)
        def _():
            reduce_rows(i - 1)

    reduce_rows(3)

    def enc_copy(d):
        return remote(es.at[turn(z, d)], enc_ref.at[:, z], en_s.at[d], en_r.at[d], z_peer(d))

    total, square = 0.0, 0.0
    for i in range(4):
        there = block_at(i)
        for e in (1, 3, 2):
            y_copy(i, e).wait_recv()
        block = own[there].reshape(128, 384).astype(f32) + po[there, c, y].astype(f32)
        for e in range(3):
            block = block + yr[e, there].astype(f32)
        res[there] = block
        es[there] = block.astype(bf16).reshape(4, 32, 384)
        total = total + jnp.sum(block, axis=-1, keepdims=True)
        square = square + jnp.sum(block * block, axis=-1, keepdims=True)
    for d in (1, 3, 2):
        ex_got(d).wait_recv()
        ec_copy(d).start()
    average, rate = share_stats(1, total, square)
    for g in range(4):
        block = (res[g] - average) * rate * fgains[g, 0:1, :]
        en[:, 384 * g : 384 * g + 384] = block.astype(bf16)
    for d in (1, 3, 2):
        enc_copy(d).start()
    enc_ref[:, z] = es[z]

    for d in (1, 3, 2):
        ec_got(d).wait_recv()
    product = jnp.dot(en[...], ew[...].reshape(1536, DD), preferred_element_type=f32)
    eo[...] = product.astype(bf16).reshape(4, 32, DD)

    def eb_copy(d):
        return remote(eo.at[turn(x, d)], er.at[d - 1], eb_s.at[d], eb_r.at[d], x_peer(d))

    for d in (1, 3, 2):
        eb_copy(d).start()
    embedded = eo[x].astype(f32)
    for d in (1, 3, 2):
        eb_copy(d).wait_recv()
        embedded = embedded + er[d - 1].astype(f32)
    vis[row] = (embedded + eb_ref[...]).astype(bf16)

    def vis_copy(k):
        block = vis.at[row]
        return remote(block, block, v_s.at[k], v_r.at[k], row_peer(k // 2, k % 2))

    for k in (4, 5, 2, 3, 6, 7, 1):
        vis_copy(k).start()

    for k in range(1, 8):
        block = vis.at[row_from(k // 2, k % 2)]
        remote(block, block, v_s.at[k], v_r.at[k], mate).wait_recv()
    one, two, keys, values = decoder_heads(vis[...].reshape(256, DD).astype(f32) + tokv[...])
    vq[0] = one
    vq[1] = two
    vk[...] = keys
    vv[:, 0:128] = values.astype(bf16)
    vv[:, 128:256] = jnp.ones((256, 128), bf16)

    def mix_copy(e, m):
        owner = turn(y, e) * 2 + c + m - 2 * c * m
        block = da.at[:, pl.ds(aligned(row * 128, 128), 128)]
        return remote(dm.at[owner], block, d_s.at[e, m], d_r.at[e, m], row_peer(e, m))

    def mix_got(e, m):
        block = da.at[:, pl.ds(aligned(row_from(e, m) * 128, 128), 128)]
        return remote(block, block, d_s.at[e, m], d_r.at[e, m], mate)

    def finish(both):
        one = both[0][:, 0:128] / both[0][:, 128:256]
        two = both[1][:, 0:128] / both[1][:, 128:256]
        return jnp.where(first_half, one, two).astype(bf16)

    visible = finish(
        [
            decoder_mix(vq[h], dk[...], dv[...]) + decoder_mix(vq[h], vk[...], vv[...])
            for h in range(2)
        ]
    )

    @pl.loop(0, 4)
    def _(i):
        e = near(3 - i)
        there = turn(y, e)
        rows = block_rows(there)
        mixed = finish(
            [base[h, rows, :] + decoder_mix(dq[h, rows, :], vk[...], vv[...]) for h in range(2)]
        )
        placed = jnp.dot(sel[rows, :], visible, preferred_element_type=f32)
        hidden = dv[rows, 128:256].astype(f32) > 0.5
        mixed = jnp.where(hidden, mixed.astype(f32), placed).astype(bf16)
        dm[there * 2] = mixed[0:128]
        dm[there * 2 + 1] = mixed[128:256]

        @pl.when(e > 0)
        def _():
            mix_copy(e, 0).start()

        mix_copy(e, 1).start()

    da[:, pl.ds(aligned(row * 128, 128), 128)] = dm[row]
    fetches[4].wait()
    fetches[5].wait()
    for k in range(1, 8):
        mix_got(k // 2, k % 2).wait_recv()
    tokens = tok[pl.ds(aligned(c * 128, 128), 128), :] + jnp.dot(
        sel[pl.ds(aligned(row * 128, 128), 128), :],
        vis[...].reshape(256, DD),
        preferred_element_type=f32,
    )
    decoded = tokens + jnp.dot(da[...], dow[...], preferred_element_type=f32)
    normed = norm(decoded, hg_ref[...]).astype(bf16)
    predicted = jnp.dot(normed, pxw[...], preferred_element_type=f32) + pb_ref[...]
    pred_ref[0] = predicted.astype(bf16)

    for d in range(1, 4):
        block = enc_ref.at[:, turn(z, 4 - d)]
        remote(block, block, en_s.at[d], en_r.at[d], mate).wait_recv()
        enc_copy(d).wait_send()
        gain_copy(d).wait_send()
        raw_copy(d).wait_send()
        own_copy(d).wait_send()
        fgain_copy(d).wait_send()
        wo_copy(d).wait_send()
        stat_copy(0, d, z).wait_send()
        stat_copy(1, d, x).wait_send()
        ex_copy(d).wait_send()
        eb_copy(d).wait_send()
        whole = att.at[x]
        remote(whole, whole, t_s.at[d], t_r.at[d], mate).wait_send()
        ec_copy(d).wait_send()
    for e in range(4):
        for block, s_y, r_y, s_c, r_c in (
            (a, ay_s, ay_r, ac_s, ac_r),
            (pos, p_s, p_r, pc_s, pc_r),
        ):
            if e > 0:
                own = block.at[y, c]
                remote(own, own, s_y.at[e], r_y.at[e], mate).wait_send()
            passed = block.at[turn(y, 4 - e), c]
            remote(passed, passed, s_c.at[e], r_c.at[e], mate).wait_send()
        mate_copy(e).wait_send()
        for i in range(1, 4):
            y_copy(e, i).wait_send()
    for k in range(1, 8):
        vis_copy(k).wait_send()
        mix_copy(k // 2, k % 2).wait_send()

    @pl.loop(0, HEADS_OWN)
    def _(j):
        for way in range(2):
            w_send(j, way).wait_send()
            w_forward(j, way).wait_send()

    @pl.loop(0, HEADS_OWN)
    def _(j):
        for way in range(2):
            c_all(j, way).wait_send()

        @pl.loop(0, 4)
        def _(s):
            hop_copy(j, s).wait_send()


VMEM = pl.BlockSpec(memory_space=pltpu.VMEM)
ANY = pl.BlockSpec(memory_space=pl.ANY)


def local(
    visible_patches,
    input_gain,
    encoder_project,
    query_gain,
    key_gain,
    output_weight,
    final_gain,
    embed_weight,
    embed_bias,
    mask_token,
    position_embed,
    script_table,
    decoder_gain,
    decoder_project,
    decoder_query,
    decoder_key,
    decoder_output,
    head_gain,
    pixel_weight,
    pixel_bias,
    visible_index,
    script_index,
):
    def flat(vector):
        return vector.reshape(1, -1)

    dma = pltpu.SemaphoreType.DMA
    two = [dma((4,)), dma((4,))]
    encoded, predicted = pl.pallas_call(
        kernel,
        out_shape=(
            jax.ShapeDtypeStruct((4, 4, 32, 384), bf16),
            jax.ShapeDtypeStruct((1, 128, 768), bf16),
        ),
        in_specs=[
            VMEM, VMEM, ANY, VMEM, VMEM, ANY, VMEM, ANY, VMEM, VMEM, ANY,
            VMEM, VMEM, ANY, VMEM, VMEM, ANY, VMEM, ANY, VMEM, VMEM, VMEM,
        ],
        out_specs=(VMEM, VMEM),
        scratch_shapes=[
            pltpu.VMEM((4, 8, 384), f32),
            pltpu.VMEM((4, 8, 384), f32),
            pltpu.VMEM((4, 4, 32, 384), bf16),
            pltpu.VMEM((4, 4, 32, 384), bf16),
            pltpu.VMEM((2, 4, 8, 128), f32),
            pltpu.VMEM((4, 2, 128, 1536), bf16),
            pltpu.VMEM((HEADS_OWN, 1536, 384), bf16),
            pltpu.VMEM((4, 768, 384), bf16),
            pltpu.VMEM((HEADS_OWN, 4, 256, 384), bf16),
            pltpu.VMEM((2, HEADS_OWN, 256, 384), bf16),
            pltpu.VMEM((HEADS_OWN, 256, 384), bf16),
            pltpu.VMEM((4, 256, 768), bf16),
            pltpu.VMEM((4, 2, 4, 128, 384), bf16),
            pltpu.VMEM((4, 4, 128, 384), bf16),
            pltpu.VMEM((3, 4, 128, 384), bf16),
            pltpu.VMEM((4, 128, 384), f32),
            pltpu.VMEM((128, 1536), bf16),
            pltpu.VMEM((4, 4, 32, 384), bf16),
            pltpu.VMEM((4, 384, DD), bf16),
            pltpu.VMEM((4, 2, 128, DD), bf16),
            pltpu.VMEM((DD, 384), bf16),
            pltpu.VMEM((DD, DD), bf16),
            pltpu.VMEM((DD, 768), bf16),
            pltpu.VMEM((4, 32, DD), bf16),
            pltpu.VMEM((3, 32, DD), bf16),
            pltpu.VMEM((8, 32, DD), bf16),
            pltpu.VMEM((8, DD), f32),
            pltpu.VMEM((1024, 256), bf16),
            pltpu.VMEM((256, DD), f32),
            pltpu.VMEM((256, DD), f32),
            pltpu.VMEM((2, 1024, 128), bf16),
            pltpu.VMEM((1024, 128), bf16),
            pltpu.VMEM((1024, 256), bf16),
            pltpu.VMEM((2, 1024, 256), f32),
            pltpu.VMEM((2, 256, 128), bf16),
            pltpu.VMEM((256, 128), bf16),
            pltpu.VMEM((256, 256), bf16),
            pltpu.VMEM((8, 128, 128), bf16),
            pltpu.VMEM((128, DD), bf16),
            dma((6,)),
            dma((HEADS_OWN,)),
            *two,
            *two,
            *two,
            *two,
            *two,
            dma((2, 4)), dma((2, 4)),
            *two,
            *two,
            dma((2, HEADS_OWN)), dma((2, HEADS_OWN)),
            dma((2, HEADS_OWN)), dma((2, HEADS_OWN)),
            dma((HEADS_OWN, 4)), dma((HEADS_OWN, 4)),
            dma((2, HEADS_OWN)), dma((2, HEADS_OWN)),
            *two,
            *two,
            *two,
            *two,
            *two,
            *two,
            dma((4, 4)), dma((4, 4)),
            *two,
            *two,
            dma((8,)), dma((8,)),
            dma((4, 2)), dma((4, 2)),
        ],
        compiler_params=pltpu.CompilerParams(
            collective_id=0, has_side_effects=True, vmem_limit_bytes=62 << 20
        ),
        name="masked_patches",
    )(
        visible_patches.reshape(4, 4, 32, 384), flat(input_gain), encoder_project, flat(query_gain), flat(key_gain),
        output_weight, flat(final_gain), embed_weight, flat(embed_bias), flat(mask_token),
        position_embed, script_table, flat(decoder_gain), decoder_project, flat(decoder_query),
        flat(decoder_key), decoder_output, flat(head_gain), pixel_weight, flat(pixel_bias),
        visible_index, flat(script_index),
    )
    return encoded.reshape(16, 32, 384), predicted


def solution(mesh):
    return jax.shard_map(
        local,
        mesh=mesh,
        in_specs=(
            P(None, "row", "col"),
            P("col"),
            P("col", "row"),
            P(),
            P(),
            P("row", "col"),
            P("col"),
            P("col", None),
            P(),
            P(),
            P("row", None),
            P(),
            P(),
            P(),
            P(),
            P(),
            P(),
            P(),
            P(),
            P(),
            P("col", None),
            P("col"),
        ),
        out_specs=(P(None, "row", "col"), P("col", "row", None)),
        check_vma=False,
    )
```

```python
import jax
import jax.numpy as jnp
from jax import lax
from jax.experimental import pallas as pl
from jax.experimental.pallas import tpu as pltpu
from jax.sharding import PartitionSpec as P

D = 6144
DD = 1024
HEADS_OWN = 6
MESH = pl.DeviceIdType.MESH
bf16 = jnp.bfloat16
f32 = jnp.float32

epsilon = 1e-06
LAST = (((1,), (1,)), ((), ()))


def turn(i, by):
    return lax.rem(i + by, 4)


def near(i):
    return i + (i // 2) * (5 - 2 * i)


def device(x, y, z, c):
    return (y * 2 + c, x * 4 + z)


def remote(src, dst, send_sem, recv_sem, where):
    return pltpu.make_async_remote_copy(
        src_ref=src,
        dst_ref=dst,
        send_sem=send_sem,
        recv_sem=recv_sem,
        device_id=where,
        device_id_type=MESH,
    )


def aligned(index, multiple):
    return pl.multiple_of(index, multiple)


def norm(values, gain_vector):
    amount = values.shape[-1]
    average = jnp.sum(values, axis=-1, keepdims=True) / amount
    spread = jnp.sum(values * values, axis=-1, keepdims=True) / amount - average * average
    return (values - average) * lax.rsqrt(spread + epsilon) * gain_vector


def pair_norm(values, gain_vector):
    first = lax.broadcasted_iota(jnp.int32, values.shape, 1) < 64

    def mean(v):
        one = jnp.sum(jnp.where(first, v, 0.0), axis=-1, keepdims=True)
        two = jnp.sum(jnp.where(first, 0.0, v), axis=-1, keepdims=True)
        return jnp.where(first, one, two) / 64

    average = mean(values)
    spread = mean(values * values) - average * average
    return (values - average) * lax.rsqrt(spread + epsilon) * gain_vector


def attention(queries, keys, values, factor):
    scores = lax.dot_general(queries, keys, LAST, preferred_element_type=f32) * factor
    weights = jnp.exp(scores).astype(bf16)
    totals = jnp.sum(weights.astype(f32), axis=-1, keepdims=True)
    mixture = jnp.dot(weights, values, preferred_element_type=f32)
    return (mixture / totals).astype(bf16)


def kernel(
    x_ref, ig_ref, w_ref, qg_ref, kg_ref, wo_ref, fg_ref, ew_ref, eb_ref, mask_ref, pos_ref,
    script_ref, dg_ref, dp_ref, dqg_ref, dkg_ref, do_ref, hg_ref, pw_ref, pb_ref, vi_ref, si_ref,
    enc_ref, pred_ref,
    gains, fgains, raw, own, stats, a, w, wo, cs, cr, hop, att, po, pr, yr, res, en, es, ew, pos, dpw, dow, pxw,
    eo, er, vis, scr, sel, tok, tokv, dq, dk, dv, base, vq, vk, vv, dm, da,
    l_s, w_s, g_s, g_r, f_s, f_r, x_s, x_r, o_s, o_r, wo_s, wo_r, st_s, st_r, ay_s, ay_r, ac_s, ac_r, wn_s, wn_r, wf_s, wf_r,
    h_s, h_r, c_s, c_r, t_s, t_r, p_s, p_r, pc_s, pc_r, ex_s, ex_r, ec_s, ec_r,
    m_s, m_r, y_s, y_r, en_s, en_r, eb_s, eb_r, v_s, v_r, d_s, d_r,
):
    row, col = lax.axis_index("row"), lax.axis_index("col")
    x, y, z, c = col // 4, row // 2, lax.rem(col, 4), lax.rem(row, 2)
    mate = device(x, y, z, 1 - c)
    right, left = turn(x, 1), turn(x, 3)

    def x_peer(d):
        return device(turn(x, d), y, z, c)

    def y_peer(d):
        return device(x, turn(y, d), z, c)

    def z_peer(d):
        return device(x, y, turn(z, d), c)

    def row_peer(e, m):
        return device(x, turn(y, e), z, c + m - 2 * c * m)

    def row_from(e, m):
        return turn(y, 4 - e) * 2 + c + m - 2 * c * m

    def w_block(j, owner, start, size):
        return w.at[j, pl.ds(aligned(owner * 384 + start, 192), size), :]

    def w_fetch(j):
        return pltpu.make_async_copy(
            w_ref.at[:, pl.ds(aligned(j * 384, 128), 384)], w_block(j, x, 0, 384), w_s.at[j]
        )

    @pl.loop(0, HEADS_OWN)
    def _(j):
        w_fetch(j).start()

    fetches = [
        pltpu.make_async_copy(wo_ref, wo.at[z], l_s.at[0]),
        pltpu.make_async_copy(ew_ref, ew.at[z], l_s.at[1]),
        pltpu.make_async_copy(pos_ref, pos.at[y, c], l_s.at[2]),
        pltpu.make_async_copy(
            dp_ref.at[:, pl.ds(aligned(row * 384, 128), 384)], dpw, l_s.at[3]
        ),
        pltpu.make_async_copy(do_ref, dow, l_s.at[4]),
        pltpu.make_async_copy(pw_ref, pxw, l_s.at[5]),
    ]

    gains[x] = jnp.broadcast_to(ig_ref[...].reshape(1, 384), (8, 384))
    fgains[z] = jnp.broadcast_to(fg_ref[...].reshape(1, 384), (8, 384))

    barrier = pltpu.get_barrier_semaphore()
    peers = (
        [x_peer(d) for d in range(1, 4)]
        + [z_peer(d) for d in range(1, 4)]
        + [row_peer(k // 2, k % 2) for k in range(1, 8)]
    )
    for peer in peers:
        pl.semaphore_signal(barrier, inc=1, device_id=peer, device_id_type=MESH)
    pl.semaphore_wait(barrier, len(peers))

    def raw_copy(d):
        return remote(x_ref.at[turn(x, d)], raw.at[x], x_s.at[d], x_r.at[d], x_peer(d))

    def gain_copy(d):
        return remote(gains.at[x], gains.at[x], g_s.at[d], g_r.at[d], x_peer(d))

    def own_copy(d):
        return remote(x_ref.at[:, turn(z, d)], own.at[z], o_s.at[d], o_r.at[d], z_peer(d))

    def fgain_copy(d):
        return remote(fgains.at[z], fgains.at[z], f_s.at[d], f_r.at[d], z_peer(d))

    def wo_copy(d, half):
        block = wo.at[z, 384 * half : 384 * half + 384]
        return remote(block, block, wo_s.at[half, d], wo_r.at[half, d], z_peer(d))

    for d in (1, 3, 2):
        gain_copy(d).start()
        raw_copy(d).start()
    for fetch in fetches:
        fetch.start()
    raw[x] = x_ref[x]
    own[z] = x_ref[:, z]

    def w_send(j, way):
        block = w_block(j, x, 0, 384)
        target = device(right if way == 0 else left, y, z, c)
        return remote(block, block, wn_s.at[way, j], wn_r.at[way, j], target)

    def w_got(j, way):
        block = w_block(j, left if way == 0 else right, 0, 384)
        return remote(block, block, wn_s.at[way, j], wn_r.at[way, j], mate)

    def w_forward(j, way):
        block = w_block(j, left if way == 0 else right, 192 * way, 192)
        target = device(right if way == 0 else left, y, z, c)
        return remote(block, block, wf_s.at[way, j], wf_r.at[way, j], target)

    def w_far(j, way):
        block = w_block(j, turn(x, 2), 192 * way, 192)
        return remote(block, block, wf_s.at[way, j], wf_r.at[way, j], mate)

    def w_start(j):
        w_fetch(j).wait()
        w_send(j, 0).start()
        w_send(j, 1).start()

    def w_step(j):
        w_got(j, 0).wait_recv()
        w_forward(j, 0).start()
        w_got(j, 1).wait_recv()
        w_forward(j, 1).start()

        @pl.when(j + 3 < HEADS_OWN)
        def _():
            w_start(j + 3)

    w_start(0)
    w_start(1)
    w_start(2)
    fetches[0].wait()
    wo_copy(1, 0).start()
    wo_copy(3, 0).start()

    def stat_copy(n, d, owner):
        block = stats.at[n, owner]
        peer = z_peer(d) if n == 0 else x_peer(d)
        return remote(block, block, st_s.at[n, d], st_r.at[n, d], peer)

    def share_stats(n, total, square):
        lane = lax.broadcasted_iota(jnp.int32, (128, 128), 1)
        me = z if n == 0 else x
        stats[n, me] = jnp.transpose(jnp.where(lane == 0, total, square))[0:8]
        for d in (1, 3, 2):
            stat_copy(n, d, me).start()
        for d in (1, 3, 2):
            stat_copy(n, d, turn(me, 4 - d)).wait_recv()
        sums = jnp.transpose(jnp.sum(stats[n], axis=0))
        average = sums[:, 0:1] / D
        spread = sums[:, 1:2] / D - average * average
        return average, lax.rsqrt(spread + epsilon)

    for d in (1, 3, 2):
        there = turn(x, 4 - d)
        remote(gains.at[there], gains.at[there], g_s.at[d], g_r.at[d], mate).wait_recv()
        remote(raw.at[there], raw.at[there], x_s.at[d], x_r.at[d], mate).wait_recv()
    total, square = 0.0, 0.0
    for g in range(4):
        block = raw[g].reshape(128, 384).astype(f32)
        total = total + jnp.sum(block, axis=-1, keepdims=True)
        square = square + jnp.sum(block * block, axis=-1, keepdims=True)
    average, rate = share_stats(0, total, square)
    for g in range(4):
        block = raw[g].reshape(128, 384).astype(f32)
        block = (block - average) * rate * gains[g, 0:1, :]
        a[y, c, :, 384 * g : 384 * g + 384] = block.astype(bf16)

    def spread_rows(block, s_y, r_y, s_c, r_c):
        for e in (1, 3, 2):
            remote(block, block, s_y.at[e], r_y.at[e], y_peer(e)).start()
        remote(block, block, s_c.at[0], r_c.at[0], mate).start()

    spread_rows(a.at[y, c], ay_s, ay_r, ac_s, ac_r)
    fetches[2].wait()
    spread_rows(pos.at[y, c], p_s, p_r, pc_s, pc_r)
    wo_copy(2, 0).start()
    for d in (1, 3, 2):
        wo_copy(d, 1).start()
    w_step(0)
    w_step(1)

    def way_of(s):
        return s // 2

    def ahead(way):
        return turn(z, 1 + 2 * way)

    def behind(way):
        return turn(z, 3 - 2 * way)

    def piece(s):
        return pl.ds(aligned(s * 64, 64), 64)

    def hop_copy(j, s):
        way = way_of(s)
        return remote(
            cs.at[j, turn(z, 2), piece(s), :],
            hop.at[j, piece(s), :],
            h_s.at[j, s],
            h_r.at[j, s],
            device(x, y, ahead(way), c),
        )

    def c_copy(j, s, way):
        there = ahead(way)
        return remote(
            cs.at[j, there, piece(s), :],
            cr.at[way, j, piece(s), :],
            c_s.at[way, j],
            c_r.at[way, j],
            device(x, y, there, c),
        )

    def c_all(j, way):
        return remote(
            cs.at[j, ahead(way)], cr.at[way, j], c_s.at[way, j], c_r.at[way, j], mate
        )

    def combine(j, i):
        s = turn(y, 4 - near(i))
        way = way_of(s)
        hop_copy(j, s).wait_recv()
        both = cs[j, ahead(way), piece(s), :].astype(f32) + hop[j, piece(s), :].astype(f32)
        cs[j, ahead(way), piece(s), :] = both.astype(bf16)
        c_copy(j, s, way).start()

    def att_send(j, heads):
        block = att.at[x, :, pl.ds(aligned(j * 128, 128), heads * 128)]
        for d in (1, 3, 2):
            remote(block, block, t_s.at[d], t_r.at[d], x_peer(d)).start()

    def attend_head(j):
        c_all(j, 0).wait_recv()
        c_all(j, 1).wait_recv()
        projected = cs[j, z].astype(f32) + cr[0, j].astype(f32) + cr[1, j].astype(f32)
        queries = norm(projected[:, 0:128], qg_ref[...]).astype(bf16)
        keys = norm(projected[:, 128:256], kg_ref[...]).astype(bf16)
        mixed = attention(queries, keys, projected[:, 256:384].astype(bf16), 128 ** (-0.5))
        att[x, :, pl.ds(aligned(j * 128, 128), 128)] = mixed

    def ew_half(owner, half):
        return ew.at[owner, pl.ds(aligned(half * 192, 192), 192), :]

    def ex_copy(d):
        block = ew_half(z, c)
        return remote(block, block, ex_s.at[d], ex_r.at[d], z_peer(d))

    def ex_got(d):
        block = ew_half(turn(z, 4 - d), c)
        return remote(block, block, ex_s.at[d], ex_r.at[d], mate)

    def ec_copy(d):
        block = ew_half(turn(z, 4 - d), c)
        return remote(block, block, ec_s.at[d], ec_r.at[d], mate)

    def ec_got(d):
        block = ew_half(turn(z, 4 - d), 1 - c)
        return remote(block, block, ec_s.at[d], ec_r.at[d], mate)

    first_half = lax.broadcasted_iota(jnp.int32, (256, 128), 1) < 64

    def decoder_heads(tokens):
        normed = norm(tokens, dg_ref[...]).astype(bf16)
        made = jnp.dot(normed, dpw[...], preferred_element_type=f32)
        queries = jnp.concatenate([made[:, 0:64], made[:, 192:256]], axis=1)
        keys = jnp.concatenate([made[:, 64:128], made[:, 256:320]], axis=1)
        values = jnp.concatenate([made[:, 128:192], made[:, 320:384]], axis=1)
        query_gain = jnp.concatenate([dqg_ref[...], dqg_ref[...]], axis=1)
        key_gain = jnp.concatenate([dkg_ref[...], dkg_ref[...]], axis=1)
        queries = pair_norm(queries, query_gain)
        one = jnp.where(first_half, queries, 0.0).astype(bf16)
        two = jnp.where(first_half, 0.0, queries).astype(bf16)
        return one, two, pair_norm(keys, key_gain).astype(bf16), values

    def decoder_mix(queries, keys, values):
        scores = lax.dot_general(queries, keys, LAST, preferred_element_type=f32)
        weights = jnp.exp(scores * 64 ** (-0.5)).astype(bf16)
        return jnp.dot(weights, values, preferred_element_type=f32)

    def block_rows(i):
        return pl.ds(aligned(i * 256, 256), 256)

    def hidden_heads(i):
        rows = block_rows(i)
        positions = lax.broadcasted_iota(jnp.int32, (256, 256), 0) + i * 256
        select = jnp.where(positions == vi_ref[...], 1.0, 0.0)
        sel[rows, :] = select.astype(bf16)
        hidden = 1.0 - jnp.sum(select, axis=1, keepdims=True)
        tokens = hidden * mask_ref[...] + pos[i].reshape(256, DD).astype(f32) + scr[0:1, :]

        @pl.when(i == y)
        def _():
            tok[...] = tokens

        one, two, keys, values = decoder_heads(tokens)
        dq[0, rows, :] = one
        dq[1, rows, :] = two
        dk[rows, :] = keys
        dv[rows, 0:128] = (values * hidden).astype(bf16)
        dv[rows, 128:256] = jnp.broadcast_to(hidden, (256, 128)).astype(bf16)

    def hidden_mix(i):
        rows = block_rows(i)
        for h in range(2):
            base[h, rows, :] = decoder_mix(dq[h, rows, :], dk[...], dv[...])

    def visible_base():
        places = jnp.broadcast_to(vi_ref[...].astype(f32), (8, 256))
        places = jnp.transpose(places)[:, 0:1].astype(jnp.int32)
        positions = lax.broadcasted_iota(jnp.int32, (256, 1024), 1)
        select = jnp.where(positions == places, 1.0, 0.0).astype(bf16)
        chosen = jnp.dot(select, pos[...].reshape(1024, DD), preferred_element_type=f32)
        tokv[...] = chosen + scr[0:1, :]

    ids = lax.broadcasted_iota(jnp.int32, script_ref.shape, 0)
    scripted = jnp.sum(
        jnp.where(ids == si_ref[...], script_ref[...].astype(f32), 0.0), axis=0, keepdims=True
    )
    scr[...] = jnp.broadcast_to(scripted, (8, DD))

    @pl.loop(0, HEADS_OWN)
    def _(j):
        w_far(j, 0).wait_recv()
        w_far(j, 1).wait_recv()

        @pl.loop(0, 4)
        def _(i):
            e = near(i)
            s = turn(y, 4 - e)

            @pl.when(j == 0)
            def _():
                @pl.when(i > 0)
                def _():
                    got = a.at[s, c]
                    remote(got, got, ay_s.at[e], ay_r.at[e], mate).wait_recv()
                    remote(got, got, ac_s.at[e], ac_r.at[e], mate).start()

                other = a.at[s, 1 - c]
                remote(other, other, ac_s.at[e], ac_r.at[e], mate).wait_recv()

            product = jnp.dot(a[s].reshape(256, 1536), w[j], preferred_element_type=f32).astype(bf16)
            for core in range(2):
                for image in range(4):
                    first = core * 128 + image * 32
                    rows = pl.ds(aligned(s * 64 + core * 32, 32), 32)
                    cs[j, image, rows, :] = product[first : first + 32]
            hop_copy(j, s).start()
            c_copy(j, s, 1 - way_of(s)).start()

            @pl.when((j == 0) & (i > 0))
            def _():
                combine(0, i - 1)

        @pl.when(j == 0)
        def _():
            combine(0, 3)

        @pl.when(j == 2)
        def _():
            for e in (1, 3, 2):
                got = pos.at[turn(y, 4 - e), c]
                remote(got, got, p_s.at[e], p_r.at[e], mate).wait_recv()
                remote(got, got, pc_s.at[e], pc_r.at[e], mate).start()

        @pl.when(j > 1)
        def _():
            @pl.loop(0, 4)
            def _(i):
                combine(j - 1, i)

            attend_head(j - 2)

        @pl.when(j + 2 < HEADS_OWN)
        def _():
            w_step(j + 2)

        @pl.when(j == 3)
        def _():
            att_send(0, 2)

        @pl.when(j > 3)
        def _():
            att_send(j - 2, 1)

        @pl.when(j == 3)
        def _():
            fetches[3].wait()
            for e in range(4):
                got = pos.at[turn(y, 4 - e), 1 - c]
                remote(got, got, pc_s.at[e], pc_r.at[e], mate).wait_recv()

        @pl.when((j == 3) | (j == 4))
        def _():
            @pl.loop(0, 2)
            def _(i):
                hidden_heads((j - 3) * 2 + i)

    @pl.loop(0, 2)
    def _(i):
        hidden_mix(i)

    @pl.loop(0, 4)
    def _(i):
        combine(HEADS_OWN - 1, i)

    attend_head(HEADS_OWN - 2)
    att_send(HEADS_OWN - 2, 1)
    fetches[1].wait()
    for d in (1, 3, 2):
        fgain_copy(d).start()
        own_copy(d).start()
        ex_copy(d).start()

    @pl.loop(2, 4)
    def _(i):
        hidden_mix(i)

    visible_base()
    attend_head(HEADS_OWN - 1)
    att_send(HEADS_OWN - 1, 1)
    for d in (1, 3, 2):
        there = turn(z, 4 - d)
        for half in range(2):
            block = wo.at[there, 384 * half : 384 * half + 384]
            remote(block, block, wo_s.at[half, d], wo_r.at[half, d], mate).wait_recv()
    for d in (1, 3, 2):
        whole = att.at[turn(x, 4 - d)]
        remote(whole, whole, t_s.at[d], t_r.at[d], mate).wait_recv()

    def block_at(i):
        return turn(z, 4 - near(i))

    def mate_copy(i):
        there = block_at(i)
        return remote(po.at[there, 1 - c], pr.at[there], m_s.at[i], m_r.at[i], mate)

    def y_copy(i, e):
        there = block_at(i)
        return remote(
            po.at[there, c, turn(y, e)], yr.at[e - 1, there], y_s.at[e, i], y_r.at[e, i], y_peer(e)
        )

    def reduce_rows(i):
        there = block_at(i)
        mate_copy(i).wait_recv()
        both = po[there, c].astype(f32) + pr[there].astype(f32)
        po[there, c] = both.astype(bf16)
        for e in (1, 3, 2):
            y_copy(i, e).start()

    @pl.loop(0, 4)
    def _(i):
        there = block_at(i)

        product = jnp.dot(
            att[...].reshape(1024, 768), wo[there], preferred_element_type=f32
        )
        product = product.astype(bf16)
        for image in range(4):
            for part in range(8):
                first = image * 256 + part * 32
                po[there, part % 2, part // 2, image * 32 : image * 32 + 32, :] = product[
                    first : first + 32
                ]
        mate_copy(i).start()

        @pl.when(i > 0)
        def _():
            reduce_rows(i - 1)

    reduce_rows(3)

    def enc_copy(d):
        return remote(es.at[turn(z, d)], enc_ref.at[:, z], en_s.at[d], en_r.at[d], z_peer(d))

    for d in (1, 3, 2):
        there = turn(z, 4 - d)
        remote(fgains.at[there], fgains.at[there], f_s.at[d], f_r.at[d], mate).wait_recv()
        remote(own.at[there], own.at[there], o_s.at[d], o_r.at[d], mate).wait_recv()
    total, square = 0.0, 0.0
    for i in range(4):
        there = block_at(i)
        for e in (1, 3, 2):
            y_copy(i, e).wait_recv()
        block = own[there].reshape(128, 384).astype(f32) + po[there, c, y].astype(f32)
        for e in range(3):
            block = block + yr[e, there].astype(f32)
        res[there] = block
        es[there] = block.astype(bf16).reshape(4, 32, 384)
        total = total + jnp.sum(block, axis=-1, keepdims=True)
        square = square + jnp.sum(block * block, axis=-1, keepdims=True)
    for d in (1, 3, 2):
        ex_got(d).wait_recv()
        ec_copy(d).start()
    average, rate = share_stats(1, total, square)
    for g in range(4):
        block = (res[g] - average) * rate * fgains[g, 0:1, :]
        en[:, 384 * g : 384 * g + 384] = block.astype(bf16)
    for d in (1, 3, 2):
        enc_copy(d).start()
    enc_ref[:, z] = es[z]

    for d in (1, 3, 2):
        ec_got(d).wait_recv()
    product = jnp.dot(en[...], ew[...].reshape(1536, DD), preferred_element_type=f32)
    eo[...] = product.astype(bf16).reshape(4, 32, DD)

    def eb_copy(d):
        return remote(eo.at[turn(x, d)], er.at[d - 1], eb_s.at[d], eb_r.at[d], x_peer(d))

    for d in (1, 3, 2):
        eb_copy(d).start()
    embedded = eo[x].astype(f32)
    for d in (1, 3, 2):
        eb_copy(d).wait_recv()
        embedded = embedded + er[d - 1].astype(f32)
    vis[row] = (embedded + eb_ref[...]).astype(bf16)

    def vis_copy(k):
        block = vis.at[row]
        return remote(block, block, v_s.at[k], v_r.at[k], row_peer(k // 2, k % 2))

    for k in (4, 5, 2, 3, 6, 7, 1):
        vis_copy(k).start()

    for k in range(1, 8):
        block = vis.at[row_from(k // 2, k % 2)]
        remote(block, block, v_s.at[k], v_r.at[k], mate).wait_recv()
    one, two, keys, values = decoder_heads(vis[...].reshape(256, DD).astype(f32) + tokv[...])
    vq[0] = one
    vq[1] = two
    vk[...] = keys
    vv[:, 0:128] = values.astype(bf16)
    vv[:, 128:256] = jnp.ones((256, 128), bf16)

    def mix_copy(e, m):
        owner = turn(y, e) * 2 + c + m - 2 * c * m
        block = da.at[:, pl.ds(aligned(row * 128, 128), 128)]
        return remote(dm.at[owner], block, d_s.at[e, m], d_r.at[e, m], row_peer(e, m))

    def mix_got(e, m):
        block = da.at[:, pl.ds(aligned(row_from(e, m) * 128, 128), 128)]
        return remote(block, block, d_s.at[e, m], d_r.at[e, m], mate)

    def finish(both):
        one = both[0][:, 0:128] / both[0][:, 128:256]
        two = both[1][:, 0:128] / both[1][:, 128:256]
        return jnp.where(first_half, one, two).astype(bf16)

    visible = finish(
        [
            decoder_mix(vq[h], dk[...], dv[...]) + decoder_mix(vq[h], vk[...], vv[...])
            for h in range(2)
        ]
    )

    @pl.loop(0, 4)
    def _(i):
        e = near(3 - i)
        there = turn(y, e)
        rows = block_rows(there)
        mixed = finish(
            [base[h, rows, :] + decoder_mix(dq[h, rows, :], vk[...], vv[...]) for h in range(2)]
        )
        placed = jnp.dot(sel[rows, :], visible, preferred_element_type=f32)
        hidden = dv[rows, 128:256].astype(f32) > 0.5
        mixed = jnp.where(hidden, mixed.astype(f32), placed).astype(bf16)
        dm[there * 2] = mixed[0:128]
        dm[there * 2 + 1] = mixed[128:256]

        @pl.when(e > 0)
        def _():
            mix_copy(e, 0).start()

        mix_copy(e, 1).start()

    da[:, pl.ds(aligned(row * 128, 128), 128)] = dm[row]
    fetches[4].wait()
    fetches[5].wait()
    for k in range(1, 8):
        mix_got(k // 2, k % 2).wait_recv()
    tokens = tok[pl.ds(aligned(c * 128, 128), 128), :] + jnp.dot(
        sel[pl.ds(aligned(row * 128, 128), 128), :],
        vis[...].reshape(256, DD),
        preferred_element_type=f32,
    )
    decoded = tokens + jnp.dot(da[...], dow[...], preferred_element_type=f32)
    normed = norm(decoded, hg_ref[...]).astype(bf16)
    predicted = jnp.dot(normed, pxw[...], preferred_element_type=f32) + pb_ref[...].reshape(1, 768)
    pred_ref[0] = predicted.astype(bf16)

    for d in range(1, 4):
        block = enc_ref.at[:, turn(z, 4 - d)]
        remote(block, block, en_s.at[d], en_r.at[d], mate).wait_recv()
        enc_copy(d).wait_send()
        gain_copy(d).wait_send()
        raw_copy(d).wait_send()
        own_copy(d).wait_send()
        fgain_copy(d).wait_send()
        wo_copy(d, 0).wait_send()
        wo_copy(d, 1).wait_send()
        stat_copy(0, d, z).wait_send()
        stat_copy(1, d, x).wait_send()
        ex_copy(d).wait_send()
        eb_copy(d).wait_send()
        whole = att.at[x]
        remote(whole, whole, t_s.at[d], t_r.at[d], mate).wait_send()
        ec_copy(d).wait_send()
    for e in range(4):
        for block, s_y, r_y, s_c, r_c in (
            (a, ay_s, ay_r, ac_s, ac_r),
            (pos, p_s, p_r, pc_s, pc_r),
        ):
            if e > 0:
                own = block.at[y, c]
                remote(own, own, s_y.at[e], r_y.at[e], mate).wait_send()
            passed = block.at[turn(y, 4 - e), c]
            remote(passed, passed, s_c.at[e], r_c.at[e], mate).wait_send()
        mate_copy(e).wait_send()
        for i in range(1, 4):
            y_copy(e, i).wait_send()
    for k in range(1, 8):
        vis_copy(k).wait_send()
        mix_copy(k // 2, k % 2).wait_send()

    @pl.loop(0, HEADS_OWN)
    def _(j):
        for way in range(2):
            w_send(j, way).wait_send()
            w_forward(j, way).wait_send()

    @pl.loop(0, HEADS_OWN)
    def _(j):
        for way in range(2):
            c_all(j, way).wait_send()

        @pl.loop(0, 4)
        def _(s):
            hop_copy(j, s).wait_send()


VMEM = pl.BlockSpec(memory_space=pltpu.VMEM)
ANY = pl.BlockSpec(memory_space=pl.ANY)


def local(
    visible_patches,
    input_gain,
    encoder_project,
    query_gain,
    key_gain,
    output_weight,
    final_gain,
    embed_weight,
    embed_bias,
    mask_token,
    position_embed,
    script_table,
    decoder_gain,
    decoder_project,
    decoder_query,
    decoder_key,
    decoder_output,
    head_gain,
    pixel_weight,
    pixel_bias,
    visible_index,
    script_index,
):
    def flat(vector):
        return vector.reshape(1, -1)

    dma = pltpu.SemaphoreType.DMA
    two = [dma((4,)), dma((4,))]
    encoded, predicted = pl.pallas_call(
        kernel,
        out_shape=(
            jax.ShapeDtypeStruct((4, 4, 32, 384), bf16),
            jax.ShapeDtypeStruct((1, 128, 768), bf16),
        ),
        in_specs=[
            VMEM, VMEM, ANY, VMEM, VMEM, ANY, VMEM, ANY, VMEM, VMEM, ANY,
            VMEM, VMEM, ANY, VMEM, VMEM, ANY, VMEM, ANY, VMEM, VMEM, VMEM,
        ],
        out_specs=(VMEM, VMEM),
        scratch_shapes=[
            pltpu.VMEM((4, 8, 384), f32),
            pltpu.VMEM((4, 8, 384), f32),
            pltpu.VMEM((4, 4, 32, 384), bf16),
            pltpu.VMEM((4, 4, 32, 384), bf16),
            pltpu.VMEM((2, 4, 8, 128), f32),
            pltpu.VMEM((4, 2, 128, 1536), bf16),
            pltpu.VMEM((HEADS_OWN, 1536, 384), bf16),
            pltpu.VMEM((4, 768, 384), bf16),
            pltpu.VMEM((HEADS_OWN, 4, 256, 384), bf16),
            pltpu.VMEM((2, HEADS_OWN, 256, 384), bf16),
            pltpu.VMEM((HEADS_OWN, 256, 384), bf16),
            pltpu.VMEM((4, 256, 768), bf16),
            pltpu.VMEM((4, 2, 4, 128, 384), bf16),
            pltpu.VMEM((4, 4, 128, 384), bf16),
            pltpu.VMEM((3, 4, 128, 384), bf16),
            pltpu.VMEM((4, 128, 384), f32),
            pltpu.VMEM((128, 1536), bf16),
            pltpu.VMEM((4, 4, 32, 384), bf16),
            pltpu.VMEM((4, 384, DD), bf16),
            pltpu.VMEM((4, 2, 128, DD), bf16),
            pltpu.VMEM((DD, 384), bf16),
            pltpu.VMEM((DD, DD), bf16),
            pltpu.VMEM((DD, 768), bf16),
            pltpu.VMEM((4, 32, DD), bf16),
            pltpu.VMEM((3, 32, DD), bf16),
            pltpu.VMEM((8, 32, DD), bf16),
            pltpu.VMEM((8, DD), f32),
            pltpu.VMEM((1024, 256), bf16),
            pltpu.VMEM((256, DD), f32),
            pltpu.VMEM((256, DD), f32),
            pltpu.VMEM((2, 1024, 128), bf16),
            pltpu.VMEM((1024, 128), bf16),
            pltpu.VMEM((1024, 256), bf16),
            pltpu.VMEM((2, 1024, 256), f32),
            pltpu.VMEM((2, 256, 128), bf16),
            pltpu.VMEM((256, 128), bf16),
            pltpu.VMEM((256, 256), bf16),
            pltpu.VMEM((8, 128, 128), bf16),
            pltpu.VMEM((128, DD), bf16),
            dma((6,)),
            dma((HEADS_OWN,)),
            *two,
            *two,
            *two,
            *two,
            dma((2, 4)), dma((2, 4)),
            dma((2, 4)), dma((2, 4)),
            *two,
            *two,
            dma((2, HEADS_OWN)), dma((2, HEADS_OWN)),
            dma((2, HEADS_OWN)), dma((2, HEADS_OWN)),
            dma((HEADS_OWN, 4)), dma((HEADS_OWN, 4)),
            dma((2, HEADS_OWN)), dma((2, HEADS_OWN)),
            *two,
            *two,
            *two,
            *two,
            *two,
            *two,
            dma((4, 4)), dma((4, 4)),
            *two,
            *two,
            dma((8,)), dma((8,)),
            dma((4, 2)), dma((4, 2)),
        ],
        compiler_params=pltpu.CompilerParams(
            collective_id=0, has_side_effects=True, vmem_limit_bytes=62 << 20
        ),
        name="masked_patches",
    )(
        visible_patches.reshape(4, 4, 32, 384), input_gain, encoder_project, flat(query_gain), flat(key_gain),
        output_weight, final_gain, embed_weight, flat(embed_bias), flat(mask_token),
        position_embed, script_table, flat(decoder_gain), decoder_project, flat(decoder_query),
        flat(decoder_key), decoder_output, flat(head_gain), pixel_weight, pixel_bias,
        visible_index, flat(script_index),
    )
    return encoded.reshape(16, 32, 384), predicted


def solution(mesh):
    return jax.shard_map(
        local,
        mesh=mesh,
        in_specs=(
            P(None, "row", "col"),
            P("col"),
            P("col", "row"),
            P(),
            P(),
            P("row", "col"),
            P("col"),
            P("col", None),
            P(),
            P(),
            P("row", None),
            P(),
            P(),
            P(),
            P(),
            P(),
            P(),
            P(),
            P(),
            P(),
            P("col", None),
            P("col"),
        ),
        out_specs=(P(None, "row", "col"), P("col", "row", None)),
        check_vma=False,
    )
```

```python
import jax
import jax.numpy as jnp
from jax import lax
from jax.experimental import pallas as pl
from jax.experimental.pallas import tpu as pltpu
from jax.sharding import PartitionSpec as P

D = 6144
DD = 1024
HEADS_OWN = 6
MESH = pl.DeviceIdType.MESH
bf16 = jnp.bfloat16
f32 = jnp.float32

epsilon = 1e-06
LAST = (((1,), (1,)), ((), ()))


def turn(i, by):
    return lax.rem(i + by, 4)


def near(i):
    return i + (i // 2) * (5 - 2 * i)


def device(x, y, z, c):
    return (y * 2 + c, x * 4 + z)


def remote(src, dst, send_sem, recv_sem, where):
    return pltpu.make_async_remote_copy(
        src_ref=src,
        dst_ref=dst,
        send_sem=send_sem,
        recv_sem=recv_sem,
        device_id=where,
        device_id_type=MESH,
    )


def aligned(index, multiple):
    return pl.multiple_of(index, multiple)


def norm(values, gain_vector):
    amount = values.shape[-1]
    average = jnp.sum(values, axis=-1, keepdims=True) / amount
    spread = jnp.sum(values * values, axis=-1, keepdims=True) / amount - average * average
    return (values - average) * lax.rsqrt(spread + epsilon) * gain_vector


def pair_norm(values, gain_vector):
    first = lax.broadcasted_iota(jnp.int32, values.shape, 1) < 64

    def mean(v):
        one = jnp.sum(jnp.where(first, v, 0.0), axis=-1, keepdims=True)
        two = jnp.sum(jnp.where(first, 0.0, v), axis=-1, keepdims=True)
        return jnp.where(first, one, two) / 64

    average = mean(values)
    spread = mean(values * values) - average * average
    return (values - average) * lax.rsqrt(spread + epsilon) * gain_vector


def attention(queries, keys, values, factor):
    scores = lax.dot_general(queries, keys, LAST, preferred_element_type=f32) * factor
    weights = jnp.exp(scores).astype(bf16)
    totals = jnp.sum(weights.astype(f32), axis=-1, keepdims=True)
    mixture = jnp.dot(weights, values, preferred_element_type=f32)
    return (mixture / totals).astype(bf16)


def kernel(
    x_ref, ig_ref, w_ref, qg_ref, kg_ref, wo_ref, fg_ref, ew_ref, eb_ref, mask_ref, pos_ref,
    script_ref, dg_ref, dp_ref, dqg_ref, dkg_ref, do_ref, hg_ref, pw_ref, pb_ref, vi_ref, si_ref,
    enc_ref, pred_ref,
    gains, fgains, raw, own, stats, a, w, wo, cs, cr, hop, att, po, pr, yr, yhop, res, en, es, ew, pos, dpw, dow, pxw,
    eo, er, vis, scr, sel, tok, tokv, dq, dk, dv, base, vq, vk, vv, dm, da,
    l_s, w_s, g_s, g_r, f_s, f_r, x_s, x_r, o_s, o_r, wo_s, wo_r, st_s, st_r, ay_s, ay_r, ac_s, ac_r, wn_s, wn_r, wf_s, wf_r,
    h_s, h_r, c_s, c_r, t_s, t_r, p_s, p_r, pc_s, pc_r, ex_s, ex_r, ec_s, ec_r,
    m_s, m_r, yh_s, yh_r, y_s, y_r, en_s, en_r, eb_s, eb_r, v_s, v_r, vc_s, vc_r, d_s, d_r,
):
    row, col = lax.axis_index("row"), lax.axis_index("col")
    x, y, z, c = col // 4, row // 2, lax.rem(col, 4), lax.rem(row, 2)
    mate = device(x, y, z, 1 - c)
    right, left = turn(x, 1), turn(x, 3)

    def x_peer(d):
        return device(turn(x, d), y, z, c)

    def y_peer(d):
        return device(x, turn(y, d), z, c)

    def z_peer(d):
        return device(x, y, turn(z, d), c)

    def row_peer(e, m):
        return device(x, turn(y, e), z, c + m - 2 * c * m)

    def row_from(e, m):
        return turn(y, 4 - e) * 2 + c + m - 2 * c * m

    def w_block(j, owner, start, size):
        return w.at[j, pl.ds(aligned(owner * 384 + start, 192), size), :]

    def w_fetch(j):
        return pltpu.make_async_copy(
            w_ref.at[:, pl.ds(aligned(j * 384, 128), 384)], w_block(j, x, 0, 384), w_s.at[j]
        )

    @pl.loop(0, HEADS_OWN)
    def _(j):
        w_fetch(j).start()

    fetches = [
        pltpu.make_async_copy(wo_ref, wo.at[z], l_s.at[0]),
        pltpu.make_async_copy(ew_ref, ew.at[z], l_s.at[1]),
        pltpu.make_async_copy(pos_ref, pos.at[y, c], l_s.at[2]),
        pltpu.make_async_copy(
            dp_ref.at[:, pl.ds(aligned(row * 384, 128), 384)], dpw, l_s.at[3]
        ),
        pltpu.make_async_copy(do_ref, dow, l_s.at[4]),
        pltpu.make_async_copy(pw_ref, pxw, l_s.at[5]),
    ]

    gains[x] = jnp.broadcast_to(ig_ref[...].reshape(1, 384), (8, 384))
    fgains[z] = jnp.broadcast_to(fg_ref[...].reshape(1, 384), (8, 384))

    barrier = pltpu.get_barrier_semaphore()
    peers = (
        [x_peer(d) for d in range(1, 4)]
        + [z_peer(d) for d in range(1, 4)]
        + [row_peer(k // 2, k % 2) for k in range(1, 8)]
    )
    for peer in peers:
        pl.semaphore_signal(barrier, inc=1, device_id=peer, device_id_type=MESH)
    pl.semaphore_wait(barrier, len(peers))

    def raw_copy(d):
        return remote(x_ref.at[turn(x, d)], raw.at[x], x_s.at[d], x_r.at[d], x_peer(d))

    def gain_copy(d):
        return remote(gains.at[x], gains.at[x], g_s.at[d], g_r.at[d], x_peer(d))

    def own_copy(d):
        return remote(x_ref.at[:, turn(z, d)], own.at[z], o_s.at[d], o_r.at[d], z_peer(d))

    def fgain_copy(d):
        return remote(fgains.at[z], fgains.at[z], f_s.at[d], f_r.at[d], z_peer(d))

    def wo_copy(d, half):
        block = wo.at[z, 384 * half : 384 * half + 384]
        return remote(block, block, wo_s.at[half, d], wo_r.at[half, d], z_peer(d))

    for d in (1, 3, 2):
        gain_copy(d).start()
        raw_copy(d).start()
    for fetch in fetches:
        fetch.start()
    raw[x] = x_ref[x]
    own[z] = x_ref[:, z]

    def w_send(j, way):
        block = w_block(j, x, 0, 384)
        target = device(right if way == 0 else left, y, z, c)
        return remote(block, block, wn_s.at[way, j], wn_r.at[way, j], target)

    def w_got(j, way):
        block = w_block(j, left if way == 0 else right, 0, 384)
        return remote(block, block, wn_s.at[way, j], wn_r.at[way, j], mate)

    def w_forward(j, way):
        block = w_block(j, left if way == 0 else right, 192 * way, 192)
        target = device(right if way == 0 else left, y, z, c)
        return remote(block, block, wf_s.at[way, j], wf_r.at[way, j], target)

    def w_far(j, way):
        block = w_block(j, turn(x, 2), 192 * way, 192)
        return remote(block, block, wf_s.at[way, j], wf_r.at[way, j], mate)

    def w_start(j):
        w_fetch(j).wait()
        w_send(j, 0).start()
        w_send(j, 1).start()

    def w_step(j):
        w_got(j, 0).wait_recv()
        w_forward(j, 0).start()
        w_got(j, 1).wait_recv()
        w_forward(j, 1).start()

        @pl.when(j + 3 < HEADS_OWN)
        def _():
            w_start(j + 3)

    w_start(0)
    w_start(1)
    w_start(2)
    fetches[0].wait()
    wo_copy(1, 0).start()
    wo_copy(3, 0).start()

    def stat_copy(n, d, owner):
        block = stats.at[n, owner]
        peer = z_peer(d) if n == 0 else x_peer(d)
        return remote(block, block, st_s.at[n, d], st_r.at[n, d], peer)

    def share_stats(n, total, square):
        lane = lax.broadcasted_iota(jnp.int32, (128, 128), 1)
        me = z if n == 0 else x
        stats[n, me] = jnp.transpose(jnp.where(lane == 0, total, square))[0:8]
        for d in (1, 3, 2):
            stat_copy(n, d, me).start()
        for d in (1, 3, 2):
            stat_copy(n, d, turn(me, 4 - d)).wait_recv()
        sums = jnp.transpose(jnp.sum(stats[n], axis=0))
        average = sums[:, 0:1] / D
        spread = sums[:, 1:2] / D - average * average
        return average, lax.rsqrt(spread + epsilon)

    for d in (1, 3, 2):
        there = turn(x, 4 - d)
        remote(gains.at[there], gains.at[there], g_s.at[d], g_r.at[d], mate).wait_recv()
        remote(raw.at[there], raw.at[there], x_s.at[d], x_r.at[d], mate).wait_recv()
    total, square = 0.0, 0.0
    for g in range(4):
        block = raw[g].reshape(128, 384).astype(f32)
        total = total + jnp.sum(block, axis=-1, keepdims=True)
        square = square + jnp.sum(block * block, axis=-1, keepdims=True)
    average, rate = share_stats(0, total, square)
    for g in range(4):
        block = raw[g].reshape(128, 384).astype(f32)
        block = (block - average) * rate * gains[g, 0:1, :]
        a[y, c, :, 384 * g : 384 * g + 384] = block.astype(bf16)

    def spread_rows(block, s_y, r_y, s_c, r_c):
        for e in (1, 3, 2):
            remote(block, block, s_y.at[e], r_y.at[e], y_peer(e)).start()
        remote(block, block, s_c.at[0], r_c.at[0], mate).start()

    spread_rows(a.at[y, c], ay_s, ay_r, ac_s, ac_r)
    fetches[2].wait()
    spread_rows(pos.at[y, c], p_s, p_r, pc_s, pc_r)
    wo_copy(2, 0).start()
    for d in (1, 3, 2):
        wo_copy(d, 1).start()
    w_step(0)
    w_step(1)

    def way_of(s):
        return s // 2

    def ahead(way):
        return turn(z, 1 + 2 * way)

    def behind(way):
        return turn(z, 3 - 2 * way)

    def piece(s):
        return pl.ds(aligned(s * 64, 64), 64)

    def hop_copy(j, s):
        way = way_of(s)
        return remote(
            cs.at[j, turn(z, 2), piece(s), :],
            hop.at[j, piece(s), :],
            h_s.at[j, s],
            h_r.at[j, s],
            device(x, y, ahead(way), c),
        )

    def c_copy(j, s, way):
        there = ahead(way)
        return remote(
            cs.at[j, there, piece(s), :],
            cr.at[way, j, piece(s), :],
            c_s.at[way, j],
            c_r.at[way, j],
            device(x, y, there, c),
        )

    def c_all(j, way):
        return remote(
            cs.at[j, ahead(way)], cr.at[way, j], c_s.at[way, j], c_r.at[way, j], mate
        )

    def combine(j, i):
        s = turn(y, 4 - near(i))
        way = way_of(s)
        hop_copy(j, s).wait_recv()
        both = cs[j, ahead(way), piece(s), :].astype(f32) + hop[j, piece(s), :].astype(f32)
        cs[j, ahead(way), piece(s), :] = both.astype(bf16)
        c_copy(j, s, way).start()

    def att_send(j, heads):
        block = att.at[x, :, pl.ds(aligned(j * 128, 128), heads * 128)]
        for d in (1, 3, 2):
            remote(block, block, t_s.at[d], t_r.at[d], x_peer(d)).start()

    def attend_head(j):
        c_all(j, 0).wait_recv()
        c_all(j, 1).wait_recv()
        projected = cs[j, z].astype(f32) + cr[0, j].astype(f32) + cr[1, j].astype(f32)
        queries = norm(projected[:, 0:128], qg_ref[...]).astype(bf16)
        keys = norm(projected[:, 128:256], kg_ref[...]).astype(bf16)
        mixed = attention(queries, keys, projected[:, 256:384].astype(bf16), 128 ** (-0.5))
        att[x, :, pl.ds(aligned(j * 128, 128), 128)] = mixed

    def ew_half(owner, half):
        return ew.at[owner, pl.ds(aligned(half * 192, 192), 192), :]

    def ex_copy(d):
        block = ew_half(z, c)
        return remote(block, block, ex_s.at[d], ex_r.at[d], z_peer(d))

    def ex_got(d):
        block = ew_half(turn(z, 4 - d), c)
        return remote(block, block, ex_s.at[d], ex_r.at[d], mate)

    def ec_copy(d):
        block = ew_half(turn(z, 4 - d), c)
        return remote(block, block, ec_s.at[d], ec_r.at[d], mate)

    def ec_got(d):
        block = ew_half(turn(z, 4 - d), 1 - c)
        return remote(block, block, ec_s.at[d], ec_r.at[d], mate)

    first_half = lax.broadcasted_iota(jnp.int32, (256, 128), 1) < 64

    def decoder_heads(tokens):
        normed = norm(tokens, dg_ref[...]).astype(bf16)
        made = jnp.dot(normed, dpw[...], preferred_element_type=f32)
        queries = jnp.concatenate([made[:, 0:64], made[:, 192:256]], axis=1)
        keys = jnp.concatenate([made[:, 64:128], made[:, 256:320]], axis=1)
        values = jnp.concatenate([made[:, 128:192], made[:, 320:384]], axis=1)
        query_gain = jnp.concatenate([dqg_ref[...], dqg_ref[...]], axis=1)
        key_gain = jnp.concatenate([dkg_ref[...], dkg_ref[...]], axis=1)
        queries = pair_norm(queries, query_gain)
        one = jnp.where(first_half, queries, 0.0).astype(bf16)
        two = jnp.where(first_half, 0.0, queries).astype(bf16)
        return one, two, pair_norm(keys, key_gain).astype(bf16), values

    def decoder_mix(queries, keys, values):
        scores = lax.dot_general(queries, keys, LAST, preferred_element_type=f32)
        weights = jnp.exp(scores * 64 ** (-0.5)).astype(bf16)
        return jnp.dot(weights, values, preferred_element_type=f32)

    def block_rows(i):
        return pl.ds(aligned(i * 256, 256), 256)

    def hidden_heads(i):
        rows = block_rows(i)
        positions = lax.broadcasted_iota(jnp.int32, (256, 256), 0) + i * 256
        select = jnp.where(positions == vi_ref[...], 1.0, 0.0)
        sel[rows, :] = select.astype(bf16)
        hidden = 1.0 - jnp.sum(select, axis=1, keepdims=True)
        tokens = hidden * mask_ref[...] + pos[i].reshape(256, DD).astype(f32) + scr[0:1, :]

        @pl.when(i == y)
        def _():
            tok[...] = tokens

        one, two, keys, values = decoder_heads(tokens)
        dq[0, rows, :] = one
        dq[1, rows, :] = two
        dk[rows, :] = keys
        dv[rows, 0:128] = (values * hidden).astype(bf16)
        dv[rows, 128:256] = jnp.broadcast_to(hidden, (256, 128)).astype(bf16)

    def hidden_mix(i):
        rows = block_rows(i)
        for h in range(2):
            base[h, rows, :] = decoder_mix(dq[h, rows, :], dk[...], dv[...])

    def visible_base():
        places = jnp.broadcast_to(vi_ref[...].astype(f32), (8, 256))
        places = jnp.transpose(places)[:, 0:1].astype(jnp.int32)
        positions = lax.broadcasted_iota(jnp.int32, (256, 1024), 1)
        select = jnp.where(positions == places, 1.0, 0.0).astype(bf16)
        chosen = jnp.dot(select, pos[...].reshape(1024, DD), preferred_element_type=f32)
        tokv[...] = chosen + scr[0:1, :]

    ids = lax.broadcasted_iota(jnp.int32, script_ref.shape, 0)
    scripted = jnp.sum(
        jnp.where(ids == si_ref[...], script_ref[...].astype(f32), 0.0), axis=0, keepdims=True
    )
    scr[...] = jnp.broadcast_to(scripted, (8, DD))

    def earlier_heads(j):
        @pl.loop(0, 4)
        def _(i):
            combine(j - 1, i)

        attend_head(j - 2)

    @pl.loop(0, HEADS_OWN)
    def _(j):
        @pl.when(j > 2)
        def _():
            earlier_heads(j)

        w_far(j, 0).wait_recv()
        w_far(j, 1).wait_recv()

        @pl.loop(0, 4)
        def _(i):
            e = near(i)
            s = turn(y, 4 - e)

            @pl.when(j == 0)
            def _():
                @pl.when(i > 0)
                def _():
                    got = a.at[s, c]
                    remote(got, got, ay_s.at[e], ay_r.at[e], mate).wait_recv()
                    remote(got, got, ac_s.at[e], ac_r.at[e], mate).start()

                other = a.at[s, 1 - c]
                remote(other, other, ac_s.at[e], ac_r.at[e], mate).wait_recv()

            product = jnp.dot(a[s].reshape(256, 1536), w[j], preferred_element_type=f32).astype(bf16)
            for core in range(2):
                for image in range(4):
                    first = core * 128 + image * 32
                    rows = pl.ds(aligned(s * 64 + core * 32, 32), 32)
                    cs[j, image, rows, :] = product[first : first + 32]
            hop_copy(j, s).start()
            c_copy(j, s, 1 - way_of(s)).start()

            @pl.when((j == 0) & (i > 0))
            def _():
                combine(0, i - 1)

        @pl.when(j == 0)
        def _():
            combine(0, 3)

        @pl.when(j == 2)
        def _():
            for e in (1, 3, 2):
                got = pos.at[turn(y, 4 - e), c]
                remote(got, got, p_s.at[e], p_r.at[e], mate).wait_recv()
                remote(got, got, pc_s.at[e], pc_r.at[e], mate).start()

        @pl.when(j == 2)
        def _():
            earlier_heads(j)

        @pl.when(j + 2 < HEADS_OWN)
        def _():
            w_step(j + 2)

        @pl.when(j == 3)
        def _():
            att_send(0, 2)

        @pl.when(j > 3)
        def _():
            att_send(j - 2, 1)

        @pl.when(j == 3)
        def _():
            fetches[3].wait()
            for e in range(4):
                got = pos.at[turn(y, 4 - e), 1 - c]
                remote(got, got, pc_s.at[e], pc_r.at[e], mate).wait_recv()

        @pl.when((j == 3) | (j == 4))
        def _():
            @pl.loop(0, 2)
            def _(i):
                hidden_heads((j - 3) * 2 + i)

    @pl.loop(0, 2)
    def _(i):
        hidden_mix(i)

    @pl.loop(0, 4)
    def _(i):
        combine(HEADS_OWN - 1, i)

    attend_head(HEADS_OWN - 2)
    att_send(HEADS_OWN - 2, 1)
    fetches[1].wait()
    for d in (1, 3, 2):
        fgain_copy(d).start()
        own_copy(d).start()
        ex_copy(d).start()

    @pl.loop(2, 4)
    def _(i):
        hidden_mix(i)

    visible_base()
    attend_head(HEADS_OWN - 1)
    att_send(HEADS_OWN - 1, 1)
    for d in (1, 3, 2):
        there = turn(z, 4 - d)
        for half in range(2):
            block = wo.at[there, 384 * half : 384 * half + 384]
            remote(block, block, wo_s.at[half, d], wo_r.at[half, d], mate).wait_recv()
    for d in (1, 3, 2):
        whole = att.at[turn(x, 4 - d)]
        remote(whole, whole, t_s.at[d], t_r.at[d], mate).wait_recv()

    def block_at(i):
        return turn(z, 4 - near(i))

    def mate_copy(i):
        there = block_at(i)
        return remote(po.at[there, 1 - c], pr.at[there], m_s.at[i], m_r.at[i], mate)

    def y_ahead(way):
        return turn(y, 1 + 2 * way)

    def half(way):
        return slice(64 * way, 64 * way + 64)

    def y_hop(i, way):
        there = block_at(i)
        return remote(
            po.at[there, c, turn(y, 2), half(way)],
            yhop.at[there, half(way)],
            yh_s.at[way, i],
            yh_r.at[way, i],
            device(x, y_ahead(way), z, c),
        )

    def y_copy(i, way, part):
        there = block_at(i)
        return remote(
            po.at[there, c, y_ahead(way), half(part)],
            yr.at[way, there, half(part)],
            y_s.at[way, i],
            y_r.at[way, i],
            device(x, y_ahead(way), z, c),
        )

    def y_all(i, way):
        there = block_at(i)
        return remote(
            po.at[there, c, y_ahead(way)], yr.at[way, there], y_s.at[way, i], y_r.at[way, i], mate
        )

    def reduce_mate(i):
        there = block_at(i)
        mate_copy(i).wait_recv()
        both = po[there, c].astype(f32) + pr[there].astype(f32)
        po[there, c] = both.astype(bf16)
        for way in range(2):
            y_hop(i, way).start()
            y_copy(i, way, 1 - way).start()

    def reduce_rows(i):
        there = block_at(i)
        for way in range(2):
            y_hop(i, way).wait_recv()
            part = po[there, c, y_ahead(way), half(way)].astype(f32)
            part = part + yhop[there, half(way)].astype(f32)
            po[there, c, y_ahead(way), half(way)] = part.astype(bf16)
            y_copy(i, way, way).start()

    @pl.loop(0, 4)
    def _(i):
        there = block_at(i)

        product = jnp.dot(
            att[...].reshape(1024, 768), wo[there], preferred_element_type=f32
        )
        product = product.astype(bf16)
        for image in range(4):
            for part in range(8):
                first = image * 256 + part * 32
                po[there, part % 2, part // 2, image * 32 : image * 32 + 32, :] = product[
                    first : first + 32
                ]
        mate_copy(i).start()

        @pl.when(i > 0)
        def _():
            reduce_mate(i - 1)

        @pl.when(i > 1)
        def _():
            reduce_rows(i - 2)

    reduce_mate(3)
    reduce_rows(2)
    reduce_rows(3)

    def enc_copy(d):
        return remote(es.at[turn(z, d)], enc_ref.at[:, z], en_s.at[d], en_r.at[d], z_peer(d))

    for d in (1, 3, 2):
        there = turn(z, 4 - d)
        remote(fgains.at[there], fgains.at[there], f_s.at[d], f_r.at[d], mate).wait_recv()
        remote(own.at[there], own.at[there], o_s.at[d], o_r.at[d], mate).wait_recv()
    total, square = 0.0, 0.0
    for i in range(4):
        there = block_at(i)
        y_all(i, 0).wait_recv()
        y_all(i, 1).wait_recv()
        block = own[there].reshape(128, 384).astype(f32) + po[there, c, y].astype(f32)
        block = block + yr[0, there].astype(f32) + yr[1, there].astype(f32)
        res[there] = block
        es[there] = block.astype(bf16).reshape(4, 32, 384)
        total = total + jnp.sum(block, axis=-1, keepdims=True)
        square = square + jnp.sum(block * block, axis=-1, keepdims=True)
    for d in (1, 3, 2):
        ex_got(d).wait_recv()
        ec_copy(d).start()
    average, rate = share_stats(1, total, square)
    for g in range(4):
        block = (res[g] - average) * rate * fgains[g, 0:1, :]
        en[:, 384 * g : 384 * g + 384] = block.astype(bf16)
    for d in (1, 3, 2):
        enc_copy(d).start()
    enc_ref[:, z] = es[z]

    for d in (1, 3, 2):
        ec_got(d).wait_recv()
    product = jnp.dot(en[...], ew[...].reshape(1536, DD), preferred_element_type=f32)
    eo[...] = product.astype(bf16).reshape(4, 32, DD)

    def eb_copy(d):
        return remote(eo.at[turn(x, d)], er.at[d - 1], eb_s.at[d], eb_r.at[d], x_peer(d))

    for d in (1, 3, 2):
        eb_copy(d).start()
    embedded = eo[x].astype(f32)
    for d in (1, 3, 2):
        eb_copy(d).wait_recv()
        embedded = embedded + er[d - 1].astype(f32)
    vis[row] = (embedded + eb_ref[...]).astype(bf16)

    spread_rows(vis.at[row], v_s, v_r, vc_s, vc_r)

    for e in (1, 3, 2):
        got = vis.at[turn(y, 4 - e) * 2 + c]
        remote(got, got, v_s.at[e], v_r.at[e], mate).wait_recv()
        remote(got, got, vc_s.at[e], vc_r.at[e], mate).start()
    for e in range(4):
        got = vis.at[turn(y, 4 - e) * 2 + 1 - c]
        remote(got, got, vc_s.at[e], vc_r.at[e], mate).wait_recv()
    one, two, keys, values = decoder_heads(vis[...].reshape(256, DD).astype(f32) + tokv[...])
    vq[0] = one
    vq[1] = two
    vk[...] = keys
    vv[:, 0:128] = values.astype(bf16)
    vv[:, 128:256] = jnp.ones((256, 128), bf16)

    def mix_copy(e, m):
        owner = turn(y, e) * 2 + c + m - 2 * c * m
        block = da.at[:, pl.ds(aligned(row * 128, 128), 128)]
        return remote(dm.at[owner], block, d_s.at[e, m], d_r.at[e, m], row_peer(e, m))

    def mix_got(e, m):
        block = da.at[:, pl.ds(aligned(row_from(e, m) * 128, 128), 128)]
        return remote(block, block, d_s.at[e, m], d_r.at[e, m], mate)

    def finish(both):
        one = both[0][:, 0:128] / both[0][:, 128:256]
        two = both[1][:, 0:128] / both[1][:, 128:256]
        return jnp.where(first_half, one, two).astype(bf16)

    visible = finish(
        [
            decoder_mix(vq[h], dk[...], dv[...]) + decoder_mix(vq[h], vk[...], vv[...])
            for h in range(2)
        ]
    )

    @pl.loop(0, 4)
    def _(i):
        e = near(3 - i)
        there = turn(y, e)
        rows = block_rows(there)
        mixed = finish(
            [base[h, rows, :] + decoder_mix(dq[h, rows, :], vk[...], vv[...]) for h in range(2)]
        )
        placed = jnp.dot(sel[rows, :], visible, preferred_element_type=f32)
        hidden = dv[rows, 128:256].astype(f32) > 0.5
        mixed = jnp.where(hidden, mixed.astype(f32), placed).astype(bf16)
        dm[there * 2] = mixed[0:128]
        dm[there * 2 + 1] = mixed[128:256]

        @pl.when(e > 0)
        def _():
            mix_copy(e, 0).start()

        mix_copy(e, 1).start()

    da[:, pl.ds(aligned(row * 128, 128), 128)] = dm[row]
    fetches[4].wait()
    fetches[5].wait()
    for k in range(1, 8):
        mix_got(k // 2, k % 2).wait_recv()
    tokens = tok[pl.ds(aligned(c * 128, 128), 128), :] + jnp.dot(
        sel[pl.ds(aligned(row * 128, 128), 128), :],
        vis[...].reshape(256, DD),
        preferred_element_type=f32,
    )
    decoded = tokens + jnp.dot(da[...], dow[...], preferred_element_type=f32)
    normed = norm(decoded, hg_ref[...]).astype(bf16)
    predicted = jnp.dot(normed, pxw[...], preferred_element_type=f32) + pb_ref[...].reshape(1, 768)
    pred_ref[0] = predicted.astype(bf16)

    for d in range(1, 4):
        block = enc_ref.at[:, turn(z, 4 - d)]
        remote(block, block, en_s.at[d], en_r.at[d], mate).wait_recv()
        enc_copy(d).wait_send()
        gain_copy(d).wait_send()
        raw_copy(d).wait_send()
        own_copy(d).wait_send()
        fgain_copy(d).wait_send()
        wo_copy(d, 0).wait_send()
        wo_copy(d, 1).wait_send()
        stat_copy(0, d, z).wait_send()
        stat_copy(1, d, x).wait_send()
        ex_copy(d).wait_send()
        eb_copy(d).wait_send()
        whole = att.at[x]
        remote(whole, whole, t_s.at[d], t_r.at[d], mate).wait_send()
        ec_copy(d).wait_send()
    for e in range(4):
        for block, s_y, r_y, s_c, r_c in (
            (a, ay_s, ay_r, ac_s, ac_r),
            (pos, p_s, p_r, pc_s, pc_r),
        ):
            if e > 0:
                own = block.at[y, c]
                remote(own, own, s_y.at[e], r_y.at[e], mate).wait_send()
            passed = block.at[turn(y, 4 - e), c]
            remote(passed, passed, s_c.at[e], r_c.at[e], mate).wait_send()
        mate_copy(e).wait_send()
        if e > 0:
            own_rows = vis.at[row]
            remote(own_rows, own_rows, v_s.at[e], v_r.at[e], mate).wait_send()
        passed = vis.at[turn(y, 4 - e) * 2 + c]
        remote(passed, passed, vc_s.at[e], vc_r.at[e], mate).wait_send()
        for way in range(2):
            y_hop(e, way).wait_send()
            y_all(e, way).wait_send()
    for k in range(1, 8):
        mix_copy(k // 2, k % 2).wait_send()

    @pl.loop(0, HEADS_OWN)
    def _(j):
        for way in range(2):
            w_send(j, way).wait_send()
            w_forward(j, way).wait_send()

    @pl.loop(0, HEADS_OWN)
    def _(j):
        for way in range(2):
            c_all(j, way).wait_send()

        @pl.loop(0, 4)
        def _(s):
            hop_copy(j, s).wait_send()


def hand_on(enc_ref, pred_ref, enc_out, pred_out, sems):
    copies = [
        pltpu.make_async_copy(enc_ref, enc_out, sems.at[0]),
        pltpu.make_async_copy(pred_ref, pred_out, sems.at[1]),
    ]
    for copy in copies:
        copy.start()
    for copy in copies:
        copy.wait()


VMEM = pl.BlockSpec(memory_space=pltpu.VMEM)
ANY = pl.BlockSpec(memory_space=pl.ANY)


def local(
    visible_patches,
    input_gain,
    encoder_project,
    query_gain,
    key_gain,
    output_weight,
    final_gain,
    embed_weight,
    embed_bias,
    mask_token,
    position_embed,
    script_table,
    decoder_gain,
    decoder_project,
    decoder_query,
    decoder_key,
    decoder_output,
    head_gain,
    pixel_weight,
    pixel_bias,
    visible_index,
    script_index,
):
    def flat(vector):
        return vector.reshape(1, -1)

    dma = pltpu.SemaphoreType.DMA
    two = [dma((4,)), dma((4,))]
    encoded, predicted = pl.pallas_call(
        kernel,
        out_shape=(
            jax.ShapeDtypeStruct((4, 4, 32, 384), bf16),
            jax.ShapeDtypeStruct((1, 128, 768), bf16),
        ),
        in_specs=[
            VMEM, VMEM, ANY, VMEM, VMEM, ANY, VMEM, ANY, VMEM, VMEM, ANY,
            VMEM, VMEM, ANY, VMEM, VMEM, ANY, VMEM, ANY, VMEM, VMEM, VMEM,
        ],
        out_specs=(VMEM, VMEM),
        scratch_shapes=[
            pltpu.VMEM((4, 8, 384), f32),
            pltpu.VMEM((4, 8, 384), f32),
            pltpu.VMEM((4, 4, 32, 384), bf16),
            pltpu.VMEM((4, 4, 32, 384), bf16),
            pltpu.VMEM((2, 4, 8, 128), f32),
            pltpu.VMEM((4, 2, 128, 1536), bf16),
            pltpu.VMEM((HEADS_OWN, 1536, 384), bf16),
            pltpu.VMEM((4, 768, 384), bf16),
            pltpu.VMEM((HEADS_OWN, 4, 256, 384), bf16),
            pltpu.VMEM((2, HEADS_OWN, 256, 384), bf16),
            pltpu.VMEM((HEADS_OWN, 256, 384), bf16),
            pltpu.VMEM((4, 256, 768), bf16),
            pltpu.VMEM((4, 2, 4, 128, 384), bf16),
            pltpu.VMEM((4, 4, 128, 384), bf16),
            pltpu.VMEM((2, 4, 128, 384), bf16),
            pltpu.VMEM((4, 128, 384), bf16),
            pltpu.VMEM((4, 128, 384), f32),
            pltpu.VMEM((128, 1536), bf16),
            pltpu.VMEM((4, 4, 32, 384), bf16),
            pltpu.VMEM((4, 384, DD), bf16),
            pltpu.VMEM((4, 2, 128, DD), bf16),
            pltpu.VMEM((DD, 384), bf16),
            pltpu.VMEM((DD, DD), bf16),
            pltpu.VMEM((DD, 768), bf16),
            pltpu.VMEM((4, 32, DD), bf16),
            pltpu.VMEM((3, 32, DD), bf16),
            pltpu.VMEM((8, 32, DD), bf16),
            pltpu.VMEM((8, DD), f32),
            pltpu.VMEM((1024, 256), bf16),
            pltpu.VMEM((256, DD), f32),
            pltpu.VMEM((256, DD), f32),
            pltpu.VMEM((2, 1024, 128), bf16),
            pltpu.VMEM((1024, 128), bf16),
            pltpu.VMEM((1024, 256), bf16),
            pltpu.VMEM((2, 1024, 256), f32),
            pltpu.VMEM((2, 256, 128), bf16),
            pltpu.VMEM((256, 128), bf16),
            pltpu.VMEM((256, 256), bf16),
            pltpu.VMEM((8, 128, 128), bf16),
            pltpu.VMEM((128, DD), bf16),
            dma((6,)),
            dma((HEADS_OWN,)),
            *two,
            *two,
            *two,
            *two,
            dma((2, 4)), dma((2, 4)),
            dma((2, 4)), dma((2, 4)),
            *two,
            *two,
            dma((2, HEADS_OWN)), dma((2, HEADS_OWN)),
            dma((2, HEADS_OWN)), dma((2, HEADS_OWN)),
            dma((HEADS_OWN, 4)), dma((HEADS_OWN, 4)),
            dma((2, HEADS_OWN)), dma((2, HEADS_OWN)),
            *two,
            *two,
            *two,
            *two,
            *two,
            *two,
            dma((2, 4)), dma((2, 4)),
            dma((2, 4)), dma((2, 4)),
            *two,
            *two,
            *two,
            *two,
            dma((4, 2)), dma((4, 2)),
        ],
        compiler_params=pltpu.CompilerParams(
            collective_id=0, has_side_effects=True, vmem_limit_bytes=62 << 20
        ),
        name="masked_patches",
    )(
        visible_patches.reshape(4, 4, 32, 384), input_gain, encoder_project, flat(query_gain), flat(key_gain),
        output_weight, final_gain, embed_weight, flat(embed_bias), flat(mask_token),
        position_embed, script_table, flat(decoder_gain), decoder_project, flat(decoder_query),
        flat(decoder_key), decoder_output, flat(head_gain), pixel_weight, pixel_bias,
        visible_index, flat(script_index),
    )
    encoded = encoded.reshape(16, 32, 384)
    return pl.pallas_call(
        hand_on,
        out_shape=(
            jax.ShapeDtypeStruct(encoded.shape, bf16),
            jax.ShapeDtypeStruct(predicted.shape, bf16),
        ),
        in_specs=[ANY, ANY],
        out_specs=(ANY, ANY),
        scratch_shapes=[dma((2,))],
        name="hand_on",
    )(encoded, predicted)


def solution(mesh):
    return jax.shard_map(
        local,
        mesh=mesh,
        in_specs=(
            P(None, "row", "col"),
            P("col"),
            P("col", "row"),
            P(),
            P(),
            P("row", "col"),
            P("col"),
            P("col", None),
            P(),
            P(),
            P("row", None),
            P(),
            P(),
            P(),
            P(),
            P(),
            P(),
            P(),
            P(),
            P(),
            P("col", None),
            P("col"),
        ),
        out_specs=(P(None, "row", "col"), P("col", "row", None)),
        check_vma=False,
    )
```

```python
import jax
import jax.numpy as jnp
from jax import lax
from jax.experimental import pallas as pl
from jax.experimental.pallas import tpu as pltpu
from jax.sharding import PartitionSpec as P

D = 6144
DD = 1024
HEADS_OWN = 6
MESH = pl.DeviceIdType.MESH
bf16 = jnp.bfloat16
f32 = jnp.float32

epsilon = 1e-06
LAST = (((1,), (1,)), ((), ()))


def turn(i, by):
    return lax.rem(i + by, 4)


def near(i):
    return i + (i // 2) * (5 - 2 * i)


def device(x, y, z, c):
    return (y * 2 + c, x * 4 + z)


def remote(src, dst, send_sem, recv_sem, where):
    return pltpu.make_async_remote_copy(
        src_ref=src,
        dst_ref=dst,
        send_sem=send_sem,
        recv_sem=recv_sem,
        device_id=where,
        device_id_type=MESH,
    )


def aligned(index, multiple):
    return pl.multiple_of(index, multiple)


def norm(values, gain_vector):
    amount = values.shape[-1]
    average = jnp.sum(values, axis=-1, keepdims=True) / amount
    spread = jnp.sum(values * values, axis=-1, keepdims=True) / amount - average * average
    return (values - average) * lax.rsqrt(spread + epsilon) * gain_vector


def pair_norm(values, gain_vector):
    first = lax.broadcasted_iota(jnp.int32, values.shape, 1) < 64

    def mean(v):
        one = jnp.sum(jnp.where(first, v, 0.0), axis=-1, keepdims=True)
        two = jnp.sum(jnp.where(first, 0.0, v), axis=-1, keepdims=True)
        return jnp.where(first, one, two) / 64

    average = mean(values)
    spread = mean(values * values) - average * average
    return (values - average) * lax.rsqrt(spread + epsilon) * gain_vector


def attention(queries, keys, values, factor):
    scores = lax.dot_general(queries, keys, LAST, preferred_element_type=f32) * factor
    weights = jnp.exp(scores).astype(bf16)
    totals = jnp.sum(weights.astype(f32), axis=-1, keepdims=True)
    mixture = jnp.dot(weights, values, preferred_element_type=f32)
    return (mixture / totals).astype(bf16)


def kernel(
    x_ref, ig_ref, w_ref, qg_ref, kg_ref, wo_ref, fg_ref, ew_ref, eb_ref, mask_ref, pos_ref,
    script_ref, dg_ref, dp_ref, dqg_ref, dkg_ref, do_ref, hg_ref, pw_ref, pb_ref, vi_ref, si_ref,
    enc_ref, pred_ref,
    gains, fgains, raw, own, stats, a, w, wo, cs, cr, hop, att, po, pr, yr, yhop, res, en, es, ew, pos, dpw, dow, pxw,
    eo, er, vis, scr, sel, tok, tokv, dq, dk, dv, base, vq, vk, vv, dm, da,
    l_s, w_s, g_s, g_r, f_s, f_r, x_s, x_r, o_s, o_r, wo_s, wo_r, st_s, st_r, ay_s, ay_r, ac_s, ac_r, wn_s, wn_r, wf_s, wf_r,
    h_s, h_r, c_s, c_r, t_s, t_r, p_s, p_r, pc_s, pc_r, ex_s, ex_r, ec_s, ec_r,
    m_s, m_r, yh_s, yh_r, y_s, y_r, en_s, en_r, eb_s, eb_r, v_s, v_r, vc_s, vc_r, d_s, d_r,
):
    row, col = lax.axis_index("row"), lax.axis_index("col")
    x, y, z, c = col // 4, row // 2, lax.rem(col, 4), lax.rem(row, 2)
    mate = device(x, y, z, 1 - c)
    right, left = turn(x, 1), turn(x, 3)

    def x_peer(d):
        return device(turn(x, d), y, z, c)

    def y_peer(d):
        return device(x, turn(y, d), z, c)

    def z_peer(d):
        return device(x, y, turn(z, d), c)

    def row_peer(e, m):
        return device(x, turn(y, e), z, c + m - 2 * c * m)

    def row_from(e, m):
        return turn(y, 4 - e) * 2 + c + m - 2 * c * m

    def w_block(j, owner, start, size):
        return w.at[j, pl.ds(aligned(owner * 384 + start, 192), size), :]

    def w_fetch(j):
        return pltpu.make_async_copy(
            w_ref.at[:, pl.ds(aligned(j * 384, 128), 384)], w_block(j, x, 0, 384), w_s.at[j]
        )

    @pl.loop(0, HEADS_OWN)
    def _(j):
        w_fetch(j).start()

    fetches = [
        pltpu.make_async_copy(wo_ref, wo.at[z], l_s.at[0]),
        pltpu.make_async_copy(ew_ref, ew.at[z], l_s.at[1]),
        pltpu.make_async_copy(pos_ref, pos.at[y, c], l_s.at[2]),
        pltpu.make_async_copy(
            dp_ref.at[:, pl.ds(aligned(row * 384, 128), 384)], dpw, l_s.at[3]
        ),
        pltpu.make_async_copy(do_ref, dow, l_s.at[4]),
        pltpu.make_async_copy(pw_ref, pxw, l_s.at[5]),
    ]

    gains[x] = jnp.broadcast_to(ig_ref[...].reshape(1, 384), (8, 384))
    fgains[z] = jnp.broadcast_to(fg_ref[...].reshape(1, 384), (8, 384))

    barrier = pltpu.get_barrier_semaphore()
    peers = (
        [x_peer(d) for d in range(1, 4)]
        + [z_peer(d) for d in range(1, 4)]
        + [row_peer(k // 2, k % 2) for k in range(1, 8)]
    )
    for peer in peers:
        pl.semaphore_signal(barrier, inc=1, device_id=peer, device_id_type=MESH)
    pl.semaphore_wait(barrier, len(peers))

    def raw_copy(d):
        return remote(x_ref.at[turn(x, d)], raw.at[x], x_s.at[d], x_r.at[d], x_peer(d))

    def gain_copy(d):
        return remote(gains.at[x], gains.at[x], g_s.at[d], g_r.at[d], x_peer(d))

    def own_copy(d):
        return remote(x_ref.at[:, turn(z, d)], own.at[z], o_s.at[d], o_r.at[d], z_peer(d))

    def fgain_copy(d):
        return remote(fgains.at[z], fgains.at[z], f_s.at[d], f_r.at[d], z_peer(d))

    def wo_copy(d, half):
        block = wo.at[z, 384 * half : 384 * half + 384]
        return remote(block, block, wo_s.at[half, d], wo_r.at[half, d], z_peer(d))

    for d in (1, 3, 2):
        gain_copy(d).start()
        raw_copy(d).start()
    for fetch in fetches:
        fetch.start()
    raw[x] = x_ref[x]
    own[z] = x_ref[:, z]

    def w_send(j, way):
        block = w_block(j, x, 0, 384)
        target = device(right if way == 0 else left, y, z, c)
        return remote(block, block, wn_s.at[way, j], wn_r.at[way, j], target)

    def w_got(j, way):
        block = w_block(j, left if way == 0 else right, 0, 384)
        return remote(block, block, wn_s.at[way, j], wn_r.at[way, j], mate)

    def w_forward(j, way):
        block = w_block(j, left if way == 0 else right, 192 * way, 192)
        target = device(right if way == 0 else left, y, z, c)
        return remote(block, block, wf_s.at[way, j], wf_r.at[way, j], target)

    def w_far(j, way):
        block = w_block(j, turn(x, 2), 192 * way, 192)
        return remote(block, block, wf_s.at[way, j], wf_r.at[way, j], mate)

    def w_start(j):
        w_fetch(j).wait()
        w_send(j, 0).start()
        w_send(j, 1).start()

    def w_step(j):
        w_got(j, 0).wait_recv()
        w_forward(j, 0).start()
        w_got(j, 1).wait_recv()
        w_forward(j, 1).start()

        @pl.when(j + 3 < HEADS_OWN)
        def _():
            w_start(j + 3)

    w_start(0)
    w_start(1)
    w_start(2)
    fetches[0].wait()
    wo_copy(1, 0).start()
    wo_copy(3, 0).start()

    def stat_copy(n, d, owner):
        block = stats.at[n, owner]
        peer = z_peer(d) if n == 0 else x_peer(d)
        return remote(block, block, st_s.at[n, d], st_r.at[n, d], peer)

    def share_stats(n, total, square):
        lane = lax.broadcasted_iota(jnp.int32, (128, 128), 1)
        me = z if n == 0 else x
        stats[n, me] = jnp.transpose(jnp.where(lane == 0, total, square))[0:8]
        for d in (1, 3, 2):
            stat_copy(n, d, me).start()
        for d in (1, 3, 2):
            stat_copy(n, d, turn(me, 4 - d)).wait_recv()
        sums = jnp.transpose(jnp.sum(stats[n], axis=0))
        average = sums[:, 0:1] / D
        spread = sums[:, 1:2] / D - average * average
        return average, lax.rsqrt(spread + epsilon)

    for d in (1, 3, 2):
        there = turn(x, 4 - d)
        remote(gains.at[there], gains.at[there], g_s.at[d], g_r.at[d], mate).wait_recv()
        remote(raw.at[there], raw.at[there], x_s.at[d], x_r.at[d], mate).wait_recv()
    total, square = 0.0, 0.0
    for g in range(4):
        block = raw[g].reshape(128, 384).astype(f32)
        total = total + jnp.sum(block, axis=-1, keepdims=True)
        square = square + jnp.sum(block * block, axis=-1, keepdims=True)
    average, rate = share_stats(0, total, square)
    for g in range(4):
        block = raw[g].reshape(128, 384).astype(f32)
        block = (block - average) * rate * gains[g, 0:1, :]
        a[y, c, :, 384 * g : 384 * g + 384] = block.astype(bf16)

    def spread_rows(block, s_y, r_y, s_c, r_c):
        for e in (1, 3, 2):
            remote(block, block, s_y.at[e], r_y.at[e], y_peer(e)).start()
        remote(block, block, s_c.at[0], r_c.at[0], mate).start()

    spread_rows(a.at[y, c], ay_s, ay_r, ac_s, ac_r)
    fetches[2].wait()
    spread_rows(pos.at[y, c], p_s, p_r, pc_s, pc_r)
    wo_copy(2, 0).start()
    for d in (1, 3, 2):
        wo_copy(d, 1).start()
    w_step(0)
    w_step(1)

    def way_of(s):
        return s // 2

    def ahead(way):
        return turn(z, 1 + 2 * way)

    def behind(way):
        return turn(z, 3 - 2 * way)

    def piece(s):
        return pl.ds(aligned(s * 64, 64), 64)

    def hop_copy(j, s):
        way = way_of(s)
        return remote(
            cs.at[j, turn(z, 2), piece(s), :],
            hop.at[j, piece(s), :],
            h_s.at[j, s],
            h_r.at[j, s],
            device(x, y, ahead(way), c),
        )

    def c_copy(j, s, way):
        there = ahead(way)
        return remote(
            cs.at[j, there, piece(s), :],
            cr.at[way, j, piece(s), :],
            c_s.at[way, j],
            c_r.at[way, j],
            device(x, y, there, c),
        )

    def c_all(j, way):
        return remote(
            cs.at[j, ahead(way)], cr.at[way, j], c_s.at[way, j], c_r.at[way, j], mate
        )

    def combine(j, i):
        s = turn(y, 4 - near(i))
        way = way_of(s)
        hop_copy(j, s).wait_recv()
        both = cs[j, ahead(way), piece(s), :].astype(f32) + hop[j, piece(s), :].astype(f32)
        cs[j, ahead(way), piece(s), :] = both.astype(bf16)
        c_copy(j, s, way).start()

    def att_send(j, heads):
        block = att.at[x, :, pl.ds(aligned(j * 128, 128), heads * 128)]
        for d in (1, 3, 2):
            remote(block, block, t_s.at[d], t_r.at[d], x_peer(d)).start()

    def attend_head(j):
        c_all(j, 0).wait_recv()
        c_all(j, 1).wait_recv()
        projected = cs[j, z].astype(f32) + cr[0, j].astype(f32) + cr[1, j].astype(f32)
        queries = norm(projected[:, 0:128], qg_ref[...]).astype(bf16)
        keys = norm(projected[:, 128:256], kg_ref[...]).astype(bf16)
        mixed = attention(queries, keys, projected[:, 256:384].astype(bf16), 128 ** (-0.5))
        att[x, :, pl.ds(aligned(j * 128, 128), 128)] = mixed

    def ew_half(owner, half):
        return ew.at[owner, pl.ds(aligned(half * 192, 192), 192), :]

    def ex_copy(d):
        block = ew_half(z, c)
        return remote(block, block, ex_s.at[d], ex_r.at[d], z_peer(d))

    def ex_got(d):
        block = ew_half(turn(z, 4 - d), c)
        return remote(block, block, ex_s.at[d], ex_r.at[d], mate)

    def ec_copy(d):
        block = ew_half(turn(z, 4 - d), c)
        return remote(block, block, ec_s.at[d], ec_r.at[d], mate)

    def ec_got(d):
        block = ew_half(turn(z, 4 - d), 1 - c)
        return remote(block, block, ec_s.at[d], ec_r.at[d], mate)

    first_half = lax.broadcasted_iota(jnp.int32, (256, 128), 1) < 64

    def decoder_heads(tokens):
        normed = norm(tokens, dg_ref[...]).astype(bf16)
        made = jnp.dot(normed, dpw[...], preferred_element_type=f32)
        queries = jnp.concatenate([made[:, 0:64], made[:, 192:256]], axis=1)
        keys = jnp.concatenate([made[:, 64:128], made[:, 256:320]], axis=1)
        values = jnp.concatenate([made[:, 128:192], made[:, 320:384]], axis=1)
        query_gain = jnp.concatenate([dqg_ref[...], dqg_ref[...]], axis=1)
        key_gain = jnp.concatenate([dkg_ref[...], dkg_ref[...]], axis=1)
        queries = pair_norm(queries, query_gain)
        one = jnp.where(first_half, queries, 0.0).astype(bf16)
        two = jnp.where(first_half, 0.0, queries).astype(bf16)
        return one, two, pair_norm(keys, key_gain).astype(bf16), values

    def decoder_mix(queries, keys, values):
        scores = lax.dot_general(queries, keys, LAST, preferred_element_type=f32)
        weights = jnp.exp(scores * 64 ** (-0.5)).astype(bf16)
        return jnp.dot(weights, values, preferred_element_type=f32)

    def block_rows(i):
        return pl.ds(aligned(i * 256, 256), 256)

    def hidden_heads(i):
        rows = block_rows(i)
        positions = lax.broadcasted_iota(jnp.int32, (256, 256), 0) + i * 256
        select = jnp.where(positions == vi_ref[...], 1.0, 0.0)
        sel[rows, :] = select.astype(bf16)
        hidden = 1.0 - jnp.sum(select, axis=1, keepdims=True)
        tokens = hidden * mask_ref[...] + pos[i].reshape(256, DD).astype(f32) + scr[0:1, :]

        @pl.when(i == y)
        def _():
            tok[...] = tokens

        one, two, keys, values = decoder_heads(tokens)
        dq[0, rows, :] = one
        dq[1, rows, :] = two
        dk[rows, :] = keys
        dv[rows, 0:128] = (values * hidden).astype(bf16)
        dv[rows, 128:256] = jnp.broadcast_to(hidden, (256, 128)).astype(bf16)

    def hidden_mix(i):
        rows = block_rows(i)
        for h in range(2):
            base[h, rows, :] = decoder_mix(dq[h, rows, :], dk[...], dv[...])

    def visible_base():
        places = jnp.broadcast_to(vi_ref[...].astype(f32), (8, 256))
        places = jnp.transpose(places)[:, 0:1].astype(jnp.int32)
        positions = lax.broadcasted_iota(jnp.int32, (256, 1024), 1)
        select = jnp.where(positions == places, 1.0, 0.0).astype(bf16)
        chosen = jnp.dot(select, pos[...].reshape(1024, DD), preferred_element_type=f32)
        tokv[...] = chosen + scr[0:1, :]

    ids = lax.broadcasted_iota(jnp.int32, script_ref.shape, 0)
    scripted = jnp.sum(
        jnp.where(ids == si_ref[...], script_ref[...].astype(f32), 0.0), axis=0, keepdims=True
    )
    scr[...] = jnp.broadcast_to(scripted, (8, DD))

    def earlier_heads(j):
        @pl.loop(0, 4)
        def _(i):
            combine(j - 1, i)

        attend_head(j - 2)

    @pl.loop(0, HEADS_OWN)
    def _(j):
        @pl.when(j > 2)
        def _():
            earlier_heads(j)

        w_far(j, 0).wait_recv()
        w_far(j, 1).wait_recv()

        @pl.loop(0, 4)
        def _(i):
            e = near(i)
            s = turn(y, 4 - e)

            @pl.when(j == 0)
            def _():
                @pl.when(i > 0)
                def _():
                    got = a.at[s, c]
                    remote(got, got, ay_s.at[e], ay_r.at[e], mate).wait_recv()
                    remote(got, got, ac_s.at[e], ac_r.at[e], mate).start()

                other = a.at[s, 1 - c]
                remote(other, other, ac_s.at[e], ac_r.at[e], mate).wait_recv()

            product = jnp.dot(a[s].reshape(256, 1536), w[j], preferred_element_type=f32).astype(bf16)
            for core in range(2):
                for image in range(4):
                    first = core * 128 + image * 32
                    rows = pl.ds(aligned(s * 64 + core * 32, 32), 32)
                    cs[j, image, rows, :] = product[first : first + 32]
            hop_copy(j, s).start()
            c_copy(j, s, 1 - way_of(s)).start()

            @pl.when((j == 0) & (i > 0))
            def _():
                combine(0, i - 1)

        @pl.when(j == 0)
        def _():
            combine(0, 3)

        @pl.when(j == 2)
        def _():
            for e in (1, 3, 2):
                got = pos.at[turn(y, 4 - e), c]
                remote(got, got, p_s.at[e], p_r.at[e], mate).wait_recv()
                remote(got, got, pc_s.at[e], pc_r.at[e], mate).start()

        @pl.when(j == 2)
        def _():
            earlier_heads(j)

        @pl.when(j + 2 < HEADS_OWN)
        def _():
            w_step(j + 2)

        @pl.when(j == 3)
        def _():
            att_send(0, 2)

        @pl.when(j > 3)
        def _():
            att_send(j - 2, 1)

        @pl.when(j == 3)
        def _():
            fetches[3].wait()
            for e in range(4):
                got = pos.at[turn(y, 4 - e), 1 - c]
                remote(got, got, pc_s.at[e], pc_r.at[e], mate).wait_recv()

        @pl.when((j == 3) | (j == 4))
        def _():
            @pl.loop(0, 2)
            def _(i):
                hidden_heads((j - 3) * 2 + i)

    @pl.loop(0, 2)
    def _(i):
        hidden_mix(i)

    @pl.loop(0, 4)
    def _(i):
        combine(HEADS_OWN - 1, i)

    attend_head(HEADS_OWN - 2)
    att_send(HEADS_OWN - 2, 1)
    fetches[1].wait()
    for d in (1, 3, 2):
        fgain_copy(d).start()
        own_copy(d).start()
        ex_copy(d).start()

    @pl.loop(2, 4)
    def _(i):
        hidden_mix(i)

    visible_base()
    attend_head(HEADS_OWN - 1)
    att_send(HEADS_OWN - 1, 1)
    for d in (1, 3, 2):
        there = turn(z, 4 - d)
        for half in range(2):
            block = wo.at[there, 384 * half : 384 * half + 384]
            remote(block, block, wo_s.at[half, d], wo_r.at[half, d], mate).wait_recv()
    for d in (1, 3, 2):
        whole = att.at[turn(x, 4 - d)]
        remote(whole, whole, t_s.at[d], t_r.at[d], mate).wait_recv()

    def block_at(i):
        return turn(z, 4 - near(i))

    def mate_copy(i):
        there = block_at(i)
        return remote(po.at[there, 1 - c], pr.at[there], m_s.at[i], m_r.at[i], mate)

    def y_ahead(way):
        return turn(y, 1 + 2 * way)

    def half(way):
        return slice(64 * way, 64 * way + 64)

    def y_hop(i, way):
        there = block_at(i)
        return remote(
            po.at[there, c, turn(y, 2), half(way)],
            yhop.at[there, half(way)],
            yh_s.at[way, i],
            yh_r.at[way, i],
            device(x, y_ahead(way), z, c),
        )

    def y_copy(i, way, part):
        there = block_at(i)
        return remote(
            po.at[there, c, y_ahead(way), half(part)],
            yr.at[way, there, half(part)],
            y_s.at[way, i],
            y_r.at[way, i],
            device(x, y_ahead(way), z, c),
        )

    def y_all(i, way):
        there = block_at(i)
        return remote(
            po.at[there, c, y_ahead(way)], yr.at[way, there], y_s.at[way, i], y_r.at[way, i], mate
        )

    def reduce_mate(i):
        there = block_at(i)
        mate_copy(i).wait_recv()
        both = po[there, c].astype(f32) + pr[there].astype(f32)
        po[there, c] = both.astype(bf16)
        for way in range(2):
            y_hop(i, way).start()
            y_copy(i, way, 1 - way).start()

    def reduce_rows(i):
        there = block_at(i)
        for way in range(2):
            y_hop(i, way).wait_recv()
            part = po[there, c, y_ahead(way), half(way)].astype(f32)
            part = part + yhop[there, half(way)].astype(f32)
            po[there, c, y_ahead(way), half(way)] = part.astype(bf16)
            y_copy(i, way, way).start()

    @pl.loop(0, 4)
    def _(i):
        there = block_at(i)

        product = jnp.dot(
            att[...].reshape(1024, 768), wo[there], preferred_element_type=f32
        )
        product = product.astype(bf16)
        for image in range(4):
            for part in range(8):
                first = image * 256 + part * 32
                po[there, part % 2, part // 2, image * 32 : image * 32 + 32, :] = product[
                    first : first + 32
                ]
        mate_copy(i).start()

        @pl.when(i > 0)
        def _():
            reduce_mate(i - 1)

        @pl.when(i > 1)
        def _():
            reduce_rows(i - 2)

    reduce_mate(3)
    reduce_rows(2)
    reduce_rows(3)

    def enc_copy(d):
        return remote(es.at[turn(z, d)], enc_ref.at[:, z], en_s.at[d], en_r.at[d], z_peer(d))

    for d in (1, 3, 2):
        there = turn(z, 4 - d)
        remote(fgains.at[there], fgains.at[there], f_s.at[d], f_r.at[d], mate).wait_recv()
        remote(own.at[there], own.at[there], o_s.at[d], o_r.at[d], mate).wait_recv()
    total, square = 0.0, 0.0
    for i in range(4):
        there = block_at(i)
        y_all(i, 0).wait_recv()
        y_all(i, 1).wait_recv()
        block = own[there].reshape(128, 384).astype(f32) + po[there, c, y].astype(f32)
        block = block + yr[0, there].astype(f32) + yr[1, there].astype(f32)
        res[there] = block
        es[there] = block.astype(bf16).reshape(4, 32, 384)
        total = total + jnp.sum(block, axis=-1, keepdims=True)
        square = square + jnp.sum(block * block, axis=-1, keepdims=True)
    for d in (1, 3, 2):
        ex_got(d).wait_recv()
        ec_copy(d).start()
    average, rate = share_stats(1, total, square)
    for g in range(4):
        block = (res[g] - average) * rate * fgains[g, 0:1, :]
        en[:, 384 * g : 384 * g + 384] = block.astype(bf16)
    for d in (1, 3, 2):
        enc_copy(d).start()
    enc_ref[:, z] = es[z]

    for d in (1, 3, 2):
        ec_got(d).wait_recv()
    product = jnp.dot(en[...], ew[...].reshape(1536, DD), preferred_element_type=f32)
    eo[...] = product.astype(bf16).reshape(4, 32, DD)

    def eb_copy(d):
        return remote(eo.at[turn(x, d)], er.at[d - 1], eb_s.at[d], eb_r.at[d], x_peer(d))

    for d in (1, 3, 2):
        eb_copy(d).start()
    embedded = eo[x].astype(f32)
    for d in (1, 3, 2):
        eb_copy(d).wait_recv()
        embedded = embedded + er[d - 1].astype(f32)
    vis[row] = (embedded + eb_ref[...]).astype(bf16)

    spread_rows(vis.at[row], v_s, v_r, vc_s, vc_r)

    for e in (1, 3, 2):
        got = vis.at[turn(y, 4 - e) * 2 + c]
        remote(got, got, v_s.at[e], v_r.at[e], mate).wait_recv()
        remote(got, got, vc_s.at[e], vc_r.at[e], mate).start()
    for e in range(4):
        got = vis.at[turn(y, 4 - e) * 2 + 1 - c]
        remote(got, got, vc_s.at[e], vc_r.at[e], mate).wait_recv()
    one, two, keys, values = decoder_heads(vis[...].reshape(256, DD).astype(f32) + tokv[...])
    vq[0] = one
    vq[1] = two
    vk[...] = keys
    vv[:, 0:128] = values.astype(bf16)
    vv[:, 128:256] = jnp.ones((256, 128), bf16)

    def mix_copy(e, m):
        owner = turn(y, e) * 2 + c + m - 2 * c * m
        block = da.at[:, pl.ds(aligned(row * 128, 128), 128)]
        return remote(dm.at[owner], block, d_s.at[e, m], d_r.at[e, m], row_peer(e, m))

    def mix_got(e, m):
        block = da.at[:, pl.ds(aligned(row_from(e, m) * 128, 128), 128)]
        return remote(block, block, d_s.at[e, m], d_r.at[e, m], mate)

    def finish(both):
        one = both[0][:, 0:128] / both[0][:, 128:256]
        two = both[1][:, 0:128] / both[1][:, 128:256]
        return jnp.where(first_half, one, two).astype(bf16)

    visible = finish(
        [
            decoder_mix(vq[h], dk[...], dv[...]) + decoder_mix(vq[h], vk[...], vv[...])
            for h in range(2)
        ]
    )

    @pl.loop(0, 4)
    def _(i):
        e = near(3 - i)
        there = turn(y, e)
        rows = block_rows(there)
        mixed = finish(
            [base[h, rows, :] + decoder_mix(dq[h, rows, :], vk[...], vv[...]) for h in range(2)]
        )
        placed = jnp.dot(sel[rows, :], visible, preferred_element_type=f32)
        hidden = dv[rows, 128:256].astype(f32) > 0.5
        mixed = jnp.where(hidden, mixed.astype(f32), placed).astype(bf16)
        dm[there * 2] = mixed[0:128]
        dm[there * 2 + 1] = mixed[128:256]

        @pl.when(e > 0)
        def _():
            mix_copy(e, 0).start()

        mix_copy(e, 1).start()

    da[:, pl.ds(aligned(row * 128, 128), 128)] = dm[row]
    fetches[4].wait()
    fetches[5].wait()
    for k in range(1, 8):
        mix_got(k // 2, k % 2).wait_recv()
    tokens = tok[pl.ds(aligned(c * 128, 128), 128), :] + jnp.dot(
        sel[pl.ds(aligned(row * 128, 128), 128), :],
        vis[...].reshape(256, DD),
        preferred_element_type=f32,
    )
    decoded = tokens + jnp.dot(da[...], dow[...], preferred_element_type=f32)
    normed = norm(decoded, hg_ref[...]).astype(bf16)
    predicted = jnp.dot(normed, pxw[...], preferred_element_type=f32) + pb_ref[...].reshape(1, 768)
    pred_ref[0] = predicted.astype(bf16)

    for d in range(1, 4):
        block = enc_ref.at[:, turn(z, 4 - d)]
        remote(block, block, en_s.at[d], en_r.at[d], mate).wait_recv()
        enc_copy(d).wait_send()
        gain_copy(d).wait_send()
        raw_copy(d).wait_send()
        own_copy(d).wait_send()
        fgain_copy(d).wait_send()
        wo_copy(d, 0).wait_send()
        wo_copy(d, 1).wait_send()
        stat_copy(0, d, z).wait_send()
        stat_copy(1, d, x).wait_send()
        ex_copy(d).wait_send()
        eb_copy(d).wait_send()
        whole = att.at[x]
        remote(whole, whole, t_s.at[d], t_r.at[d], mate).wait_send()
        ec_copy(d).wait_send()
    for e in range(4):
        for block, s_y, r_y, s_c, r_c in (
            (a, ay_s, ay_r, ac_s, ac_r),
            (pos, p_s, p_r, pc_s, pc_r),
        ):
            if e > 0:
                own = block.at[y, c]
                remote(own, own, s_y.at[e], r_y.at[e], mate).wait_send()
            passed = block.at[turn(y, 4 - e), c]
            remote(passed, passed, s_c.at[e], r_c.at[e], mate).wait_send()
        mate_copy(e).wait_send()
        if e > 0:
            own_rows = vis.at[row]
            remote(own_rows, own_rows, v_s.at[e], v_r.at[e], mate).wait_send()
        passed = vis.at[turn(y, 4 - e) * 2 + c]
        remote(passed, passed, vc_s.at[e], vc_r.at[e], mate).wait_send()
        for way in range(2):
            y_hop(e, way).wait_send()
            y_all(e, way).wait_send()
    for k in range(1, 8):
        mix_copy(k // 2, k % 2).wait_send()

    @pl.loop(0, HEADS_OWN)
    def _(j):
        for way in range(2):
            w_send(j, way).wait_send()
            w_forward(j, way).wait_send()

    @pl.loop(0, HEADS_OWN)
    def _(j):
        for way in range(2):
            c_all(j, way).wait_send()

        @pl.loop(0, 4)
        def _(s):
            hop_copy(j, s).wait_send()


def hand_on(enc_ref, pred_ref, enc_out, pred_out):
    enc_out[...] = enc_ref[...]
    pred_out[...] = pred_ref[...]


VMEM = pl.BlockSpec(memory_space=pltpu.VMEM)
ANY = pl.BlockSpec(memory_space=pl.ANY)


def local(
    visible_patches,
    input_gain,
    encoder_project,
    query_gain,
    key_gain,
    output_weight,
    final_gain,
    embed_weight,
    embed_bias,
    mask_token,
    position_embed,
    script_table,
    decoder_gain,
    decoder_project,
    decoder_query,
    decoder_key,
    decoder_output,
    head_gain,
    pixel_weight,
    pixel_bias,
    visible_index,
    script_index,
):
    def flat(vector):
        return vector.reshape(1, -1)

    dma = pltpu.SemaphoreType.DMA
    two = [dma((4,)), dma((4,))]
    encoded, predicted = pl.pallas_call(
        kernel,
        out_shape=(
            jax.ShapeDtypeStruct((4, 4, 32, 384), bf16),
            jax.ShapeDtypeStruct((1, 128, 768), bf16),
        ),
        in_specs=[
            VMEM, VMEM, ANY, VMEM, VMEM, ANY, VMEM, ANY, VMEM, VMEM, ANY,
            VMEM, VMEM, ANY, VMEM, VMEM, ANY, VMEM, ANY, VMEM, VMEM, VMEM,
        ],
        out_specs=(VMEM, VMEM),
        scratch_shapes=[
            pltpu.VMEM((4, 8, 384), f32),
            pltpu.VMEM((4, 8, 384), f32),
            pltpu.VMEM((4, 4, 32, 384), bf16),
            pltpu.VMEM((4, 4, 32, 384), bf16),
            pltpu.VMEM((2, 4, 8, 128), f32),
            pltpu.VMEM((4, 2, 128, 1536), bf16),
            pltpu.VMEM((HEADS_OWN, 1536, 384), bf16),
            pltpu.VMEM((4, 768, 384), bf16),
            pltpu.VMEM((HEADS_OWN, 4, 256, 384), bf16),
            pltpu.VMEM((2, HEADS_OWN, 256, 384), bf16),
            pltpu.VMEM((HEADS_OWN, 256, 384), bf16),
            pltpu.VMEM((4, 256, 768), bf16),
            pltpu.VMEM((4, 2, 4, 128, 384), bf16),
            pltpu.VMEM((4, 4, 128, 384), bf16),
            pltpu.VMEM((2, 4, 128, 384), bf16),
            pltpu.VMEM((4, 128, 384), bf16),
            pltpu.VMEM((4, 128, 384), f32),
            pltpu.VMEM((128, 1536), bf16),
            pltpu.VMEM((4, 4, 32, 384), bf16),
            pltpu.VMEM((4, 384, DD), bf16),
            pltpu.VMEM((4, 2, 128, DD), bf16),
            pltpu.VMEM((DD, 384), bf16),
            pltpu.VMEM((DD, DD), bf16),
            pltpu.VMEM((DD, 768), bf16),
            pltpu.VMEM((4, 32, DD), bf16),
            pltpu.VMEM((3, 32, DD), bf16),
            pltpu.VMEM((8, 32, DD), bf16),
            pltpu.VMEM((8, DD), f32),
            pltpu.VMEM((1024, 256), bf16),
            pltpu.VMEM((256, DD), f32),
            pltpu.VMEM((256, DD), f32),
            pltpu.VMEM((2, 1024, 128), bf16),
            pltpu.VMEM((1024, 128), bf16),
            pltpu.VMEM((1024, 256), bf16),
            pltpu.VMEM((2, 1024, 256), f32),
            pltpu.VMEM((2, 256, 128), bf16),
            pltpu.VMEM((256, 128), bf16),
            pltpu.VMEM((256, 256), bf16),
            pltpu.VMEM((8, 128, 128), bf16),
            pltpu.VMEM((128, DD), bf16),
            dma((6,)),
            dma((HEADS_OWN,)),
            *two,
            *two,
            *two,
            *two,
            dma((2, 4)), dma((2, 4)),
            dma((2, 4)), dma((2, 4)),
            *two,
            *two,
            dma((2, HEADS_OWN)), dma((2, HEADS_OWN)),
            dma((2, HEADS_OWN)), dma((2, HEADS_OWN)),
            dma((HEADS_OWN, 4)), dma((HEADS_OWN, 4)),
            dma((2, HEADS_OWN)), dma((2, HEADS_OWN)),
            *two,
            *two,
            *two,
            *two,
            *two,
            *two,
            dma((2, 4)), dma((2, 4)),
            dma((2, 4)), dma((2, 4)),
            *two,
            *two,
            *two,
            *two,
            dma((4, 2)), dma((4, 2)),
        ],
        compiler_params=pltpu.CompilerParams(
            collective_id=0, has_side_effects=True, vmem_limit_bytes=62 << 20
        ),
        name="masked_patches",
    )(
        visible_patches.reshape(4, 4, 32, 384), input_gain, encoder_project, flat(query_gain), flat(key_gain),
        output_weight, final_gain, embed_weight, flat(embed_bias), flat(mask_token),
        position_embed, script_table, flat(decoder_gain), decoder_project, flat(decoder_query),
        flat(decoder_key), decoder_output, flat(head_gain), pixel_weight, pixel_bias,
        visible_index, flat(script_index),
    )
    encoded = encoded.reshape(16, 32, 384)
    return pl.pallas_call(
        hand_on,
        out_shape=(
            jax.ShapeDtypeStruct(encoded.shape, bf16),
            jax.ShapeDtypeStruct(predicted.shape, bf16),
        ),
        in_specs=[VMEM, VMEM],
        out_specs=(VMEM, VMEM),
        name="hand_on",
    )(encoded, predicted)


def solution(mesh):
    return jax.shard_map(
        local,
        mesh=mesh,
        in_specs=(
            P(None, "row", "col"),
            P("col"),
            P("col", "row"),
            P(),
            P(),
            P("row", "col"),
            P("col"),
            P("col", None),
            P(),
            P(),
            P("row", None),
            P(),
            P(),
            P(),
            P(),
            P(),
            P(),
            P(),
            P(),
            P(),
            P("col", None),
            P("col"),
        ),
        out_specs=(P(None, "row", "col"), P("col", "row", None)),
        check_vma=False,
    )
```

```python
import jax
import jax.numpy as jnp
from jax import lax
from jax.experimental import pallas as pl
from jax.experimental.pallas import tpu as pltpu
from jax.sharding import PartitionSpec as P

D = 6144
DD = 1024
HEADS_OWN = 6
HEADS_X = 5
MESH = pl.DeviceIdType.MESH
bf16 = jnp.bfloat16
f32 = jnp.float32

epsilon = 1e-06
LAST = (((1,), (1,)), ((), ()))


def turn(i, by):
    return lax.rem(i + by, 4)


def near(i):
    return i + (i // 2) * (5 - 2 * i)


def device(x, y, z, c):
    return (y * 2 + c, x * 4 + z)


def remote(src, dst, send_sem, recv_sem, where):
    return pltpu.make_async_remote_copy(
        src_ref=src,
        dst_ref=dst,
        send_sem=send_sem,
        recv_sem=recv_sem,
        device_id=where,
        device_id_type=MESH,
    )


def aligned(index, multiple):
    return pl.multiple_of(index, multiple)


def norm(values, gain_vector):
    amount = values.shape[-1]
    average = jnp.sum(values, axis=-1, keepdims=True) / amount
    spread = jnp.sum(values * values, axis=-1, keepdims=True) / amount - average * average
    return (values - average) * lax.rsqrt(spread + epsilon) * gain_vector


def pair_norm(values, gain_vector):
    first = lax.broadcasted_iota(jnp.int32, values.shape, 1) < 64

    def mean(v):
        one = jnp.sum(jnp.where(first, v, 0.0), axis=-1, keepdims=True)
        two = jnp.sum(jnp.where(first, 0.0, v), axis=-1, keepdims=True)
        return jnp.where(first, one, two) / 64

    average = mean(values)
    spread = mean(values * values) - average * average
    return (values - average) * lax.rsqrt(spread + epsilon) * gain_vector


def attention(queries, keys, values, factor):
    scores = lax.dot_general(queries, keys, LAST, preferred_element_type=f32) * factor
    weights = jnp.exp(scores).astype(bf16)
    totals = jnp.sum(weights.astype(f32), axis=-1, keepdims=True)
    mixture = jnp.dot(weights, values, preferred_element_type=f32)
    return (mixture / totals).astype(bf16)


def kernel(
    x_ref, ig_ref, w_ref, qg_ref, kg_ref, wo_ref, fg_ref, ew_ref, eb_ref, mask_ref, pos_ref,
    script_ref, dg_ref, dp_ref, dqg_ref, dkg_ref, do_ref, hg_ref, pw_ref, pb_ref, vi_ref, si_ref,
    enc_ref, pred_ref,
    gains, zgains, raw, own, stats, a, a2, w, wz, wo, cs, cr, hop, att, po, pr, yr, yhop, res, en, es, ew, pos, dpw, dow, pxw,
    eo, er, vis, scr, sel, tok, tokv, dq, dk, dv, base, vq, vk, vv, dm, da,
    l_s, w_s, g_s, g_r, f_s, f_r, x_s, x_r, o_s, o_r, wo_s, wo_r, wz_s, wz_r, st_s, st_r, ay_s, ay_r, ac_s, ac_r,
    by_s, by_r, bc_s, bc_r, wn_s, wn_r, wf_s, wf_r,
    h_s, h_r, c_s, c_r, t_s, t_r, p_s, p_r, pc_s, pc_r, ex_s, ex_r, ec_s, ec_r,
    m_s, m_r, yh_s, yh_r, y_s, y_r, en_s, en_r, eb_s, eb_r, v_s, v_r, vc_s, vc_r, d_s, d_r,
):
    row, col = lax.axis_index("row"), lax.axis_index("col")
    x, y, z, c = col // 4, row // 2, lax.rem(col, 4), lax.rem(row, 2)
    mate = device(x, y, z, 1 - c)
    right, left = turn(x, 1), turn(x, 3)

    def x_peer(d):
        return device(turn(x, d), y, z, c)

    def y_peer(d):
        return device(x, turn(y, d), z, c)

    def z_peer(d):
        return device(x, y, turn(z, d), c)

    def row_peer(e, m):
        return device(x, turn(y, e), z, c + m - 2 * c * m)

    def row_from(e, m):
        return turn(y, 4 - e) * 2 + c + m - 2 * c * m

    def w_block(j, owner, start, size):
        return w.at[j, pl.ds(aligned(owner * 384 + start, 192), size), :]

    def w_fetch(j):
        return pltpu.make_async_copy(
            w_ref.at[:, pl.ds(aligned(j * 384, 128), 384)], w_block(j, x, 0, 384), w_s.at[j]
        )

    @pl.loop(0, HEADS_X)
    def _(j):
        w_fetch(j).start()

    fetches = [
        pltpu.make_async_copy(wo_ref, wo.at[z], l_s.at[0]),
        pltpu.make_async_copy(ew_ref, ew.at[z], l_s.at[1]),
        pltpu.make_async_copy(pos_ref, pos.at[y, c], l_s.at[2]),
        pltpu.make_async_copy(
            dp_ref.at[:, pl.ds(aligned(row * 384, 128), 384)], dpw, l_s.at[3]
        ),
        pltpu.make_async_copy(do_ref, dow, l_s.at[4]),
        pltpu.make_async_copy(pw_ref, pxw, l_s.at[5]),
        pltpu.make_async_copy(
            w_ref.at[:, HEADS_X * 384 :], wz.at[pl.ds(aligned(z * 384, 384), 384), :], l_s.at[6]
        ),
    ]

    gains[x] = jnp.broadcast_to(ig_ref[...].reshape(1, 384), (8, 384))
    zgains[z] = jnp.where(
        lax.broadcasted_iota(jnp.int32, (8, 384), 0) == 0,
        fg_ref[...].reshape(1, 384),
        ig_ref[...].reshape(1, 384),
    )

    barrier = pltpu.get_barrier_semaphore()
    peers = (
        [x_peer(d) for d in range(1, 4)]
        + [z_peer(d) for d in range(1, 4)]
        + [row_peer(k // 2, k % 2) for k in range(1, 8)]
    )
    for peer in peers:
        pl.semaphore_signal(barrier, inc=1, device_id=peer, device_id_type=MESH)
    pl.semaphore_wait(barrier, len(peers))

    def raw_copy(d):
        return remote(x_ref.at[turn(x, d)], raw.at[x], x_s.at[d], x_r.at[d], x_peer(d))

    def gain_copy(d):
        return remote(gains.at[x], gains.at[x], g_s.at[d], g_r.at[d], x_peer(d))

    def own_copy(d):
        return remote(x_ref.at[:, turn(z, d)], own.at[z], o_s.at[d], o_r.at[d], z_peer(d))

    def zgain_copy(d):
        return remote(zgains.at[z], zgains.at[z], f_s.at[d], f_r.at[d], z_peer(d))

    def wo_copy(d):
        return remote(wo.at[z], wo.at[z], wo_s.at[d], wo_r.at[d], z_peer(d))

    def wo_got(d):
        block = wo.at[turn(z, 4 - d)]
        return remote(block, block, wo_s.at[d], wo_r.at[d], mate)

    def wz_copy(d):
        block = wz.at[pl.ds(aligned(z * 384, 384), 384), :]
        return remote(block, block, wz_s.at[d], wz_r.at[d], z_peer(d))

    def wz_got(d):
        block = wz.at[pl.ds(aligned(turn(z, 4 - d) * 384, 384), 384), :]
        return remote(block, block, wz_s.at[d], wz_r.at[d], mate)

    for d in (1, 3, 2):
        gain_copy(d).start()
        raw_copy(d).start()
        zgain_copy(d).start()
        own_copy(d).start()
    for fetch in fetches:
        fetch.start()
    raw[x] = x_ref[x]
    own[z] = x_ref[:, z]

    def w_send(j, way):
        block = w_block(j, x, 0, 384)
        target = device(right if way == 0 else left, y, z, c)
        return remote(block, block, wn_s.at[way, j], wn_r.at[way, j], target)

    def w_got(j, way):
        block = w_block(j, left if way == 0 else right, 0, 384)
        return remote(block, block, wn_s.at[way, j], wn_r.at[way, j], mate)

    def w_forward(j, way):
        block = w_block(j, left if way == 0 else right, 192 * way, 192)
        target = device(right if way == 0 else left, y, z, c)
        return remote(block, block, wf_s.at[way, j], wf_r.at[way, j], target)

    def w_far(j, way):
        block = w_block(j, turn(x, 2), 192 * way, 192)
        return remote(block, block, wf_s.at[way, j], wf_r.at[way, j], mate)

    def w_start(j):
        w_fetch(j).wait()
        w_send(j, 0).start()
        w_send(j, 1).start()

    def w_step(j):
        w_got(j, 0).wait_recv()
        w_forward(j, 0).start()
        w_got(j, 1).wait_recv()
        w_forward(j, 1).start()

        @pl.when(j + 3 < HEADS_X)
        def _():
            w_start(j + 3)

    w_start(0)
    w_start(1)
    w_start(2)

    def stat_copy(n, d, owner):
        block = stats.at[n, owner]
        peer = z_peer(d) if n == 0 else x_peer(d)
        return remote(block, block, st_s.at[n, d], st_r.at[n, d], peer)

    def send_stats(n, total, square):
        lane = lax.broadcasted_iota(jnp.int32, (128, 128), 1)
        me = z if n == 0 else x
        stats[n, me] = jnp.transpose(jnp.where(lane == 0, total, square))[0:8]
        for d in (1, 3, 2):
            stat_copy(n, d, me).start()

    def take_stats(n):
        me = z if n == 0 else x
        for d in (1, 3, 2):
            stat_copy(n, d, turn(me, 4 - d)).wait_recv()
        sums = jnp.transpose(jnp.sum(stats[n], axis=0))
        average = sums[:, 0:1] / D
        spread = sums[:, 1:2] / D - average * average
        return average, lax.rsqrt(spread + epsilon)

    for d in (1, 3, 2):
        there = turn(x, 4 - d)
        remote(gains.at[there], gains.at[there], g_s.at[d], g_r.at[d], mate).wait_recv()
        remote(raw.at[there], raw.at[there], x_s.at[d], x_r.at[d], mate).wait_recv()

    def sums_of(blocks):
        total, square = 0.0, 0.0
        for g in range(4):
            block = blocks[g].reshape(128, 384).astype(f32)
            total = total + jnp.sum(block, axis=-1, keepdims=True)
            square = square + jnp.sum(block * block, axis=-1, keepdims=True)
        return total, square

    def input_norm(n, blocks, into, gain_of):
        average, rate = take_stats(n)
        for g in range(4):
            block = blocks[g].reshape(128, 384).astype(f32)
            block = (block - average) * rate * gain_of(g)
            into[y, c, :, 384 * g : 384 * g + 384] = block.astype(bf16)

    send_stats(0, *sums_of(raw))
    input_norm(0, raw, a, lambda g: gains[g, 0:1, :])

    def spread_rows(block, s_y, r_y, s_c, r_c):
        for e in (1, 3, 2):
            remote(block, block, s_y.at[e], r_y.at[e], y_peer(e)).start()
        remote(block, block, s_c.at[0], r_c.at[0], mate).start()

    spread_rows(a.at[y, c], ay_s, ay_r, ac_s, ac_r)
    fetches[2].wait()
    spread_rows(pos.at[y, c], p_s, p_r, pc_s, pc_r)
    fetches[6].wait()
    for d in (1, 3, 2):
        wz_copy(d).start()
    fetches[0].wait()
    wo_copy(1).start()
    wo_copy(3).start()
    for d in (1, 3, 2):
        there = turn(z, 4 - d)
        remote(zgains.at[there], zgains.at[there], f_s.at[d], f_r.at[d], mate).wait_recv()
        remote(own.at[there], own.at[there], o_s.at[d], o_r.at[d], mate).wait_recv()
    send_stats(2, *sums_of(own))
    w_step(0)
    w_step(1)
    input_norm(2, own, a2, lambda g: zgains[g, 1:2, :])
    spread_rows(a2.at[y, c], by_s, by_r, bc_s, bc_r)

    def way_of(s):
        return s // 2

    def ahead(way, last):
        return turn(x if last else z, 1 + 2 * way)

    def owner_at(i, last):
        return device(i, y, z, c) if last else device(x, y, i, c)

    def piece(s):
        return pl.ds(aligned(s * 64, 64), 64)

    def hop_copy(j, s, last=False):
        return remote(
            cs.at[j, turn(x if last else z, 2), piece(s), :],
            hop.at[j, piece(s), :],
            h_s.at[j, s],
            h_r.at[j, s],
            owner_at(ahead(way_of(s), last), last),
        )

    def c_copy(j, s, way, last=False):
        there = ahead(way, last)
        return remote(
            cs.at[j, there, piece(s), :],
            cr.at[way, j, piece(s), :],
            c_s.at[way, j],
            c_r.at[way, j],
            owner_at(there, last),
        )

    def c_all(j, way, last=False):
        return remote(
            cs.at[j, ahead(way, last)], cr.at[way, j], c_s.at[way, j], c_r.at[way, j], mate
        )

    def project(j, s, rows, weight, last=False):
        product = jnp.dot(rows.reshape(256, 1536), weight, preferred_element_type=f32).astype(bf16)
        for core in range(2):
            for image in range(4):
                first = core * 128 + image * 32
                there = pl.ds(aligned(s * 64 + core * 32, 32), 32)
                cs[j, image, there, :] = product[first : first + 32]
        hop_copy(j, s, last).start()
        c_copy(j, s, 1 - way_of(s), last).start()

    def combine(j, i, last=False):
        s = turn(y, 4 - near(i))
        way = way_of(s)
        there = ahead(way, last)
        hop_copy(j, s, last).wait_recv()
        both = cs[j, there, piece(s), :].astype(f32) + hop[j, piece(s), :].astype(f32)
        cs[j, there, piece(s), :] = both.astype(bf16)
        c_copy(j, s, way, last).start()

    def att_send(j, heads):
        block = att.at[x, :, pl.ds(aligned(j * 128, 128), heads * 128)]
        for d in (1, 3, 2):
            remote(block, block, t_s.at[d], t_r.at[d], x_peer(d)).start()

    def attend_head(j, last=False):
        c_all(j, 0, last).wait_recv()
        c_all(j, 1, last).wait_recv()
        projected = cs[j, x if last else z].astype(f32) + cr[0, j].astype(f32) + cr[1, j].astype(f32)
        queries = norm(projected[:, 0:128], qg_ref[...]).astype(bf16)
        keys = norm(projected[:, 128:256], kg_ref[...]).astype(bf16)
        mixed = attention(queries, keys, projected[:, 256:384].astype(bf16), 128 ** (-0.5))
        att[x, :, pl.ds(aligned(j * 128, 128), 128)] = mixed

    def ew_half(owner, half):
        return ew.at[owner, pl.ds(aligned(half * 192, 192), 192), :]

    def ex_copy(d):
        block = ew_half(z, c)
        return remote(block, block, ex_s.at[d], ex_r.at[d], z_peer(d))

    def ex_got(d):
        block = ew_half(turn(z, 4 - d), c)
        return remote(block, block, ex_s.at[d], ex_r.at[d], mate)

    def ec_copy(d):
        block = ew_half(turn(z, 4 - d), c)
        return remote(block, block, ec_s.at[d], ec_r.at[d], mate)

    def ec_got(d):
        block = ew_half(turn(z, 4 - d), 1 - c)
        return remote(block, block, ec_s.at[d], ec_r.at[d], mate)

    first_half = lax.broadcasted_iota(jnp.int32, (256, 128), 1) < 64

    def decoder_heads(tokens):
        normed = norm(tokens, dg_ref[...]).astype(bf16)
        made = jnp.dot(normed, dpw[...], preferred_element_type=f32)
        queries = jnp.concatenate([made[:, 0:64], made[:, 192:256]], axis=1)
        keys = jnp.concatenate([made[:, 64:128], made[:, 256:320]], axis=1)
        values = jnp.concatenate([made[:, 128:192], made[:, 320:384]], axis=1)
        query_gain = jnp.concatenate([dqg_ref[...], dqg_ref[...]], axis=1)
        key_gain = jnp.concatenate([dkg_ref[...], dkg_ref[...]], axis=1)
        queries = pair_norm(queries, query_gain)
        one = jnp.where(first_half, queries, 0.0).astype(bf16)
        two = jnp.where(first_half, 0.0, queries).astype(bf16)
        return one, two, pair_norm(keys, key_gain).astype(bf16), values

    def decoder_mix(queries, keys, values):
        scores = lax.dot_general(queries, keys, LAST, preferred_element_type=f32)
        weights = jnp.exp(scores * 64 ** (-0.5)).astype(bf16)
        return jnp.dot(weights, values, preferred_element_type=f32)

    def block_rows(i):
        return pl.ds(aligned(i * 256, 256), 256)

    def hidden_heads(i):
        rows = block_rows(i)
        positions = lax.broadcasted_iota(jnp.int32, (256, 256), 0) + i * 256
        select = jnp.where(positions == vi_ref[...], 1.0, 0.0)
        sel[rows, :] = select.astype(bf16)
        hidden = 1.0 - jnp.sum(select, axis=1, keepdims=True)
        tokens = hidden * mask_ref[...] + pos[i].reshape(256, DD).astype(f32) + scr[0:1, :]

        @pl.when(i == y)
        def _():
            tok[...] = tokens

        one, two, keys, values = decoder_heads(tokens)
        dq[0, rows, :] = one
        dq[1, rows, :] = two
        dk[rows, :] = keys
        dv[rows, 0:128] = (values * hidden).astype(bf16)
        dv[rows, 128:256] = jnp.broadcast_to(hidden, (256, 128)).astype(bf16)

    def hidden_mix(i):
        rows = block_rows(i)
        for h in range(2):
            base[h, rows, :] = decoder_mix(dq[h, rows, :], dk[...], dv[...])

    def visible_base():
        places = jnp.broadcast_to(vi_ref[...].astype(f32), (8, 256))
        places = jnp.transpose(places)[:, 0:1].astype(jnp.int32)
        positions = lax.broadcasted_iota(jnp.int32, (256, 1024), 1)
        select = jnp.where(positions == places, 1.0, 0.0).astype(bf16)
        chosen = jnp.dot(select, pos[...].reshape(1024, DD), preferred_element_type=f32)
        tokv[...] = chosen + scr[0:1, :]

    ids = lax.broadcasted_iota(jnp.int32, script_ref.shape, 0)
    scripted = jnp.sum(
        jnp.where(ids == si_ref[...], script_ref[...].astype(f32), 0.0), axis=0, keepdims=True
    )
    scr[...] = jnp.broadcast_to(scripted, (8, DD))

    def earlier_heads(j):
        @pl.loop(0, 4)
        def _(i):
            combine(j - 1, i)

        attend_head(j - 2)

    @pl.loop(0, HEADS_X)
    def _(j):
        @pl.when(j > 2)
        def _():
            earlier_heads(j)

        w_far(j, 0).wait_recv()
        w_far(j, 1).wait_recv()

        @pl.loop(0, 4)
        def _(i):
            e = near(i)
            s = turn(y, 4 - e)

            @pl.when(j == 0)
            def _():
                @pl.when(i > 0)
                def _():
                    got = a.at[s, c]
                    remote(got, got, ay_s.at[e], ay_r.at[e], mate).wait_recv()
                    remote(got, got, ac_s.at[e], ac_r.at[e], mate).start()

                other = a.at[s, 1 - c]
                remote(other, other, ac_s.at[e], ac_r.at[e], mate).wait_recv()

            project(j, s, a[s], w[j])

            @pl.when((j == 0) & (i > 0))
            def _():
                combine(0, i - 1)

        @pl.when(j == 0)
        def _():
            combine(0, 3)

        @pl.when(j == 2)
        def _():
            for e in (1, 3, 2):
                got = pos.at[turn(y, 4 - e), c]
                remote(got, got, p_s.at[e], p_r.at[e], mate).wait_recv()
                remote(got, got, pc_s.at[e], pc_r.at[e], mate).start()

        @pl.when(j == 2)
        def _():
            earlier_heads(j)

        @pl.when(j + 2 < HEADS_X)
        def _():
            w_step(j + 2)

        @pl.when(j == 3)
        def _():
            att_send(0, 2)

        @pl.when(j > 3)
        def _():
            att_send(j - 2, 1)

        @pl.when(j == 3)
        def _():
            fetches[3].wait()
            for e in range(4):
                got = pos.at[turn(y, 4 - e), 1 - c]
                remote(got, got, pc_s.at[e], pc_r.at[e], mate).wait_recv()

        @pl.when(j == 3)
        def _():
            @pl.loop(0, 2)
            def _(i):
                hidden_heads(i)

    for e in (1, 3, 2):
        got = a2.at[turn(y, 4 - e), c]
        remote(got, got, by_s.at[e], by_r.at[e], mate).wait_recv()
        remote(got, got, bc_s.at[e], bc_r.at[e], mate).start()
    for d in (1, 3, 2):
        wz_got(d).wait_recv()

    @pl.loop(0, 4)
    def _(i):
        s = turn(y, 4 - near(i))
        other = a2.at[s, 1 - c]
        remote(other, other, bc_s.at[near(i)], bc_r.at[near(i)], mate).wait_recv()
        project(HEADS_X, s, a2[s], wz[...], True)

    @pl.loop(0, 4)
    def _(i):
        combine(HEADS_X - 1, i)

    attend_head(HEADS_X - 2)
    att_send(HEADS_X - 2, 1)

    @pl.loop(0, 4)
    def _(i):
        combine(HEADS_X, i, True)

    wo_copy(2).start()
    fetches[1].wait()
    for d in (1, 3, 2):
        ex_copy(d).start()

    @pl.loop(2, 4)
    def _(i):
        hidden_heads(i)

    attend_head(HEADS_X - 1)
    att_send(HEADS_X - 1, 1)
    attend_head(HEADS_X, True)
    att_send(HEADS_X, 1)
    wo_got(1).wait_recv()
    wo_got(3).wait_recv()
    for d in (1, 3, 2):
        whole = att.at[turn(x, 4 - d)]
        remote(whole, whole, t_s.at[d], t_r.at[d], mate).wait_recv()

    def block_at(i):
        return turn(z, 4 - near(i))

    def mate_copy(i):
        there = block_at(i)
        return remote(po.at[there, 1 - c], pr.at[there], m_s.at[i], m_r.at[i], mate)

    def y_ahead(way):
        return turn(y, 1 + 2 * way)

    def half(way):
        return slice(64 * way, 64 * way + 64)

    def y_hop(i, way):
        there = block_at(i)
        return remote(
            po.at[there, c, turn(y, 2), half(way)],
            yhop.at[there, half(way)],
            yh_s.at[way, i],
            yh_r.at[way, i],
            device(x, y_ahead(way), z, c),
        )

    def y_copy(i, way, part):
        there = block_at(i)
        return remote(
            po.at[there, c, y_ahead(way), half(part)],
            yr.at[way, there, half(part)],
            y_s.at[way, i],
            y_r.at[way, i],
            device(x, y_ahead(way), z, c),
        )

    def y_all(i, way):
        there = block_at(i)
        return remote(
            po.at[there, c, y_ahead(way)], yr.at[way, there], y_s.at[way, i], y_r.at[way, i], mate
        )

    def reduce_mate(i):
        there = block_at(i)
        mate_copy(i).wait_recv()
        both = po[there, c].astype(f32) + pr[there].astype(f32)
        po[there, c] = both.astype(bf16)
        for way in range(2):
            y_hop(i, way).start()
            y_copy(i, way, 1 - way).start()

    def reduce_rows(i):
        there = block_at(i)
        for way in range(2):
            y_hop(i, way).wait_recv()
            part = po[there, c, y_ahead(way), half(way)].astype(f32)
            part = part + yhop[there, half(way)].astype(f32)
            po[there, c, y_ahead(way), half(way)] = part.astype(bf16)
            y_copy(i, way, way).start()

    @pl.loop(0, 4)
    def _(i):
        there = block_at(i)

        @pl.when(i == 3)
        def _():
            wo_got(2).wait_recv()

        product = jnp.dot(
            att[...].reshape(1024, 768), wo[there], preferred_element_type=f32
        )
        product = product.astype(bf16)
        for image in range(4):
            for part in range(8):
                first = image * 256 + part * 32
                po[there, part % 2, part // 2, image * 32 : image * 32 + 32, :] = product[
                    first : first + 32
                ]
        mate_copy(i).start()

        @pl.when(i > 0)
        def _():
            reduce_mate(i - 1)

        @pl.when(i > 1)
        def _():
            reduce_rows(i - 2)

    reduce_mate(3)
    reduce_rows(2)
    reduce_rows(3)

    def enc_copy(d):
        return remote(es.at[turn(z, d)], enc_ref.at[:, z], en_s.at[d], en_r.at[d], z_peer(d))

    @pl.loop(0, 2)
    def _(i):
        hidden_mix(i)

    total, square = 0.0, 0.0
    for i in range(4):
        there = block_at(i)
        y_all(i, 0).wait_recv()
        y_all(i, 1).wait_recv()
        block = own[there].reshape(128, 384).astype(f32) + po[there, c, y].astype(f32)
        block = block + yr[0, there].astype(f32) + yr[1, there].astype(f32)
        res[there] = block
        es[there] = block.astype(bf16).reshape(4, 32, 384)
        total = total + jnp.sum(block, axis=-1, keepdims=True)
        square = square + jnp.sum(block * block, axis=-1, keepdims=True)
    for d in (1, 3, 2):
        ex_got(d).wait_recv()
        ec_copy(d).start()
    send_stats(1, total, square)
    visible_base()
    average, rate = take_stats(1)
    for g in range(4):
        block = (res[g] - average) * rate * zgains[g, 0:1, :]
        en[:, 384 * g : 384 * g + 384] = block.astype(bf16)
    for d in (1, 3, 2):
        enc_copy(d).start()
    enc_ref[:, z] = es[z]

    for d in (1, 3, 2):
        ec_got(d).wait_recv()
    product = jnp.dot(en[...], ew[...].reshape(1536, DD), preferred_element_type=f32)
    eo[...] = product.astype(bf16).reshape(4, 32, DD)

    def eb_copy(d):
        return remote(eo.at[turn(x, d)], er.at[d - 1], eb_s.at[d], eb_r.at[d], x_peer(d))

    for d in (1, 3, 2):
        eb_copy(d).start()
    hidden_mix(2)
    embedded = eo[x].astype(f32)
    for d in (1, 3, 2):
        eb_copy(d).wait_recv()
        embedded = embedded + er[d - 1].astype(f32)
    vis[row] = (embedded + eb_ref[...]).astype(bf16)

    spread_rows(vis.at[row], v_s, v_r, vc_s, vc_r)
    hidden_mix(3)

    for e in (1, 3, 2):
        got = vis.at[turn(y, 4 - e) * 2 + c]
        remote(got, got, v_s.at[e], v_r.at[e], mate).wait_recv()
        remote(got, got, vc_s.at[e], vc_r.at[e], mate).start()
    for e in range(4):
        got = vis.at[turn(y, 4 - e) * 2 + 1 - c]
        remote(got, got, vc_s.at[e], vc_r.at[e], mate).wait_recv()
    one, two, keys, values = decoder_heads(vis[...].reshape(256, DD).astype(f32) + tokv[...])
    vq[0] = one
    vq[1] = two
    vk[...] = keys
    vv[:, 0:128] = values.astype(bf16)
    vv[:, 128:256] = jnp.ones((256, 128), bf16)

    def mix_copy(e, m):
        owner = turn(y, e) * 2 + c + m - 2 * c * m
        block = da.at[:, pl.ds(aligned(row * 128, 128), 128)]
        return remote(dm.at[owner], block, d_s.at[e, m], d_r.at[e, m], row_peer(e, m))

    def mix_got(e, m):
        block = da.at[:, pl.ds(aligned(row_from(e, m) * 128, 128), 128)]
        return remote(block, block, d_s.at[e, m], d_r.at[e, m], mate)

    def finish(both):
        one = both[0][:, 0:128] / both[0][:, 128:256]
        two = both[1][:, 0:128] / both[1][:, 128:256]
        return jnp.where(first_half, one, two).astype(bf16)

    visible = finish(
        [
            decoder_mix(vq[h], dk[...], dv[...]) + decoder_mix(vq[h], vk[...], vv[...])
            for h in range(2)
        ]
    )

    @pl.loop(0, 4)
    def _(i):
        e = near(3 - i)
        there = turn(y, e)
        rows = block_rows(there)
        mixed = finish(
            [base[h, rows, :] + decoder_mix(dq[h, rows, :], vk[...], vv[...]) for h in range(2)]
        )
        placed = jnp.dot(sel[rows, :], visible, preferred_element_type=f32)
        hidden = dv[rows, 128:256].astype(f32) > 0.5
        mixed = jnp.where(hidden, mixed.astype(f32), placed).astype(bf16)
        dm[there * 2] = mixed[0:128]
        dm[there * 2 + 1] = mixed[128:256]

        @pl.when(e > 0)
        def _():
            mix_copy(e, 0).start()

        mix_copy(e, 1).start()

    da[:, pl.ds(aligned(row * 128, 128), 128)] = dm[row]
    fetches[4].wait()
    fetches[5].wait()
    for k in range(1, 8):
        mix_got(k // 2, k % 2).wait_recv()
    tokens = tok[pl.ds(aligned(c * 128, 128), 128), :] + jnp.dot(
        sel[pl.ds(aligned(row * 128, 128), 128), :],
        vis[...].reshape(256, DD),
        preferred_element_type=f32,
    )
    decoded = tokens + jnp.dot(da[...], dow[...], preferred_element_type=f32)
    normed = norm(decoded, hg_ref[...]).astype(bf16)
    predicted = jnp.dot(normed, pxw[...], preferred_element_type=f32) + pb_ref[...].reshape(1, 768)
    pred_ref[0] = predicted.astype(bf16)

    for d in range(1, 4):
        block = enc_ref.at[:, turn(z, 4 - d)]
        remote(block, block, en_s.at[d], en_r.at[d], mate).wait_recv()
        enc_copy(d).wait_send()
        gain_copy(d).wait_send()
        raw_copy(d).wait_send()
        own_copy(d).wait_send()
        zgain_copy(d).wait_send()
        wo_copy(d).wait_send()
        wz_copy(d).wait_send()
        stat_copy(2, d, x).wait_send()
        stat_copy(0, d, z).wait_send()
        stat_copy(1, d, x).wait_send()
        ex_copy(d).wait_send()
        eb_copy(d).wait_send()
        whole = att.at[x]
        remote(whole, whole, t_s.at[d], t_r.at[d], mate).wait_send()
        ec_copy(d).wait_send()
    for e in range(4):
        for block, s_y, r_y, s_c, r_c in (
            (a, ay_s, ay_r, ac_s, ac_r),
            (a2, by_s, by_r, bc_s, bc_r),
            (pos, p_s, p_r, pc_s, pc_r),
        ):
            if e > 0:
                own = block.at[y, c]
                remote(own, own, s_y.at[e], r_y.at[e], mate).wait_send()
            passed = block.at[turn(y, 4 - e), c]
            remote(passed, passed, s_c.at[e], r_c.at[e], mate).wait_send()
        mate_copy(e).wait_send()
        if e > 0:
            own_rows = vis.at[row]
            remote(own_rows, own_rows, v_s.at[e], v_r.at[e], mate).wait_send()
        passed = vis.at[turn(y, 4 - e) * 2 + c]
        remote(passed, passed, vc_s.at[e], vc_r.at[e], mate).wait_send()
        for way in range(2):
            y_hop(e, way).wait_send()
            y_all(e, way).wait_send()
    for k in range(1, 8):
        mix_copy(k // 2, k % 2).wait_send()

    @pl.loop(0, HEADS_X)
    def _(j):
        for way in range(2):
            w_send(j, way).wait_send()
            w_forward(j, way).wait_send()

    @pl.loop(0, HEADS_OWN)
    def _(j):
        for way in range(2):
            c_all(j, way).wait_send()

        @pl.loop(0, 4)
        def _(s):
            hop_copy(j, s).wait_send()


def hand_on(enc_ref, pred_ref, enc_out, pred_out):
    enc_out[...] = enc_ref[...]
    pred_out[...] = pred_ref[...]


VMEM = pl.BlockSpec(memory_space=pltpu.VMEM)
ANY = pl.BlockSpec(memory_space=pl.ANY)


def local(
    visible_patches,
    input_gain,
    encoder_project,
    query_gain,
    key_gain,
    output_weight,
    final_gain,
    embed_weight,
    embed_bias,
    mask_token,
    position_embed,
    script_table,
    decoder_gain,
    decoder_project,
    decoder_query,
    decoder_key,
    decoder_output,
    head_gain,
    pixel_weight,
    pixel_bias,
    visible_index,
    script_index,
):
    def flat(vector):
        return vector.reshape(1, -1)

    dma = pltpu.SemaphoreType.DMA
    two = [dma((4,)), dma((4,))]
    encoded, predicted = pl.pallas_call(
        kernel,
        out_shape=(
            jax.ShapeDtypeStruct((4, 4, 32, 384), bf16),
            jax.ShapeDtypeStruct((1, 128, 768), bf16),
        ),
        in_specs=[
            VMEM, VMEM, ANY, VMEM, VMEM, ANY, VMEM, ANY, VMEM, VMEM, ANY,
            VMEM, VMEM, ANY, VMEM, VMEM, ANY, VMEM, ANY, VMEM, VMEM, VMEM,
        ],
        out_specs=(VMEM, VMEM),
        scratch_shapes=[
            pltpu.VMEM((4, 8, 384), f32),
            pltpu.VMEM((4, 8, 384), f32),
            pltpu.VMEM((4, 4, 32, 384), bf16),
            pltpu.VMEM((4, 4, 32, 384), bf16),
            pltpu.VMEM((3, 4, 8, 128), f32),
            pltpu.VMEM((4, 2, 128, 1536), bf16),
            pltpu.VMEM((4, 2, 128, 1536), bf16),
            pltpu.VMEM((HEADS_X, 1536, 384), bf16),
            pltpu.VMEM((1536, 384), bf16),
            pltpu.VMEM((4, 768, 384), bf16),
            pltpu.VMEM((HEADS_OWN, 4, 256, 384), bf16),
            pltpu.VMEM((2, HEADS_OWN, 256, 384), bf16),
            pltpu.VMEM((HEADS_OWN, 256, 384), bf16),
            pltpu.VMEM((4, 256, 768), bf16),
            pltpu.VMEM((4, 2, 4, 128, 384), bf16),
            pltpu.VMEM((4, 4, 128, 384), bf16),
            pltpu.VMEM((2, 4, 128, 384), bf16),
            pltpu.VMEM((4, 128, 384), bf16),
            pltpu.VMEM((4, 128, 384), f32),
            pltpu.VMEM((128, 1536), bf16),
            pltpu.VMEM((4, 4, 32, 384), bf16),
            pltpu.VMEM((4, 384, DD), bf16),
            pltpu.VMEM((4, 2, 128, DD), bf16),
            pltpu.VMEM((DD, 384), bf16),
            pltpu.VMEM((DD, DD), bf16),
            pltpu.VMEM((DD, 768), bf16),
            pltpu.VMEM((4, 32, DD), bf16),
            pltpu.VMEM((3, 32, DD), bf16),
            pltpu.VMEM((8, 32, DD), bf16),
            pltpu.VMEM((8, DD), f32),
            pltpu.VMEM((1024, 256), bf16),
            pltpu.VMEM((256, DD), f32),
            pltpu.VMEM((256, DD), f32),
            pltpu.VMEM((2, 1024, 128), bf16),
            pltpu.VMEM((1024, 128), bf16),
            pltpu.VMEM((1024, 256), bf16),
            pltpu.VMEM((2, 1024, 256), f32),
            pltpu.VMEM((2, 256, 128), bf16),
            pltpu.VMEM((256, 128), bf16),
            pltpu.VMEM((256, 256), bf16),
            pltpu.VMEM((8, 128, 128), bf16),
            pltpu.VMEM((128, DD), bf16),
            dma((7,)),
            dma((HEADS_X,)),
            *two,
            *two,
            *two,
            *two,
            *two,
            *two,
            dma((3, 4)), dma((3, 4)),
            *two,
            *two,
            *two,
            *two,
            dma((2, HEADS_X)), dma((2, HEADS_X)),
            dma((2, HEADS_X)), dma((2, HEADS_X)),
            dma((HEADS_OWN, 4)), dma((HEADS_OWN, 4)),
            dma((2, HEADS_OWN)), dma((2, HEADS_OWN)),
            *two,
            *two,
            *two,
            *two,
            *two,
            *two,
            dma((2, 4)), dma((2, 4)),
            dma((2, 4)), dma((2, 4)),
            *two,
            *two,
            *two,
            *two,
            dma((4, 2)), dma((4, 2)),
        ],
        compiler_params=pltpu.CompilerParams(
            collective_id=0, has_side_effects=True, vmem_limit_bytes=62 << 20
        ),
        name="masked_patches",
    )(
        visible_patches.reshape(4, 4, 32, 384), input_gain, encoder_project, flat(query_gain), flat(key_gain),
        output_weight, final_gain, embed_weight, flat(embed_bias), flat(mask_token),
        position_embed, script_table, flat(decoder_gain), decoder_project, flat(decoder_query),
        flat(decoder_key), decoder_output, flat(head_gain), pixel_weight, pixel_bias,
        visible_index, flat(script_index),
    )
    encoded = encoded.reshape(16, 32, 384)
    return pl.pallas_call(
        hand_on,
        out_shape=(
            jax.ShapeDtypeStruct(encoded.shape, bf16),
            jax.ShapeDtypeStruct(predicted.shape, bf16),
        ),
        in_specs=[VMEM, VMEM],
        out_specs=(VMEM, VMEM),
        name="hand_on",
    )(encoded, predicted)


def solution(mesh):
    return jax.shard_map(
        local,
        mesh=mesh,
        in_specs=(
            P(None, "row", "col"),
            P("col"),
            P("col", "row"),
            P(),
            P(),
            P("row", "col"),
            P("col"),
            P("col", None),
            P(),
            P(),
            P("row", None),
            P(),
            P(),
            P(),
            P(),
            P(),
            P(),
            P(),
            P(),
            P(),
            P("col", None),
            P("col"),
        ),
        out_specs=(P(None, "row", "col"), P("col", "row", None)),
        check_vma=False,
    )
```

```python
import jax
import jax.numpy as jnp
from jax import lax
from jax.experimental import pallas as pl
from jax.experimental.pallas import tpu as pltpu
from jax.sharding import PartitionSpec as P

D = 6144
DD = 1024
HEADS_OWN = 6
MESH = pl.DeviceIdType.MESH
bf16 = jnp.bfloat16
f32 = jnp.float32

epsilon = 1e-06
LAST = (((1,), (1,)), ((), ()))


def turn(i, by):
    return lax.rem(i + by, 4)


def near(i):
    return i + (i // 2) * (5 - 2 * i)


def device(x, y, z, c):
    return (y * 2 + c, x * 4 + z)


def remote(src, dst, send_sem, recv_sem, where):
    return pltpu.make_async_remote_copy(
        src_ref=src,
        dst_ref=dst,
        send_sem=send_sem,
        recv_sem=recv_sem,
        device_id=where,
        device_id_type=MESH,
    )


def aligned(index, multiple):
    return pl.multiple_of(index, multiple)


def norm(values, gain_vector):
    amount = values.shape[-1]
    average = jnp.sum(values, axis=-1, keepdims=True) / amount
    spread = jnp.sum(values * values, axis=-1, keepdims=True) / amount - average * average
    return (values - average) * lax.rsqrt(spread + epsilon) * gain_vector


def pair_norm(values, gain_vector):
    first = lax.broadcasted_iota(jnp.int32, values.shape, 1) < 64

    def mean(v):
        one = jnp.sum(jnp.where(first, v, 0.0), axis=-1, keepdims=True)
        two = jnp.sum(jnp.where(first, 0.0, v), axis=-1, keepdims=True)
        return jnp.where(first, one, two) / 64

    average = mean(values)
    spread = mean(values * values) - average * average
    return (values - average) * lax.rsqrt(spread + epsilon) * gain_vector


def attention(queries, keys, values, factor):
    scores = lax.dot_general(queries, keys, LAST, preferred_element_type=f32) * factor
    weights = jnp.exp(scores).astype(bf16)
    totals = jnp.sum(weights.astype(f32), axis=-1, keepdims=True)
    mixture = jnp.dot(weights, values, preferred_element_type=f32)
    return (mixture / totals).astype(bf16)


SMALL = (1, 3, 4, 6, 8, 9, 11, 12, 14, 15, 17, 19, 20, 21)


def kernel(*refs):
    operands, outputs, rest = list(refs[:22]), refs[22:24], refs[24:]
    held, sems, rest = rest[: len(SMALL)], rest[len(SMALL)], rest[len(SMALL) + 1 :]
    small = []
    for k, index in enumerate(SMALL):
        small.append(pltpu.make_async_copy(operands[index], held[k], sems.at[k]))
        operands[index] = held[k]
    for copy in small:
        copy.start()
    body(small, *operands, *outputs, *rest)


def body(
    small,
    x_ref, ig_ref, w_ref, qg_ref, kg_ref, wo_ref, fg_ref, ew_ref, eb_ref, mask_ref, pos_ref,
    script_ref, dg_ref, dp_ref, dqg_ref, dkg_ref, do_ref, hg_ref, pw_ref, pb_ref, vi_ref, si_ref,
    enc_ref, pred_ref,
    gains, fgains, raw, own, stats, a, w, wo, cs, cr, hop, att, po, pr, yr, yhop, res, en, es, ew, pos, dpw, dow, pxw,
    eo, er, vis, scr, sel, tok, tokv, dq, dk, dv, base, vq, vk, vv, dm, da, pred,
    l_s, w_s, g_s, g_r, f_s, f_r, x_s, x_r, o_s, o_r, wo_s, wo_r, st_s, st_r, ay_s, ay_r, ac_s, ac_r, wn_s, wn_r, wf_s, wf_r,
    h_s, h_r, c_s, c_r, t_s, t_r, p_s, p_r, pc_s, pc_r, ex_s, ex_r, ec_s, ec_r,
    m_s, m_r, yh_s, yh_r, y_s, y_r, en_s, en_r, eb_s, eb_r, v_s, v_r, vc_s, vc_r, d_s, d_r,
):
    row, col = lax.axis_index("row"), lax.axis_index("col")
    x, y, z, c = col // 4, row // 2, lax.rem(col, 4), lax.rem(row, 2)
    mate = device(x, y, z, 1 - c)
    right, left = turn(x, 1), turn(x, 3)

    def x_peer(d):
        return device(turn(x, d), y, z, c)

    def y_peer(d):
        return device(x, turn(y, d), z, c)

    def z_peer(d):
        return device(x, y, turn(z, d), c)

    def row_peer(e, m):
        return device(x, turn(y, e), z, c + m - 2 * c * m)

    def row_from(e, m):
        return turn(y, 4 - e) * 2 + c + m - 2 * c * m

    def w_block(j, owner, start, size):
        return w.at[j, pl.ds(aligned(owner * 384 + start, 192), size), :]

    def w_fetch(j):
        return pltpu.make_async_copy(
            w_ref.at[:, pl.ds(aligned(j * 384, 128), 384)], w_block(j, x, 0, 384), w_s.at[j]
        )

    @pl.loop(0, HEADS_OWN)
    def _(j):
        w_fetch(j).start()

    fetches = [
        pltpu.make_async_copy(wo_ref, wo.at[z], l_s.at[0]),
        pltpu.make_async_copy(ew_ref, ew.at[z], l_s.at[1]),
        pltpu.make_async_copy(pos_ref, pos.at[y, c], l_s.at[2]),
        pltpu.make_async_copy(
            dp_ref.at[:, pl.ds(aligned(row * 384, 128), 384)], dpw, l_s.at[3]
        ),
        pltpu.make_async_copy(do_ref, dow, l_s.at[4]),
        pltpu.make_async_copy(pw_ref, pxw, l_s.at[5]),
    ]

    barrier = pltpu.get_barrier_semaphore()
    peers = (
        [x_peer(d) for d in range(1, 4)]
        + [z_peer(d) for d in range(1, 4)]
        + [row_peer(k // 2, k % 2) for k in range(1, 8)]
    )
    for peer in peers:
        pl.semaphore_signal(barrier, inc=1, device_id=peer, device_id_type=MESH)
    mine = [
        pltpu.make_async_copy(x_ref.at[x], raw.at[x], l_s.at[6]),
        pltpu.make_async_copy(x_ref.at[:, z], own.at[z], l_s.at[7]),
    ]
    for copy in mine:
        copy.start()
    for copy in small:
        copy.wait()
    gains[x] = jnp.broadcast_to(ig_ref[...].reshape(1, 384), (8, 384))
    fgains[z] = jnp.broadcast_to(fg_ref[...].reshape(1, 384), (8, 384))
    pl.semaphore_wait(barrier, len(peers))

    def raw_copy(d):
        return remote(x_ref.at[turn(x, d)], raw.at[x], x_s.at[d], x_r.at[d], x_peer(d))

    def gain_copy(d):
        return remote(gains.at[x], gains.at[x], g_s.at[d], g_r.at[d], x_peer(d))

    def own_copy(d):
        return remote(x_ref.at[:, turn(z, d)], own.at[z], o_s.at[d], o_r.at[d], z_peer(d))

    def fgain_copy(d):
        return remote(fgains.at[z], fgains.at[z], f_s.at[d], f_r.at[d], z_peer(d))

    def wo_copy(d, half):
        block = wo.at[z, 384 * half : 384 * half + 384]
        return remote(block, block, wo_s.at[half, d], wo_r.at[half, d], z_peer(d))

    for d in (1, 3, 2):
        gain_copy(d).start()
        raw_copy(d).start()
    for fetch in fetches:
        fetch.start()

    def w_send(j, way):
        block = w_block(j, x, 0, 384)
        target = device(right if way == 0 else left, y, z, c)
        return remote(block, block, wn_s.at[way, j], wn_r.at[way, j], target)

    def w_got(j, way):
        block = w_block(j, left if way == 0 else right, 0, 384)
        return remote(block, block, wn_s.at[way, j], wn_r.at[way, j], mate)

    def w_forward(j, way):
        block = w_block(j, left if way == 0 else right, 192 * way, 192)
        target = device(right if way == 0 else left, y, z, c)
        return remote(block, block, wf_s.at[way, j], wf_r.at[way, j], target)

    def w_far(j, way):
        block = w_block(j, turn(x, 2), 192 * way, 192)
        return remote(block, block, wf_s.at[way, j], wf_r.at[way, j], mate)

    def w_start(j):
        w_fetch(j).wait()
        w_send(j, 0).start()
        w_send(j, 1).start()

    def w_step(j):
        w_got(j, 0).wait_recv()
        w_forward(j, 0).start()
        w_got(j, 1).wait_recv()
        w_forward(j, 1).start()

        @pl.when(j + 3 < HEADS_OWN)
        def _():
            w_start(j + 3)

    w_start(0)
    w_start(1)
    w_start(2)
    fetches[0].wait()
    wo_copy(1, 0).start()
    wo_copy(3, 0).start()

    def stat_copy(n, d, owner):
        block = stats.at[n, owner]
        peer = z_peer(d) if n == 0 else x_peer(d)
        return remote(block, block, st_s.at[n, d], st_r.at[n, d], peer)

    def share_stats(n, total, square):
        lane = lax.broadcasted_iota(jnp.int32, (128, 128), 1)
        me = z if n == 0 else x
        stats[n, me] = jnp.transpose(jnp.where(lane == 0, total, square))[0:8]
        for d in (1, 3, 2):
            stat_copy(n, d, me).start()
        for d in (1, 3, 2):
            stat_copy(n, d, turn(me, 4 - d)).wait_recv()
        sums = jnp.transpose(jnp.sum(stats[n], axis=0))
        average = sums[:, 0:1] / D
        spread = sums[:, 1:2] / D - average * average
        return average, lax.rsqrt(spread + epsilon)

    for copy in mine:
        copy.wait()
    for d in (1, 3, 2):
        there = turn(x, 4 - d)
        remote(gains.at[there], gains.at[there], g_s.at[d], g_r.at[d], mate).wait_recv()
        remote(raw.at[there], raw.at[there], x_s.at[d], x_r.at[d], mate).wait_recv()
    total, square = 0.0, 0.0
    for g in range(4):
        block = raw[g].reshape(128, 384).astype(f32)
        total = total + jnp.sum(block, axis=-1, keepdims=True)
        square = square + jnp.sum(block * block, axis=-1, keepdims=True)
    average, rate = share_stats(0, total, square)
    for g in range(4):
        block = raw[g].reshape(128, 384).astype(f32)
        block = (block - average) * rate * gains[g, 0:1, :]
        a[y, c, :, 384 * g : 384 * g + 384] = block.astype(bf16)

    def spread_rows(block, s_y, r_y, s_c, r_c):
        for e in (1, 3, 2):
            remote(block, block, s_y.at[e], r_y.at[e], y_peer(e)).start()
        remote(block, block, s_c.at[0], r_c.at[0], mate).start()

    spread_rows(a.at[y, c], ay_s, ay_r, ac_s, ac_r)
    fetches[2].wait()
    spread_rows(pos.at[y, c], p_s, p_r, pc_s, pc_r)
    wo_copy(2, 0).start()
    for d in (1, 3, 2):
        wo_copy(d, 1).start()
    w_step(0)
    w_step(1)

    def way_of(s):
        return s // 2

    def ahead(way):
        return turn(z, 1 + 2 * way)

    def behind(way):
        return turn(z, 3 - 2 * way)

    def piece(s):
        return pl.ds(aligned(s * 64, 64), 64)

    def hop_copy(j, s):
        way = way_of(s)
        return remote(
            cs.at[j, turn(z, 2), piece(s), :],
            hop.at[j, piece(s), :],
            h_s.at[j, s],
            h_r.at[j, s],
            device(x, y, ahead(way), c),
        )

    def c_copy(j, s, way):
        there = ahead(way)
        return remote(
            cs.at[j, there, piece(s), :],
            cr.at[way, j, piece(s), :],
            c_s.at[way, j],
            c_r.at[way, j],
            device(x, y, there, c),
        )

    def c_all(j, way):
        return remote(
            cs.at[j, ahead(way)], cr.at[way, j], c_s.at[way, j], c_r.at[way, j], mate
        )

    def combine(j, i):
        s = turn(y, 4 - near(i))
        way = way_of(s)
        hop_copy(j, s).wait_recv()
        both = cs[j, ahead(way), piece(s), :].astype(f32) + hop[j, piece(s), :].astype(f32)
        cs[j, ahead(way), piece(s), :] = both.astype(bf16)
        c_copy(j, s, way).start()

    def att_send(j, heads):
        block = att.at[x, :, pl.ds(aligned(j * 128, 128), heads * 128)]
        for d in (1, 3, 2):
            remote(block, block, t_s.at[d], t_r.at[d], x_peer(d)).start()

    def attend_head(j):
        c_all(j, 0).wait_recv()
        c_all(j, 1).wait_recv()
        projected = cs[j, z].astype(f32) + cr[0, j].astype(f32) + cr[1, j].astype(f32)
        queries = norm(projected[:, 0:128], qg_ref[...]).astype(bf16)
        keys = norm(projected[:, 128:256], kg_ref[...]).astype(bf16)
        mixed = attention(queries, keys, projected[:, 256:384].astype(bf16), 128 ** (-0.5))
        att[x, :, pl.ds(aligned(j * 128, 128), 128)] = mixed

    def ew_half(owner, half):
        return ew.at[owner, pl.ds(aligned(half * 192, 192), 192), :]

    def ex_copy(d):
        block = ew_half(z, c)
        return remote(block, block, ex_s.at[d], ex_r.at[d], z_peer(d))

    def ex_got(d):
        block = ew_half(turn(z, 4 - d), c)
        return remote(block, block, ex_s.at[d], ex_r.at[d], mate)

    def ec_copy(d):
        block = ew_half(turn(z, 4 - d), c)
        return remote(block, block, ec_s.at[d], ec_r.at[d], mate)

    def ec_got(d):
        block = ew_half(turn(z, 4 - d), 1 - c)
        return remote(block, block, ec_s.at[d], ec_r.at[d], mate)

    first_half = lax.broadcasted_iota(jnp.int32, (256, 128), 1) < 64

    def decoder_heads(tokens):
        normed = norm(tokens, dg_ref[...]).astype(bf16)
        made = jnp.dot(normed, dpw[...], preferred_element_type=f32)
        queries = jnp.concatenate([made[:, 0:64], made[:, 192:256]], axis=1)
        keys = jnp.concatenate([made[:, 64:128], made[:, 256:320]], axis=1)
        values = jnp.concatenate([made[:, 128:192], made[:, 320:384]], axis=1)
        query_gain = jnp.concatenate([dqg_ref[...], dqg_ref[...]], axis=1)
        key_gain = jnp.concatenate([dkg_ref[...], dkg_ref[...]], axis=1)
        queries = pair_norm(queries, query_gain)
        one = jnp.where(first_half, queries, 0.0).astype(bf16)
        two = jnp.where(first_half, 0.0, queries).astype(bf16)
        return one, two, pair_norm(keys, key_gain).astype(bf16), values

    def decoder_mix(queries, keys, values):
        scores = lax.dot_general(queries, keys, LAST, preferred_element_type=f32)
        weights = jnp.exp(scores * 64 ** (-0.5)).astype(bf16)
        return jnp.dot(weights, values, preferred_element_type=f32)

    def block_rows(i):
        return pl.ds(aligned(i * 256, 256), 256)

    def hidden_heads(i):
        rows = block_rows(i)
        positions = lax.broadcasted_iota(jnp.int32, (256, 256), 0) + i * 256
        select = jnp.where(positions == vi_ref[...], 1.0, 0.0)
        sel[rows, :] = select.astype(bf16)
        hidden = 1.0 - jnp.sum(select, axis=1, keepdims=True)
        tokens = hidden * mask_ref[...] + pos[i].reshape(256, DD).astype(f32) + scr[0:1, :]

        @pl.when(i == y)
        def _():
            tok[...] = tokens

        one, two, keys, values = decoder_heads(tokens)
        dq[0, rows, :] = one
        dq[1, rows, :] = two
        dk[rows, :] = keys
        dv[rows, 0:128] = (values * hidden).astype(bf16)
        dv[rows, 128:256] = jnp.broadcast_to(hidden, (256, 128)).astype(bf16)

    def hidden_mix(i):
        rows = block_rows(i)
        for h in range(2):
            base[h, rows, :] = decoder_mix(dq[h, rows, :], dk[...], dv[...])

    def visible_base():
        places = jnp.broadcast_to(vi_ref[...].astype(f32), (8, 256))
        places = jnp.transpose(places)[:, 0:1].astype(jnp.int32)
        positions = lax.broadcasted_iota(jnp.int32, (256, 1024), 1)
        select = jnp.where(positions == places, 1.0, 0.0).astype(bf16)
        chosen = jnp.dot(select, pos[...].reshape(1024, DD), preferred_element_type=f32)
        tokv[...] = chosen + scr[0:1, :]

    ids = lax.broadcasted_iota(jnp.int32, script_ref.shape, 0)
    scripted = jnp.sum(
        jnp.where(ids == si_ref[...], script_ref[...].astype(f32), 0.0), axis=0, keepdims=True
    )
    scr[...] = jnp.broadcast_to(scripted, (8, DD))

    def earlier_heads(j):
        @pl.loop(0, 4)
        def _(i):
            combine(j - 1, i)

        attend_head(j - 2)

    @pl.loop(0, HEADS_OWN)
    def _(j):
        @pl.when(j > 2)
        def _():
            earlier_heads(j)

        w_far(j, 0).wait_recv()
        w_far(j, 1).wait_recv()

        @pl.when(j + 2 < HEADS_OWN)
        def _():
            w_step(j + 2)

        @pl.loop(0, 4)
        def _(i):
            e = near(i)
            s = turn(y, 4 - e)

            @pl.when(j == 0)
            def _():
                @pl.when(i > 0)
                def _():
                    got = a.at[s, c]
                    remote(got, got, ay_s.at[e], ay_r.at[e], mate).wait_recv()
                    remote(got, got, ac_s.at[e], ac_r.at[e], mate).start()

                other = a.at[s, 1 - c]
                remote(other, other, ac_s.at[e], ac_r.at[e], mate).wait_recv()

            product = jnp.dot(a[s].reshape(256, 1536), w[j], preferred_element_type=f32).astype(bf16)
            for core in range(2):
                for image in range(4):
                    first = core * 128 + image * 32
                    rows = pl.ds(aligned(s * 64 + core * 32, 32), 32)
                    cs[j, image, rows, :] = product[first : first + 32]
            hop_copy(j, s).start()
            c_copy(j, s, 1 - way_of(s)).start()

            @pl.when((j == 0) & (i > 0))
            def _():
                combine(0, i - 1)

        @pl.when(j == 0)
        def _():
            combine(0, 3)

        @pl.when(j == 2)
        def _():
            for e in (1, 3, 2):
                got = pos.at[turn(y, 4 - e), c]
                remote(got, got, p_s.at[e], p_r.at[e], mate).wait_recv()
                remote(got, got, pc_s.at[e], pc_r.at[e], mate).start()

        @pl.when(j == 2)
        def _():
            earlier_heads(j)

        @pl.when(j == 3)
        def _():
            att_send(0, 2)

        @pl.when(j > 3)
        def _():
            att_send(j - 2, 1)

        @pl.when(j == 3)
        def _():
            fetches[3].wait()
            for e in range(4):
                got = pos.at[turn(y, 4 - e), 1 - c]
                remote(got, got, pc_s.at[e], pc_r.at[e], mate).wait_recv()

        @pl.when((j == 3) | (j == 4))
        def _():
            @pl.loop(0, 2)
            def _(i):
                hidden_heads((j - 3) * 2 + i)

    @pl.loop(0, 2)
    def _(i):
        hidden_mix(i)

    @pl.loop(0, 4)
    def _(i):
        combine(HEADS_OWN - 1, i)

    attend_head(HEADS_OWN - 2)
    att_send(HEADS_OWN - 2, 1)
    fetches[1].wait()
    for d in (1, 3, 2):
        fgain_copy(d).start()
        own_copy(d).start()
        ex_copy(d).start()

    @pl.loop(2, 4)
    def _(i):
        hidden_mix(i)

    visible_base()
    attend_head(HEADS_OWN - 1)
    att_send(HEADS_OWN - 1, 1)
    for d in (1, 3, 2):
        there = turn(z, 4 - d)
        for half in range(2):
            block = wo.at[there, 384 * half : 384 * half + 384]
            remote(block, block, wo_s.at[half, d], wo_r.at[half, d], mate).wait_recv()
    for d in (1, 3, 2):
        whole = att.at[turn(x, 4 - d)]
        remote(whole, whole, t_s.at[d], t_r.at[d], mate).wait_recv()

    def block_at(i):
        return turn(z, 4 - near(i))

    def mate_copy(i):
        there = block_at(i)
        return remote(po.at[there, 1 - c], pr.at[there], m_s.at[i], m_r.at[i], mate)

    def y_ahead(way):
        return turn(y, 1 + 2 * way)

    def half(way):
        return slice(64 * way, 64 * way + 64)

    def y_hop(i, way):
        there = block_at(i)
        return remote(
            po.at[there, c, turn(y, 2), half(way)],
            yhop.at[there, half(way)],
            yh_s.at[way, i],
            yh_r.at[way, i],
            device(x, y_ahead(way), z, c),
        )

    def y_copy(i, way, part):
        there = block_at(i)
        return remote(
            po.at[there, c, y_ahead(way), half(part)],
            yr.at[way, there, half(part)],
            y_s.at[way, i],
            y_r.at[way, i],
            device(x, y_ahead(way), z, c),
        )

    def y_all(i, way):
        there = block_at(i)
        return remote(
            po.at[there, c, y_ahead(way)], yr.at[way, there], y_s.at[way, i], y_r.at[way, i], mate
        )

    def reduce_mate(i):
        there = block_at(i)
        mate_copy(i).wait_recv()
        both = po[there, c].astype(f32) + pr[there].astype(f32)
        po[there, c] = both.astype(bf16)
        for way in range(2):
            y_hop(i, way).start()
            y_copy(i, way, 1 - way).start()

    def reduce_rows(i):
        there = block_at(i)
        for way in range(2):
            y_hop(i, way).wait_recv()
            part = po[there, c, y_ahead(way), half(way)].astype(f32)
            part = part + yhop[there, half(way)].astype(f32)
            po[there, c, y_ahead(way), half(way)] = part.astype(bf16)
            y_copy(i, way, way).start()

    @pl.loop(0, 4)
    def _(i):
        there = block_at(i)

        product = jnp.dot(
            att[...].reshape(1024, 768), wo[there], preferred_element_type=f32
        )
        product = product.astype(bf16)
        for image in range(4):
            for part in range(8):
                first = image * 256 + part * 32
                po[there, part % 2, part // 2, image * 32 : image * 32 + 32, :] = product[
                    first : first + 32
                ]
        mate_copy(i).start()

        @pl.when(i > 0)
        def _():
            reduce_mate(i - 1)

        @pl.when(i > 1)
        def _():
            reduce_rows(i - 2)

    reduce_mate(3)
    reduce_rows(2)
    reduce_rows(3)

    def enc_copy(d):
        return remote(es.at[turn(z, d)], enc_ref.at[:, z], en_s.at[d], en_r.at[d], z_peer(d))

    for d in (1, 3, 2):
        there = turn(z, 4 - d)
        remote(fgains.at[there], fgains.at[there], f_s.at[d], f_r.at[d], mate).wait_recv()
        remote(own.at[there], own.at[there], o_s.at[d], o_r.at[d], mate).wait_recv()
    total, square = 0.0, 0.0
    for i in range(4):
        there = block_at(i)
        y_all(i, 0).wait_recv()
        y_all(i, 1).wait_recv()
        block = own[there].reshape(128, 384).astype(f32) + po[there, c, y].astype(f32)
        block = block + yr[0, there].astype(f32) + yr[1, there].astype(f32)
        res[there] = block
        es[there] = block.astype(bf16).reshape(4, 32, 384)
        total = total + jnp.sum(block, axis=-1, keepdims=True)
        square = square + jnp.sum(block * block, axis=-1, keepdims=True)
    for d in (1, 3, 2):
        ex_got(d).wait_recv()
        ec_copy(d).start()
    average, rate = share_stats(1, total, square)
    for g in range(4):
        block = (res[g] - average) * rate * fgains[g, 0:1, :]
        en[:, 384 * g : 384 * g + 384] = block.astype(bf16)
    for d in (1, 3, 2):
        enc_copy(d).start()
    enc_mine = pltpu.make_async_copy(es.at[z], enc_ref.at[:, z], l_s.at[8])
    enc_mine.start()

    for d in (1, 3, 2):
        ec_got(d).wait_recv()
    product = jnp.dot(en[...], ew[...].reshape(1536, DD), preferred_element_type=f32)
    eo[...] = product.astype(bf16).reshape(4, 32, DD)

    def eb_copy(d):
        return remote(eo.at[turn(x, d)], er.at[d - 1], eb_s.at[d], eb_r.at[d], x_peer(d))

    for d in (1, 3, 2):
        eb_copy(d).start()
    embedded = eo[x].astype(f32)
    for d in (1, 3, 2):
        eb_copy(d).wait_recv()
        embedded = embedded + er[d - 1].astype(f32)
    vis[row] = (embedded + eb_ref[...]).astype(bf16)

    spread_rows(vis.at[row], v_s, v_r, vc_s, vc_r)

    for e in (1, 3, 2):
        got = vis.at[turn(y, 4 - e) * 2 + c]
        remote(got, got, v_s.at[e], v_r.at[e], mate).wait_recv()
        remote(got, got, vc_s.at[e], vc_r.at[e], mate).start()
    for e in range(4):
        got = vis.at[turn(y, 4 - e) * 2 + 1 - c]
        remote(got, got, vc_s.at[e], vc_r.at[e], mate).wait_recv()
    one, two, keys, values = decoder_heads(vis[...].reshape(256, DD).astype(f32) + tokv[...])
    vq[0] = one
    vq[1] = two
    vk[...] = keys
    vv[:, 0:128] = values.astype(bf16)
    vv[:, 128:256] = jnp.ones((256, 128), bf16)

    def mix_copy(e, m):
        owner = turn(y, e) * 2 + c + m - 2 * c * m
        block = da.at[:, pl.ds(aligned(row * 128, 128), 128)]
        return remote(dm.at[owner], block, d_s.at[e, m], d_r.at[e, m], row_peer(e, m))

    def mix_got(e, m):
        block = da.at[:, pl.ds(aligned(row_from(e, m) * 128, 128), 128)]
        return remote(block, block, d_s.at[e, m], d_r.at[e, m], mate)

    def finish(both):
        one = both[0][:, 0:128] / both[0][:, 128:256]
        two = both[1][:, 0:128] / both[1][:, 128:256]
        return jnp.where(first_half, one, two).astype(bf16)

    visible = finish(
        [
            decoder_mix(vq[h], dk[...], dv[...]) + decoder_mix(vq[h], vk[...], vv[...])
            for h in range(2)
        ]
    )

    @pl.loop(0, 4)
    def _(i):
        e = near(3 - i)
        there = turn(y, e)
        rows = block_rows(there)
        mixed = finish(
            [base[h, rows, :] + decoder_mix(dq[h, rows, :], vk[...], vv[...]) for h in range(2)]
        )
        placed = jnp.dot(sel[rows, :], visible, preferred_element_type=f32)
        hidden = dv[rows, 128:256].astype(f32) > 0.5
        mixed = jnp.where(hidden, mixed.astype(f32), placed).astype(bf16)
        dm[there * 2] = mixed[0:128]
        dm[there * 2 + 1] = mixed[128:256]

        @pl.when(e > 0)
        def _():
            mix_copy(e, 0).start()

        mix_copy(e, 1).start()

    da[:, pl.ds(aligned(row * 128, 128), 128)] = dm[row]
    fetches[4].wait()
    fetches[5].wait()
    for k in range(1, 8):
        mix_got(k // 2, k % 2).wait_recv()
    tokens = tok[pl.ds(aligned(c * 128, 128), 128), :] + jnp.dot(
        sel[pl.ds(aligned(row * 128, 128), 128), :],
        vis[...].reshape(256, DD),
        preferred_element_type=f32,
    )
    decoded = tokens + jnp.dot(da[...], dow[...], preferred_element_type=f32)
    normed = norm(decoded, hg_ref[...]).astype(bf16)
    predicted = jnp.dot(normed, pxw[...], preferred_element_type=f32) + pb_ref[...].reshape(1, 768)
    pred[...] = predicted.astype(bf16)
    pred_mine = pltpu.make_async_copy(pred, pred_ref.at[0], l_s.at[9])
    pred_mine.start()

    enc_mine.wait()
    for d in range(1, 4):
        block = enc_ref.at[:, turn(z, 4 - d)]
        remote(block, block, en_s.at[d], en_r.at[d], mate).wait_recv()
        enc_copy(d).wait_send()
        gain_copy(d).wait_send()
        raw_copy(d).wait_send()
        own_copy(d).wait_send()
        fgain_copy(d).wait_send()
        wo_copy(d, 0).wait_send()
        wo_copy(d, 1).wait_send()
        stat_copy(0, d, z).wait_send()
        stat_copy(1, d, x).wait_send()
        ex_copy(d).wait_send()
        eb_copy(d).wait_send()
        whole = att.at[x]
        remote(whole, whole, t_s.at[d], t_r.at[d], mate).wait_send()
        ec_copy(d).wait_send()
    for e in range(4):
        for block, s_y, r_y, s_c, r_c in (
            (a, ay_s, ay_r, ac_s, ac_r),
            (pos, p_s, p_r, pc_s, pc_r),
        ):
            if e > 0:
                own = block.at[y, c]
                remote(own, own, s_y.at[e], r_y.at[e], mate).wait_send()
            passed = block.at[turn(y, 4 - e), c]
            remote(passed, passed, s_c.at[e], r_c.at[e], mate).wait_send()
        mate_copy(e).wait_send()
        if e > 0:
            own_rows = vis.at[row]
            remote(own_rows, own_rows, v_s.at[e], v_r.at[e], mate).wait_send()
        passed = vis.at[turn(y, 4 - e) * 2 + c]
        remote(passed, passed, vc_s.at[e], vc_r.at[e], mate).wait_send()
        for way in range(2):
            y_hop(e, way).wait_send()
            y_all(e, way).wait_send()
    for k in range(1, 8):
        mix_copy(k // 2, k % 2).wait_send()

    @pl.loop(0, HEADS_OWN)
    def _(j):
        for way in range(2):
            w_send(j, way).wait_send()
            w_forward(j, way).wait_send()

    @pl.loop(0, HEADS_OWN)
    def _(j):
        for way in range(2):
            c_all(j, way).wait_send()

        @pl.loop(0, 4)
        def _(s):
            hop_copy(j, s).wait_send()
    pred_mine.wait()


def hand_on(enc_ref, pred_ref, enc_out, pred_out):
    enc_out[...] = enc_ref[...]
    pred_out[...] = pred_ref[...]


VMEM = pl.BlockSpec(memory_space=pltpu.VMEM)
ANY = pl.BlockSpec(memory_space=pl.ANY)


def local(
    visible_patches,
    input_gain,
    encoder_project,
    query_gain,
    key_gain,
    output_weight,
    final_gain,
    embed_weight,
    embed_bias,
    mask_token,
    position_embed,
    script_table,
    decoder_gain,
    decoder_project,
    decoder_query,
    decoder_key,
    decoder_output,
    head_gain,
    pixel_weight,
    pixel_bias,
    visible_index,
    script_index,
):
    def flat(vector):
        return vector.reshape(1, -1)

    dma = pltpu.SemaphoreType.DMA
    two = [dma((4,)), dma((4,))]
    operands = (
        visible_patches.reshape(4, 4, 32, 384), input_gain, encoder_project, flat(query_gain), flat(key_gain),
        output_weight, final_gain, embed_weight, flat(embed_bias), flat(mask_token),
        position_embed, script_table, flat(decoder_gain), decoder_project, flat(decoder_query),
        flat(decoder_key), decoder_output, flat(head_gain), pixel_weight, pixel_bias,
        visible_index, flat(script_index),
    )
    encoded, predicted = pl.pallas_call(
        kernel,
        out_shape=(
            jax.ShapeDtypeStruct((4, 4, 32, 384), bf16),
            jax.ShapeDtypeStruct((1, 128, 768), bf16),
        ),
        in_specs=[ANY] * 22,
        out_specs=(ANY, ANY),
        scratch_shapes=[
            *[pltpu.VMEM(operands[index].shape, operands[index].dtype) for index in SMALL],
            dma((len(SMALL),)),
            pltpu.VMEM((4, 8, 384), f32),
            pltpu.VMEM((4, 8, 384), f32),
            pltpu.VMEM((4, 4, 32, 384), bf16),
            pltpu.VMEM((4, 4, 32, 384), bf16),
            pltpu.VMEM((2, 4, 8, 128), f32),
            pltpu.VMEM((4, 2, 128, 1536), bf16),
            pltpu.VMEM((HEADS_OWN, 1536, 384), bf16),
            pltpu.VMEM((4, 768, 384), bf16),
            pltpu.VMEM((HEADS_OWN, 4, 256, 384), bf16),
            pltpu.VMEM((2, HEADS_OWN, 256, 384), bf16),
            pltpu.VMEM((HEADS_OWN, 256, 384), bf16),
            pltpu.VMEM((4, 256, 768), bf16),
            pltpu.VMEM((4, 2, 4, 128, 384), bf16),
            pltpu.VMEM((4, 4, 128, 384), bf16),
            pltpu.VMEM((2, 4, 128, 384), bf16),
            pltpu.VMEM((4, 128, 384), bf16),
            pltpu.VMEM((4, 128, 384), f32),
            pltpu.VMEM((128, 1536), bf16),
            pltpu.VMEM((4, 4, 32, 384), bf16),
            pltpu.VMEM((4, 384, DD), bf16),
            pltpu.VMEM((4, 2, 128, DD), bf16),
            pltpu.VMEM((DD, 384), bf16),
            pltpu.VMEM((DD, DD), bf16),
            pltpu.VMEM((DD, 768), bf16),
            pltpu.VMEM((4, 32, DD), bf16),
            pltpu.VMEM((3, 32, DD), bf16),
            pltpu.VMEM((8, 32, DD), bf16),
            pltpu.VMEM((8, DD), f32),
            pltpu.VMEM((1024, 256), bf16),
            pltpu.VMEM((256, DD), f32),
            pltpu.VMEM((256, DD), f32),
            pltpu.VMEM((2, 1024, 128), bf16),
            pltpu.VMEM((1024, 128), bf16),
            pltpu.VMEM((1024, 256), bf16),
            pltpu.VMEM((2, 1024, 256), f32),
            pltpu.VMEM((2, 256, 128), bf16),
            pltpu.VMEM((256, 128), bf16),
            pltpu.VMEM((256, 256), bf16),
            pltpu.VMEM((8, 128, 128), bf16),
            pltpu.VMEM((128, DD), bf16),
            pltpu.VMEM((128, 768), bf16),
            dma((10,)),
            dma((HEADS_OWN,)),
            *two,
            *two,
            *two,
            *two,
            dma((2, 4)), dma((2, 4)),
            dma((2, 4)), dma((2, 4)),
            *two,
            *two,
            dma((2, HEADS_OWN)), dma((2, HEADS_OWN)),
            dma((2, HEADS_OWN)), dma((2, HEADS_OWN)),
            dma((HEADS_OWN, 4)), dma((HEADS_OWN, 4)),
            dma((2, HEADS_OWN)), dma((2, HEADS_OWN)),
            *two,
            *two,
            *two,
            *two,
            *two,
            *two,
            dma((2, 4)), dma((2, 4)),
            dma((2, 4)), dma((2, 4)),
            *two,
            *two,
            *two,
            *two,
            dma((4, 2)), dma((4, 2)),
        ],
        compiler_params=pltpu.CompilerParams(
            collective_id=0, has_side_effects=True, vmem_limit_bytes=62 << 20
        ),
        name="masked_patches",
    )(*operands)
    encoded = encoded.reshape(16, 32, 384)
    return pl.pallas_call(
        hand_on,
        out_shape=(
            jax.ShapeDtypeStruct(encoded.shape, bf16),
            jax.ShapeDtypeStruct(predicted.shape, bf16),
        ),
        in_specs=[VMEM, VMEM],
        out_specs=(VMEM, VMEM),
        name="hand_on",
    )(encoded, predicted)


def solution(mesh):
    return jax.shard_map(
        local,
        mesh=mesh,
        in_specs=(
            P(None, "row", "col"),
            P("col"),
            P("col", "row"),
            P(),
            P(),
            P("row", "col"),
            P("col"),
            P("col", None),
            P(),
            P(),
            P("row", None),
            P(),
            P(),
            P(),
            P(),
            P(),
            P(),
            P(),
            P(),
            P(),
            P("col", None),
            P("col"),
        ),
        out_specs=(P(None, "row", "col"), P("col", "row", None)),
        check_vma=False,
    )
```

```python
import jax
import jax.numpy as jnp
from jax import lax
from jax.experimental import pallas as pl
from jax.experimental.pallas import tpu as pltpu
from jax.sharding import PartitionSpec as P

D = 6144
DD = 1024
HEADS_OWN = 6
MESH = pl.DeviceIdType.MESH
bf16 = jnp.bfloat16
f32 = jnp.float32

epsilon = 1e-06
LAST = (((1,), (1,)), ((), ()))


def turn(i, by):
    return lax.rem(i + by, 4)


def near(i):
    return i + (i // 2) * (5 - 2 * i)


def device(x, y, z, c):
    return (y * 2 + c, x * 4 + z)


def remote(src, dst, send_sem, recv_sem, where):
    return pltpu.make_async_remote_copy(
        src_ref=src,
        dst_ref=dst,
        send_sem=send_sem,
        recv_sem=recv_sem,
        device_id=where,
        device_id_type=MESH,
    )


def aligned(index, multiple):
    return pl.multiple_of(index, multiple)


def norm(values, gain_vector):
    amount = values.shape[-1]
    average = jnp.sum(values, axis=-1, keepdims=True) / amount
    spread = jnp.sum(values * values, axis=-1, keepdims=True) / amount - average * average
    return (values - average) * lax.rsqrt(spread + epsilon) * gain_vector


def pair_norm(values, gain_vector):
    first = lax.broadcasted_iota(jnp.int32, values.shape, 1) < 64

    def mean(v):
        one = jnp.sum(jnp.where(first, v, 0.0), axis=-1, keepdims=True)
        two = jnp.sum(jnp.where(first, 0.0, v), axis=-1, keepdims=True)
        return jnp.where(first, one, two) / 64

    average = mean(values)
    spread = mean(values * values) - average * average
    return (values - average) * lax.rsqrt(spread + epsilon) * gain_vector


def attention(queries, keys, values, factor):
    scores = lax.dot_general(queries, keys, LAST, preferred_element_type=f32) * factor
    weights = jnp.exp(scores).astype(bf16)
    totals = jnp.sum(weights.astype(f32), axis=-1, keepdims=True)
    mixture = jnp.dot(weights, values, preferred_element_type=f32)
    return (mixture / totals).astype(bf16)


SMALL = (1, 3, 4, 6, 8, 9, 11, 12, 14, 15, 17, 19, 20, 21)


def kernel(*refs):
    operands, outputs, rest = list(refs[:22]), refs[22:24], refs[24:]
    held, sems, rest = rest[: len(SMALL)], rest[len(SMALL)], rest[len(SMALL) + 1 :]
    small = []
    for k, index in enumerate(SMALL):
        small.append(pltpu.make_async_copy(operands[index], held[k], sems.at[k]))
        operands[index] = held[k]
    for copy in small:
        copy.start()
    body(small, *operands, *outputs, *rest)


def body(
    small,
    x_ref, ig_ref, w_ref, qg_ref, kg_ref, wo_ref, fg_ref, ew_ref, eb_ref, mask_ref, pos_ref,
    script_ref, dg_ref, dp_ref, dqg_ref, dkg_ref, do_ref, hg_ref, pw_ref, pb_ref, vi_ref, si_ref,
    enc_ref, pred_ref,
    gains, fgains, raw, own, stats, a, w, wo, cs, cr, hop, att, po, pr, yr, yhop, res, en, es, ew, pos, dpw, dow, pxw,
    eo, er, vis, scr, sel, tok, tokv, dq, dk, dv, base, vq, vk, vv, dm, da, pred,
    l_s, w_s, g_s, g_r, f_s, f_r, x_s, x_r, o_s, o_r, wo_s, wo_r, st_s, st_r, ay_s, ay_r, ac_s, ac_r, wn_s, wn_r, wf_s, wf_r,
    h_s, h_r, c_s, c_r, t_s, t_r, p_s, p_r, pc_s, pc_r, ex_s, ex_r, ec_s, ec_r,
    m_s, m_r, yh_s, yh_r, y_s, y_r, en_s, en_r, eb_s, eb_r, v_s, v_r, vc_s, vc_r, d_s, d_r,
):
    row, col = lax.axis_index("row"), lax.axis_index("col")
    x, y, z, c = col // 4, row // 2, lax.rem(col, 4), lax.rem(row, 2)
    mate = device(x, y, z, 1 - c)
    right, left = turn(x, 1), turn(x, 3)

    def x_peer(d):
        return device(turn(x, d), y, z, c)

    def y_peer(d):
        return device(x, turn(y, d), z, c)

    def z_peer(d):
        return device(x, y, turn(z, d), c)

    def row_peer(e, m):
        return device(x, turn(y, e), z, c + m - 2 * c * m)

    def row_from(e, m):
        return turn(y, 4 - e) * 2 + c + m - 2 * c * m

    def w_block(j, owner, start, size):
        return w.at[j, pl.ds(aligned(owner * 384 + start, 192), size), :]

    def w_fetch(j):
        return pltpu.make_async_copy(
            w_ref.at[:, pl.ds(aligned(j * 384, 128), 384)], w_block(j, x, 0, 384), w_s.at[j]
        )

    @pl.loop(0, HEADS_OWN)
    def _(j):
        w_fetch(j).start()

    fetches = [
        pltpu.make_async_copy(wo_ref, wo.at[z], l_s.at[0]),
        pltpu.make_async_copy(ew_ref, ew.at[z], l_s.at[1]),
        pltpu.make_async_copy(pos_ref, pos.at[y, c], l_s.at[2]),
        pltpu.make_async_copy(
            dp_ref.at[:, pl.ds(aligned(row * 384, 128), 384)], dpw, l_s.at[3]
        ),
        pltpu.make_async_copy(do_ref, dow, l_s.at[4]),
        pltpu.make_async_copy(pw_ref, pxw, l_s.at[5]),
    ]

    barrier = pltpu.get_barrier_semaphore()
    peers = (
        [x_peer(d) for d in range(1, 4)]
        + [z_peer(d) for d in range(1, 4)]
        + [row_peer(k // 2, k % 2) for k in range(1, 8)]
    )
    for peer in peers:
        pl.semaphore_signal(barrier, inc=1, device_id=peer, device_id_type=MESH)
    mine = [
        pltpu.make_async_copy(x_ref.at[x], raw.at[x], l_s.at[6]),
        pltpu.make_async_copy(x_ref.at[:, z], own.at[z], l_s.at[7]),
    ]
    for copy in mine:
        copy.start()
    for copy in small:
        copy.wait()
    gains[x] = jnp.broadcast_to(ig_ref[...].reshape(1, 384), (8, 384))
    fgains[z] = jnp.broadcast_to(fg_ref[...].reshape(1, 384), (8, 384))
    pl.semaphore_wait(barrier, len(peers))

    def raw_copy(d):
        return remote(x_ref.at[turn(x, d)], raw.at[x], x_s.at[d], x_r.at[d], x_peer(d))

    def gain_copy(d):
        return remote(gains.at[x], gains.at[x], g_s.at[d], g_r.at[d], x_peer(d))

    def own_copy(d):
        return remote(x_ref.at[:, turn(z, d)], own.at[z], o_s.at[d], o_r.at[d], z_peer(d))

    def fgain_copy(d):
        return remote(fgains.at[z], fgains.at[z], f_s.at[d], f_r.at[d], z_peer(d))

    def wo_copy(d, half):
        block = wo.at[z, 384 * half : 384 * half + 384]
        return remote(block, block, wo_s.at[half, d], wo_r.at[half, d], z_peer(d))

    for d in (1, 3, 2):
        gain_copy(d).start()
        raw_copy(d).start()
    for fetch in fetches:
        fetch.start()

    def w_send(j, way):
        block = w_block(j, x, 0, 384)
        target = device(right if way == 0 else left, y, z, c)
        return remote(block, block, wn_s.at[way, j], wn_r.at[way, j], target)

    def w_got(j, way):
        block = w_block(j, left if way == 0 else right, 0, 384)
        return remote(block, block, wn_s.at[way, j], wn_r.at[way, j], mate)

    def w_forward(j, way):
        block = w_block(j, left if way == 0 else right, 192 * way, 192)
        target = device(right if way == 0 else left, y, z, c)
        return remote(block, block, wf_s.at[way, j], wf_r.at[way, j], target)

    def w_far(j, way):
        block = w_block(j, turn(x, 2), 192 * way, 192)
        return remote(block, block, wf_s.at[way, j], wf_r.at[way, j], mate)

    def w_start(j):
        w_fetch(j).wait()
        w_send(j, 0).start()
        w_send(j, 1).start()

    def w_step(j):
        w_got(j, 0).wait_recv()
        w_forward(j, 0).start()
        w_got(j, 1).wait_recv()
        w_forward(j, 1).start()

        @pl.when(j + 2 < HEADS_OWN)
        def _():
            w_start(j + 2)

    w_start(0)
    w_start(1)
    fetches[0].wait()
    wo_copy(1, 0).start()
    wo_copy(3, 0).start()

    def stat_copy(n, d, owner):
        block = stats.at[n, owner]
        peer = z_peer(d) if n == 0 else x_peer(d)
        return remote(block, block, st_s.at[n, d], st_r.at[n, d], peer)

    def share_stats(n, total, square):
        lane = lax.broadcasted_iota(jnp.int32, (128, 128), 1)
        me = z if n == 0 else x
        stats[n, me] = jnp.transpose(jnp.where(lane == 0, total, square))[0:8]
        for d in (1, 3, 2):
            stat_copy(n, d, me).start()
        for d in (1, 3, 2):
            stat_copy(n, d, turn(me, 4 - d)).wait_recv()
        sums = jnp.transpose(jnp.sum(stats[n], axis=0))
        average = sums[:, 0:1] / D
        spread = sums[:, 1:2] / D - average * average
        return average, lax.rsqrt(spread + epsilon)

    for copy in mine:
        copy.wait()
    for d in (1, 3, 2):
        there = turn(x, 4 - d)
        remote(gains.at[there], gains.at[there], g_s.at[d], g_r.at[d], mate).wait_recv()
        remote(raw.at[there], raw.at[there], x_s.at[d], x_r.at[d], mate).wait_recv()
    total, square = 0.0, 0.0
    for g in range(4):
        block = raw[g].reshape(128, 384).astype(f32)
        total = total + jnp.sum(block, axis=-1, keepdims=True)
        square = square + jnp.sum(block * block, axis=-1, keepdims=True)
    average, rate = share_stats(0, total, square)
    for g in range(4):
        block = raw[g].reshape(128, 384).astype(f32)
        block = (block - average) * rate * gains[g, 0:1, :]
        a[y, c, :, 384 * g : 384 * g + 384] = block.astype(bf16)

    def spread_rows(block, s_y, r_y, s_c, r_c):
        for e in (1, 3, 2):
            remote(block, block, s_y.at[e], r_y.at[e], y_peer(e)).start()
        remote(block, block, s_c.at[0], r_c.at[0], mate).start()

    spread_rows(a.at[y, c], ay_s, ay_r, ac_s, ac_r)
    fetches[2].wait()
    spread_rows(pos.at[y, c], p_s, p_r, pc_s, pc_r)
    wo_copy(2, 0).start()
    for d in (1, 3, 2):
        wo_copy(d, 1).start()
    w_step(0)
    w_step(1)

    def way_of(s):
        return s // 2

    def ahead(way):
        return turn(z, 1 + 2 * way)

    def behind(way):
        return turn(z, 3 - 2 * way)

    def piece(s):
        return pl.ds(aligned(s * 64, 64), 64)

    def hop_copy(j, s):
        way = way_of(s)
        return remote(
            cs.at[j, turn(z, 2), piece(s), :],
            hop.at[j, piece(s), :],
            h_s.at[j, s],
            h_r.at[j, s],
            device(x, y, ahead(way), c),
        )

    def c_copy(j, s, way):
        there = ahead(way)
        return remote(
            cs.at[j, there, piece(s), :],
            cr.at[way, j, piece(s), :],
            c_s.at[way, j],
            c_r.at[way, j],
            device(x, y, there, c),
        )

    def c_all(j, way):
        return remote(
            cs.at[j, ahead(way)], cr.at[way, j], c_s.at[way, j], c_r.at[way, j], mate
        )

    def combine(j, i):
        s = turn(y, 4 - near(i))
        way = way_of(s)
        hop_copy(j, s).wait_recv()
        both = cs[j, ahead(way), piece(s), :].astype(f32) + hop[j, piece(s), :].astype(f32)
        cs[j, ahead(way), piece(s), :] = both.astype(bf16)
        c_copy(j, s, way).start()

    def att_send(j, heads):
        block = att.at[x, :, pl.ds(aligned(j * 128, 128), heads * 128)]
        for d in (1, 3, 2):
            remote(block, block, t_s.at[d], t_r.at[d], x_peer(d)).start()

    def attend_head(j):
        c_all(j, 0).wait_recv()
        c_all(j, 1).wait_recv()
        projected = cs[j, z].astype(f32) + cr[0, j].astype(f32) + cr[1, j].astype(f32)
        queries = norm(projected[:, 0:128], qg_ref[...]).astype(bf16)
        keys = norm(projected[:, 128:256], kg_ref[...]).astype(bf16)
        mixed = attention(queries, keys, projected[:, 256:384].astype(bf16), 128 ** (-0.5))
        att[x, :, pl.ds(aligned(j * 128, 128), 128)] = mixed

    def ew_half(owner, half):
        return ew.at[owner, pl.ds(aligned(half * 192, 192), 192), :]

    def ex_copy(d):
        block = ew_half(z, c)
        return remote(block, block, ex_s.at[d], ex_r.at[d], z_peer(d))

    def ex_got(d):
        block = ew_half(turn(z, 4 - d), c)
        return remote(block, block, ex_s.at[d], ex_r.at[d], mate)

    def ec_copy(d):
        block = ew_half(turn(z, 4 - d), c)
        return remote(block, block, ec_s.at[d], ec_r.at[d], mate)

    def ec_got(d):
        block = ew_half(turn(z, 4 - d), 1 - c)
        return remote(block, block, ec_s.at[d], ec_r.at[d], mate)

    first_half = lax.broadcasted_iota(jnp.int32, (256, 128), 1) < 64

    def decoder_heads(tokens):
        normed = norm(tokens, dg_ref[...]).astype(bf16)
        made = jnp.dot(normed, dpw[...], preferred_element_type=f32)
        queries = jnp.concatenate([made[:, 0:64], made[:, 192:256]], axis=1)
        keys = jnp.concatenate([made[:, 64:128], made[:, 256:320]], axis=1)
        values = jnp.concatenate([made[:, 128:192], made[:, 320:384]], axis=1)
        query_gain = jnp.concatenate([dqg_ref[...], dqg_ref[...]], axis=1)
        key_gain = jnp.concatenate([dkg_ref[...], dkg_ref[...]], axis=1)
        queries = pair_norm(queries, query_gain)
        one = jnp.where(first_half, queries, 0.0).astype(bf16)
        two = jnp.where(first_half, 0.0, queries).astype(bf16)
        return one, two, pair_norm(keys, key_gain).astype(bf16), values

    def decoder_mix(queries, keys, values):
        scores = lax.dot_general(queries, keys, LAST, preferred_element_type=f32)
        weights = jnp.exp(scores * 64 ** (-0.5)).astype(bf16)
        return jnp.dot(weights, values, preferred_element_type=f32)

    def block_rows(i):
        return pl.ds(aligned(i * 256, 256), 256)

    def hidden_heads(i):
        rows = block_rows(i)
        positions = lax.broadcasted_iota(jnp.int32, (256, 256), 0) + i * 256
        select = jnp.where(positions == vi_ref[...], 1.0, 0.0)
        sel[rows, :] = select.astype(bf16)
        hidden = 1.0 - jnp.sum(select, axis=1, keepdims=True)
        tokens = hidden * mask_ref[...] + pos[i].reshape(256, DD).astype(f32) + scr[0:1, :]

        @pl.when(i == y)
        def _():
            tok[...] = tokens

        one, two, keys, values = decoder_heads(tokens)
        dq[0, rows, :] = one
        dq[1, rows, :] = two
        dk[rows, :] = keys
        dv[rows, 0:128] = (values * hidden).astype(bf16)
        dv[rows, 128:256] = jnp.broadcast_to(hidden, (256, 128)).astype(bf16)

    def hidden_mix(i):
        rows = block_rows(i)
        for h in range(2):
            base[h, rows, :] = decoder_mix(dq[h, rows, :], dk[...], dv[...])

    def visible_base():
        places = jnp.broadcast_to(vi_ref[...].astype(f32), (8, 256))
        places = jnp.transpose(places)[:, 0:1].astype(jnp.int32)
        positions = lax.broadcasted_iota(jnp.int32, (256, 1024), 1)
        select = jnp.where(positions == places, 1.0, 0.0).astype(bf16)
        chosen = jnp.dot(select, pos[...].reshape(1024, DD), preferred_element_type=f32)
        tokv[...] = chosen + scr[0:1, :]

    ids = lax.broadcasted_iota(jnp.int32, script_ref.shape, 0)
    scripted = jnp.sum(
        jnp.where(ids == si_ref[...], script_ref[...].astype(f32), 0.0), axis=0, keepdims=True
    )
    scr[...] = jnp.broadcast_to(scripted, (8, DD))

    def earlier_heads(j):
        @pl.loop(0, 4)
        def _(i):
            combine(j - 1, i)

        attend_head(j - 2)

    @pl.loop(0, HEADS_OWN)
    def _(j):
        @pl.when(j > 2)
        def _():
            earlier_heads(j)

        w_far(j, 0).wait_recv()
        w_far(j, 1).wait_recv()

        @pl.when(j + 2 < HEADS_OWN)
        def _():
            w_step(j + 2)

        @pl.loop(0, 4)
        def _(i):
            e = near(i)
            s = turn(y, 4 - e)

            @pl.when(j == 0)
            def _():
                @pl.when(i > 0)
                def _():
                    got = a.at[s, c]
                    remote(got, got, ay_s.at[e], ay_r.at[e], mate).wait_recv()
                    remote(got, got, ac_s.at[e], ac_r.at[e], mate).start()

                other = a.at[s, 1 - c]
                remote(other, other, ac_s.at[e], ac_r.at[e], mate).wait_recv()

            product = jnp.dot(a[s].reshape(256, 1536), w[j], preferred_element_type=f32).astype(bf16)
            for core in range(2):
                for image in range(4):
                    first = core * 128 + image * 32
                    rows = pl.ds(aligned(s * 64 + core * 32, 32), 32)
                    cs[j, image, rows, :] = product[first : first + 32]
            hop_copy(j, s).start()
            c_copy(j, s, 1 - way_of(s)).start()

            @pl.when((j == 0) & (i > 0))
            def _():
                combine(0, i - 1)

        @pl.when(j == 0)
        def _():
            combine(0, 3)

        @pl.when(j == 2)
        def _():
            for e in (1, 3, 2):
                got = pos.at[turn(y, 4 - e), c]
                remote(got, got, p_s.at[e], p_r.at[e], mate).wait_recv()
                remote(got, got, pc_s.at[e], pc_r.at[e], mate).start()

        @pl.when(j == 2)
        def _():
            earlier_heads(j)

        @pl.when(j == 3)
        def _():
            att_send(0, 2)

        @pl.when(j > 3)
        def _():
            att_send(j - 2, 1)

        @pl.when(j == 3)
        def _():
            fetches[3].wait()
            for e in range(4):
                got = pos.at[turn(y, 4 - e), 1 - c]
                remote(got, got, pc_s.at[e], pc_r.at[e], mate).wait_recv()

        @pl.when((j == 3) | (j == 4))
        def _():
            @pl.loop(0, 2)
            def _(i):
                hidden_heads((j - 3) * 2 + i)

    @pl.loop(0, 2)
    def _(i):
        hidden_mix(i)

    @pl.loop(0, 4)
    def _(i):
        combine(HEADS_OWN - 1, i)

    attend_head(HEADS_OWN - 2)
    att_send(HEADS_OWN - 2, 1)
    fetches[1].wait()
    for d in (1, 3, 2):
        fgain_copy(d).start()
        own_copy(d).start()
        ex_copy(d).start()

    @pl.loop(2, 4)
    def _(i):
        hidden_mix(i)

    visible_base()
    attend_head(HEADS_OWN - 1)
    att_send(HEADS_OWN - 1, 1)
    for d in (1, 3, 2):
        there = turn(z, 4 - d)
        for half in range(2):
            block = wo.at[there, 384 * half : 384 * half + 384]
            remote(block, block, wo_s.at[half, d], wo_r.at[half, d], mate).wait_recv()
    for d in (1, 3, 2):
        whole = att.at[turn(x, 4 - d)]
        remote(whole, whole, t_s.at[d], t_r.at[d], mate).wait_recv()

    def block_at(i):
        return turn(z, 4 - near(i))

    def mate_copy(i):
        there = block_at(i)
        return remote(po.at[there, 1 - c], pr.at[there], m_s.at[i], m_r.at[i], mate)

    def y_ahead(way):
        return turn(y, 1 + 2 * way)

    def half(way):
        return slice(64 * way, 64 * way + 64)

    def y_hop(i, way):
        there = block_at(i)
        return remote(
            po.at[there, c, turn(y, 2), half(way)],
            yhop.at[there, half(way)],
            yh_s.at[way, i],
            yh_r.at[way, i],
            device(x, y_ahead(way), z, c),
        )

    def y_copy(i, way, part):
        there = block_at(i)
        return remote(
            po.at[there, c, y_ahead(way), half(part)],
            yr.at[way, there, half(part)],
            y_s.at[way, i],
            y_r.at[way, i],
            device(x, y_ahead(way), z, c),
        )

    def y_all(i, way):
        there = block_at(i)
        return remote(
            po.at[there, c, y_ahead(way)], yr.at[way, there], y_s.at[way, i], y_r.at[way, i], mate
        )

    def reduce_mate(i):
        there = block_at(i)
        mate_copy(i).wait_recv()
        both = po[there, c].astype(f32) + pr[there].astype(f32)
        po[there, c] = both.astype(bf16)
        for way in range(2):
            y_hop(i, way).start()
            y_copy(i, way, 1 - way).start()

    def reduce_rows(i):
        there = block_at(i)
        for way in range(2):
            y_hop(i, way).wait_recv()
            part = po[there, c, y_ahead(way), half(way)].astype(f32)
            part = part + yhop[there, half(way)].astype(f32)
            po[there, c, y_ahead(way), half(way)] = part.astype(bf16)
            y_copy(i, way, way).start()

    @pl.loop(0, 4)
    def _(i):
        there = block_at(i)

        product = jnp.dot(
            att[...].reshape(1024, 768), wo[there], preferred_element_type=f32
        )
        product = product.astype(bf16)
        for image in range(4):
            for part in range(8):
                first = image * 256 + part * 32
                po[there, part % 2, part // 2, image * 32 : image * 32 + 32, :] = product[
                    first : first + 32
                ]
        mate_copy(i).start()

        @pl.when(i > 0)
        def _():
            reduce_mate(i - 1)

        @pl.when(i > 1)
        def _():
            reduce_rows(i - 2)

    reduce_mate(3)
    reduce_rows(2)
    reduce_rows(3)

    def enc_copy(d):
        return remote(es.at[turn(z, d)], enc_ref.at[:, z], en_s.at[d], en_r.at[d], z_peer(d))

    for d in (1, 3, 2):
        there = turn(z, 4 - d)
        remote(fgains.at[there], fgains.at[there], f_s.at[d], f_r.at[d], mate).wait_recv()
        remote(own.at[there], own.at[there], o_s.at[d], o_r.at[d], mate).wait_recv()
    total, square = 0.0, 0.0
    for i in range(4):
        there = block_at(i)
        y_all(i, 0).wait_recv()
        y_all(i, 1).wait_recv()
        block = own[there].reshape(128, 384).astype(f32) + po[there, c, y].astype(f32)
        block = block + yr[0, there].astype(f32) + yr[1, there].astype(f32)
        res[there] = block
        es[there] = block.astype(bf16).reshape(4, 32, 384)
        total = total + jnp.sum(block, axis=-1, keepdims=True)
        square = square + jnp.sum(block * block, axis=-1, keepdims=True)
    for d in (1, 3, 2):
        ex_got(d).wait_recv()
        ec_copy(d).start()
    average, rate = share_stats(1, total, square)
    for g in range(4):
        block = (res[g] - average) * rate * fgains[g, 0:1, :]
        en[:, 384 * g : 384 * g + 384] = block.astype(bf16)
    for d in (1, 3, 2):
        enc_copy(d).start()
    enc_mine = pltpu.make_async_copy(es.at[z], enc_ref.at[:, z], l_s.at[8])
    enc_mine.start()

    for d in (1, 3, 2):
        ec_got(d).wait_recv()
    product = jnp.dot(en[...], ew[...].reshape(1536, DD), preferred_element_type=f32)
    eo[...] = product.astype(bf16).reshape(4, 32, DD)

    def eb_copy(d):
        return remote(eo.at[turn(x, d)], er.at[d - 1], eb_s.at[d], eb_r.at[d], x_peer(d))

    for d in (1, 3, 2):
        eb_copy(d).start()
    embedded = eo[x].astype(f32)
    for d in (1, 3, 2):
        eb_copy(d).wait_recv()
        embedded = embedded + er[d - 1].astype(f32)
    vis[row] = (embedded + eb_ref[...]).astype(bf16)

    spread_rows(vis.at[row], v_s, v_r, vc_s, vc_r)

    for e in (1, 3, 2):
        got = vis.at[turn(y, 4 - e) * 2 + c]
        remote(got, got, v_s.at[e], v_r.at[e], mate).wait_recv()
        remote(got, got, vc_s.at[e], vc_r.at[e], mate).start()
    for e in range(4):
        got = vis.at[turn(y, 4 - e) * 2 + 1 - c]
        remote(got, got, vc_s.at[e], vc_r.at[e], mate).wait_recv()
    one, two, keys, values = decoder_heads(vis[...].reshape(256, DD).astype(f32) + tokv[...])
    vq[0] = one
    vq[1] = two
    vk[...] = keys
    vv[:, 0:128] = values.astype(bf16)
    vv[:, 128:256] = jnp.ones((256, 128), bf16)

    def mix_copy(e, m):
        owner = turn(y, e) * 2 + c + m - 2 * c * m
        block = da.at[:, pl.ds(aligned(row * 128, 128), 128)]
        return remote(dm.at[owner], block, d_s.at[e, m], d_r.at[e, m], row_peer(e, m))

    def mix_got(e, m):
        block = da.at[:, pl.ds(aligned(row_from(e, m) * 128, 128), 128)]
        return remote(block, block, d_s.at[e, m], d_r.at[e, m], mate)

    def finish(both):
        one = both[0][:, 0:128] / both[0][:, 128:256]
        two = both[1][:, 0:128] / both[1][:, 128:256]
        return jnp.where(first_half, one, two).astype(bf16)

    visible = finish(
        [
            decoder_mix(vq[h], dk[...], dv[...]) + decoder_mix(vq[h], vk[...], vv[...])
            for h in range(2)
        ]
    )

    @pl.loop(0, 4)
    def _(i):
        e = near(3 - i)
        there = turn(y, e)
        rows = block_rows(there)
        mixed = finish(
            [base[h, rows, :] + decoder_mix(dq[h, rows, :], vk[...], vv[...]) for h in range(2)]
        )
        placed = jnp.dot(sel[rows, :], visible, preferred_element_type=f32)
        hidden = dv[rows, 128:256].astype(f32) > 0.5
        mixed = jnp.where(hidden, mixed.astype(f32), placed).astype(bf16)
        dm[there * 2] = mixed[0:128]
        dm[there * 2 + 1] = mixed[128:256]

        @pl.when(e > 0)
        def _():
            mix_copy(e, 0).start()

        mix_copy(e, 1).start()

    da[:, pl.ds(aligned(row * 128, 128), 128)] = dm[row]
    fetches[4].wait()
    fetches[5].wait()
    for k in range(1, 8):
        mix_got(k // 2, k % 2).wait_recv()
    tokens = tok[pl.ds(aligned(c * 128, 128), 128), :] + jnp.dot(
        sel[pl.ds(aligned(row * 128, 128), 128), :],
        vis[...].reshape(256, DD),
        preferred_element_type=f32,
    )
    decoded = tokens + jnp.dot(da[...], dow[...], preferred_element_type=f32)
    normed = norm(decoded, hg_ref[...]).astype(bf16)
    predicted = jnp.dot(normed, pxw[...], preferred_element_type=f32) + pb_ref[...].reshape(1, 768)
    pred[...] = predicted.astype(bf16)
    pred_mine = pltpu.make_async_copy(pred, pred_ref.at[0], l_s.at[9])
    pred_mine.start()

    enc_mine.wait()
    for d in range(1, 4):
        block = enc_ref.at[:, turn(z, 4 - d)]
        remote(block, block, en_s.at[d], en_r.at[d], mate).wait_recv()
        enc_copy(d).wait_send()
        gain_copy(d).wait_send()
        raw_copy(d).wait_send()
        own_copy(d).wait_send()
        fgain_copy(d).wait_send()
        wo_copy(d, 0).wait_send()
        wo_copy(d, 1).wait_send()
        stat_copy(0, d, z).wait_send()
        stat_copy(1, d, x).wait_send()
        ex_copy(d).wait_send()
        eb_copy(d).wait_send()
        whole = att.at[x]
        remote(whole, whole, t_s.at[d], t_r.at[d], mate).wait_send()
        ec_copy(d).wait_send()
    for e in range(4):
        for block, s_y, r_y, s_c, r_c in (
            (a, ay_s, ay_r, ac_s, ac_r),
            (pos, p_s, p_r, pc_s, pc_r),
        ):
            if e > 0:
                own = block.at[y, c]
                remote(own, own, s_y.at[e], r_y.at[e], mate).wait_send()
            passed = block.at[turn(y, 4 - e), c]
            remote(passed, passed, s_c.at[e], r_c.at[e], mate).wait_send()
        mate_copy(e).wait_send()
        if e > 0:
            own_rows = vis.at[row]
            remote(own_rows, own_rows, v_s.at[e], v_r.at[e], mate).wait_send()
        passed = vis.at[turn(y, 4 - e) * 2 + c]
        remote(passed, passed, vc_s.at[e], vc_r.at[e], mate).wait_send()
        for way in range(2):
            y_hop(e, way).wait_send()
            y_all(e, way).wait_send()
    for k in range(1, 8):
        mix_copy(k // 2, k % 2).wait_send()

    @pl.loop(0, HEADS_OWN)
    def _(j):
        for way in range(2):
            w_send(j, way).wait_send()
            w_forward(j, way).wait_send()

    @pl.loop(0, HEADS_OWN)
    def _(j):
        for way in range(2):
            c_all(j, way).wait_send()

        @pl.loop(0, 4)
        def _(s):
            hop_copy(j, s).wait_send()
    pred_mine.wait()


def hand_on(enc_ref, pred_ref, enc_out, pred_out):
    enc_out[...] = enc_ref[...]
    pred_out[...] = pred_ref[...]


VMEM = pl.BlockSpec(memory_space=pltpu.VMEM)
ANY = pl.BlockSpec(memory_space=pl.ANY)


def local(
    visible_patches,
    input_gain,
    encoder_project,
    query_gain,
    key_gain,
    output_weight,
    final_gain,
    embed_weight,
    embed_bias,
    mask_token,
    position_embed,
    script_table,
    decoder_gain,
    decoder_project,
    decoder_query,
    decoder_key,
    decoder_output,
    head_gain,
    pixel_weight,
    pixel_bias,
    visible_index,
    script_index,
):
    def flat(vector):
        return vector.reshape(1, -1)

    dma = pltpu.SemaphoreType.DMA
    two = [dma((4,)), dma((4,))]
    operands = (
        visible_patches.reshape(4, 4, 32, 384), input_gain, encoder_project, flat(query_gain), flat(key_gain),
        output_weight, final_gain, embed_weight, flat(embed_bias), flat(mask_token),
        position_embed, script_table, flat(decoder_gain), decoder_project, flat(decoder_query),
        flat(decoder_key), decoder_output, flat(head_gain), pixel_weight, pixel_bias,
        visible_index, flat(script_index),
    )
    encoded, predicted = pl.pallas_call(
        kernel,
        out_shape=(
            jax.ShapeDtypeStruct((4, 4, 32, 384), bf16),
            jax.ShapeDtypeStruct((1, 128, 768), bf16),
        ),
        in_specs=[ANY] * 22,
        out_specs=(ANY, ANY),
        scratch_shapes=[
            *[pltpu.VMEM(operands[index].shape, operands[index].dtype) for index in SMALL],
            dma((len(SMALL),)),
            pltpu.VMEM((4, 8, 384), f32),
            pltpu.VMEM((4, 8, 384), f32),
            pltpu.VMEM((4, 4, 32, 384), bf16),
            pltpu.VMEM((4, 4, 32, 384), bf16),
            pltpu.VMEM((2, 4, 8, 128), f32),
            pltpu.VMEM((4, 2, 128, 1536), bf16),
            pltpu.VMEM((HEADS_OWN, 1536, 384), bf16),
            pltpu.VMEM((4, 768, 384), bf16),
            pltpu.VMEM((HEADS_OWN, 4, 256, 384), bf16),
            pltpu.VMEM((2, HEADS_OWN, 256, 384), bf16),
            pltpu.VMEM((HEADS_OWN, 256, 384), bf16),
            pltpu.VMEM((4, 256, 768), bf16),
            pltpu.VMEM((4, 2, 4, 128, 384), bf16),
            pltpu.VMEM((4, 4, 128, 384), bf16),
            pltpu.VMEM((2, 4, 128, 384), bf16),
            pltpu.VMEM((4, 128, 384), bf16),
            pltpu.VMEM((4, 128, 384), f32),
            pltpu.VMEM((128, 1536), bf16),
            pltpu.VMEM((4, 4, 32, 384), bf16),
            pltpu.VMEM((4, 384, DD), bf16),
            pltpu.VMEM((4, 2, 128, DD), bf16),
            pltpu.VMEM((DD, 384), bf16),
            pltpu.VMEM((DD, DD), bf16),
            pltpu.VMEM((DD, 768), bf16),
            pltpu.VMEM((4, 32, DD), bf16),
            pltpu.VMEM((3, 32, DD), bf16),
            pltpu.VMEM((8, 32, DD), bf16),
            pltpu.VMEM((8, DD), f32),
            pltpu.VMEM((1024, 256), bf16),
            pltpu.VMEM((256, DD), f32),
            pltpu.VMEM((256, DD), f32),
            pltpu.VMEM((2, 1024, 128), bf16),
            pltpu.VMEM((1024, 128), bf16),
            pltpu.VMEM((1024, 256), bf16),
            pltpu.VMEM((2, 1024, 256), f32),
            pltpu.VMEM((2, 256, 128), bf16),
            pltpu.VMEM((256, 128), bf16),
            pltpu.VMEM((256, 256), bf16),
            pltpu.VMEM((8, 128, 128), bf16),
            pltpu.VMEM((128, DD), bf16),
            pltpu.VMEM((128, 768), bf16),
            dma((10,)),
            dma((HEADS_OWN,)),
            *two,
            *two,
            *two,
            *two,
            dma((2, 4)), dma((2, 4)),
            dma((2, 4)), dma((2, 4)),
            *two,
            *two,
            dma((2, HEADS_OWN)), dma((2, HEADS_OWN)),
            dma((2, HEADS_OWN)), dma((2, HEADS_OWN)),
            dma((HEADS_OWN, 4)), dma((HEADS_OWN, 4)),
            dma((2, HEADS_OWN)), dma((2, HEADS_OWN)),
            *two,
            *two,
            *two,
            *two,
            *two,
            *two,
            dma((2, 4)), dma((2, 4)),
            dma((2, 4)), dma((2, 4)),
            *two,
            *two,
            *two,
            *two,
            dma((4, 2)), dma((4, 2)),
        ],
        compiler_params=pltpu.CompilerParams(
            collective_id=0, has_side_effects=True, vmem_limit_bytes=62 << 20
        ),
        name="masked_patches",
    )(*operands)
    encoded = encoded.reshape(16, 32, 384)
    return pl.pallas_call(
        hand_on,
        out_shape=(
            jax.ShapeDtypeStruct(encoded.shape, bf16),
            jax.ShapeDtypeStruct(predicted.shape, bf16),
        ),
        in_specs=[VMEM, VMEM],
        out_specs=(VMEM, VMEM),
        name="hand_on",
    )(encoded, predicted)


def solution(mesh):
    return jax.shard_map(
        local,
        mesh=mesh,
        in_specs=(
            P(None, "row", "col"),
            P("col"),
            P("col", "row"),
            P(),
            P(),
            P("row", "col"),
            P("col"),
            P("col", None),
            P(),
            P(),
            P("row", None),
            P(),
            P(),
            P(),
            P(),
            P(),
            P(),
            P(),
            P(),
            P(),
            P("col", None),
            P("col"),
        ),
        out_specs=(P(None, "row", "col"), P("col", "row", None)),
        check_vma=False,
    )
```
